32 devices in a mesh: rep: 4 (over y, core), grp: 8 (over z, x).
Axes of the slice: x: 2, y: 2, z: 4, core: 2. Of those that a mesh axis runs over, the one named last changes fastest.
Arguments:
- master_weight: float32 [16, 384, 2048], P('grp', 'rep'), may hold values from -0.3125 to 0.3125
- m_code: bfloat16 [16, 384, 2048], P('grp', 'rep'), may hold values from -1 to 1
- m_scale: float32 [16, 384, 16], P('grp', 'rep'), may hold values from 0.1 to 3
- v_code: bfloat16 [16, 384, 2048], P('grp', 'rep'), may hold values from 0.0099487305 to 1
- v_scale: float32 [16, 384, 16], P('grp', 'rep'), may hold values from 0.1 to 3
- placement: int32 [16], replicated, may hold values from 0 to 15, each once
- route: int32 [8192], P(('rep', 'grp')), may hold values from 0 to 15, as said below
- x_rows: bfloat16 [8192, 384], P(('rep', 'grp')), may hold values from -6 to 6
- y_cot: bfloat16 [8192, 2048], P(('rep', 'grp')), may hold values from -6 to 6
Outputs:
- y_rows: bfloat16 [8192, 2048], P(('rep', 'grp'))
- x_grad: bfloat16 [8192, 384], P(('rep', 'grp'))
- master_next: float32 [16, 384, 2048], P('grp', 'rep')
- m_code_next: bfloat16 [16, 384, 2048], P('grp', 'rep')
- m_scale_next: float32 [16, 384, 16], P('grp', 'rep')
- v_code_next: bfloat16 [16, 384, 2048], P('grp', 'rep')
- v_scale_next: float32 [16, 384, 16], P('grp', 'rep')
The draws below stay inside these ranges and needn't reach their ends.
Inputs may be any that keep to these rules, and one draw needn't show every extreme that they name: Each expert once; slot s of the weight and moment arrays holds the expert placement[s]. `route`: in the 256 rows of one device no expert appears more than 24 times, and one expert appears exactly 24 times in the rows of every device.
All inputs are finite; a program needn't handle non-finite values. Where the reference program divides by a largest or mean magnitude, that divisor is 1e-20 or more.
Results may differ from the reference program's by a relative error of at most 0.015.
Values may be sent and summed in bfloat16 or wider, within the bound.
No kernel may reach another device: no remote copies, remote signals or barrier semaphores. Data moves between devices by JAX's collectives and lax.ppermute only.
A program may use at most 64 MiB of HBM per device.

```python
import math
import jax
import jax.numpy as jnp
from jax import lax

D = 2048
FF = 384
EXPERTS = 16
ROWS_DEV = 256
ROW_LIMIT = 24
ROWS_REP = 2048
ROWS_ALL = 8192
PER_EXPERT = 512
BLOCK = 128
ADAM_STEP = 100
N_REP = 4
N_GRP = 8


def draw_route(key, part):
    block_count = ROWS_ALL // ROWS_DEV
    remaining_experts = EXPERTS - 1
    popular_random_key, boost_random_key, block_random_key = jax.random.split(jax.random.fold_in(key, 7), 3)
    hot_expert = jax.random.randint(popular_random_key, (), 0, EXPERTS)
    routing_boost = jnp.repeat(jax.random.randint(boost_random_key, (remaining_experts,), 0, 4) * 256, ROW_LIMIT)
    candidate_expert = jnp.arange(remaining_experts * ROW_LIMIT, dtype=jnp.int32)

    def one_block(block_key):
        key_noise, key_order = jax.random.split(block_key)
        random_jitter = jax.random.randint(key_noise, (remaining_experts * ROW_LIMIT,), 0, 1024)
        routing_score = (random_jitter + routing_boost) * 4096 + candidate_expert
        unused, picked = lax.top_k(routing_score, ROWS_DEV - ROW_LIMIT)
        chosen = (hot_expert + 1 + picked // ROW_LIMIT) % EXPERTS
        filled = jnp.concatenate([jnp.full((ROW_LIMIT,), hot_expert, jnp.int32), chosen.astype(jnp.int32)])
        order = jax.random.permutation(key_order, ROWS_DEV)
        return filled[order]
    block_keys = jax.random.split(block_random_key, block_count)
    return jax.vmap(one_block)(block_keys).reshape(-1).astype(jnp.int32)


def shard_levels(key, shape, cuts, least, top_value):
    def one(dim, shards_of):
        draws = jax.random.uniform(jax.random.fold_in(jax.random.fold_in(key, 6), dim), (shards_of,), jnp.float32, least / len(cuts), top_value / len(cuts))
        return jnp.repeat(jnp.exp(draws), shape[dim] // shards_of).reshape((-1,) + (1,) * (len(shape) - dim - 1))

    gain = one(*cuts[0])
    for cut in cuts[1:]:
        gain = gain * one(*cut)
    return gain


def normal_values(key, shape, scale, bound, cuts=(), kind=jnp.bfloat16):
    array = scale * jax.random.normal(key, shape, jnp.float32)
    if cuts:
        array = array * shard_levels(key, shape, cuts, -0.22, 0.18)
    return jnp.clip(array, -bound, bound).astype(kind)


def setup_inputs(seed: int = 0) -> dict:
    streams_of = jax.random.split(jax.random.key(seed), 10)
    master_weight = normal_values(streams_of[0], (EXPERTS, FF, D), FF ** -0.5, 0.3125, ((0, 8), (1, 4)), jnp.float32)
    m_code = jnp.clip(jax.random.uniform(streams_of[1], (EXPERTS, FF, D), jnp.float32, -1.0, 1.0) * shard_levels(streams_of[1], (EXPERTS, FF, D), ((0, 8), (1, 4)), -0.4, 0.0), -1.0, 1.0).astype(jnp.bfloat16)
    m_scale = jnp.clip(jnp.exp(math.log(3.0) - 3.4011974 * jax.random.uniform(streams_of[2], (EXPERTS, FF, D // BLOCK), jnp.float32) ** shard_levels(streams_of[2], (EXPERTS, FF, D // BLOCK), ((0, 8), (1, 4)), -0.2, 0.2)), 0.1, 3.0)
    v_code = jnp.clip(0.0099487305 + 0.99005127 * jax.random.uniform(streams_of[3], (EXPERTS, FF, D), jnp.float32) ** shard_levels(streams_of[3], (EXPERTS, FF, D), ((0, 8), (1, 4)), -0.2, 0.2), 0.0099487305, 1.0).astype(jnp.bfloat16)
    v_scale = jnp.clip(jnp.exp(math.log(3.0) - 3.4011974 * jax.random.uniform(streams_of[4], (EXPERTS, FF, D // BLOCK), jnp.float32) ** shard_levels(streams_of[4], (EXPERTS, FF, D // BLOCK), ((0, 8), (1, 4)), -0.2, 0.2)), 0.1, 3.0)
    placement = jax.random.permutation(streams_of[5], EXPERTS).astype(jnp.int32)
    route = draw_route(jax.random.fold_in(streams_of[9], 71), 0)
    x_rows = normal_values(streams_of[7], (ROWS_ALL, FF), 1.0, 6.0, ((0, 32),))
    y_cot = normal_values(streams_of[8], (ROWS_ALL, D), 1.0, 6.0, ((0, 32),))
    return dict(master_weight=master_weight, m_code=m_code, m_scale=m_scale, v_code=v_code, v_scale=v_scale, placement=placement, route=route, x_rows=x_rows, y_cot=y_cot)


beta_one = 0.9
beta_two = 0.95
learn_rate = 0.01

def adam_update(master_weight, grad, m_code, m_scale, v_code, v_scale):
    full_shape = master_weight.shape
    blocked = full_shape[:-1] + (full_shape[-1] // BLOCK, BLOCK)
    m_old = (m_code.astype(jnp.float32).reshape(blocked) * m_scale[..., None]).reshape(full_shape)
    v_old = (v_code.astype(jnp.float32).reshape(blocked) * v_scale[..., None]).reshape(full_shape)
    m_next = beta_one * m_old + (1.0 - beta_one) * grad
    v_next = beta_two * v_old + (1.0 - beta_two) * grad * grad
    corr_one = 1.0 - beta_one ** ADAM_STEP
    corr_two = 1.0 - beta_two ** ADAM_STEP
    step_size = m_next / corr_one / (jnp.sqrt(v_next / corr_two) + 1e-08)
    master_next = master_weight - learn_rate * step_size
    m_blocks = m_next.reshape(blocked)
    v_blocks = v_next.reshape(blocked)
    m_scale_next = lax.optimization_barrier(jnp.max(jnp.abs(m_blocks), axis=-1)) + 1e-06
    v_scale_next = lax.optimization_barrier(jnp.max(v_blocks, axis=-1)) + 1e-06
    m_code_next = (m_blocks / m_scale_next[..., None]).reshape(full_shape).astype(jnp.bfloat16)
    v_code_next = (v_blocks / v_scale_next[..., None]).reshape(full_shape).astype(jnp.bfloat16)
    return (master_next, m_code_next, m_scale_next, v_code_next, v_scale_next)

def reference(master_weight, m_code, m_scale, v_code, v_scale, placement, route, x_rows, y_cot):
    expert_ids = jnp.arange(EXPERTS, dtype=jnp.int32)
    slot_rows = N_GRP * ROW_LIMIT
    grad_factor = float(PER_EXPERT) ** (-0.5)
    weight_low = master_weight.astype(jnp.bfloat16)
    weight_full = lax.optimization_barrier(weight_low).astype(jnp.float32)
    sources = jnp.arange(N_GRP, dtype=jnp.int32)

    def replica(total, inputs):
        routes_here, x_here, g_here = inputs
        slot = lax.optimization_barrier(jnp.sum(jnp.where(placement[None, :] == routes_here[:, None], expert_ids[None, :], 0), axis=1)).astype(jnp.int32)
        slot_grid = slot.reshape(N_GRP, ROWS_DEV)
        slot_hot = (slot_grid[:, :, None] == expert_ids[None, None, :]).astype(jnp.int32)
        position = lax.optimization_barrier(jnp.sum(slot_hot * (jnp.cumsum(slot_hot, axis=1) - 1), axis=2)).astype(jnp.int32)
        target = (slot_grid * slot_rows + sources[:, None] * ROW_LIMIT + position).reshape(-1).astype(jnp.int32)
        buffer_x = jnp.zeros((EXPERTS * slot_rows, FF), jnp.float32).at[target].set(x_here.astype(jnp.float32))
        buffer_g = jnp.zeros((EXPERTS * slot_rows, D), jnp.float32).at[target].set(g_here.astype(jnp.float32))
        buffer_x = buffer_x.reshape(EXPERTS, slot_rows, FF)
        buffer_g = buffer_g.reshape(EXPERTS, slot_rows, D)
        out_y = jnp.einsum('esf,efd->esd', buffer_x, weight_full)
        out_dx = jnp.einsum('esd,efd->esf', buffer_g, weight_full)
        part_low = (jnp.einsum('esf,esd->efd', buffer_x, buffer_g) * grad_factor).astype(jnp.bfloat16)
        part_grad = lax.optimization_barrier(part_low).astype(jnp.float32)
        y_here = out_y.reshape(-1, D)[target].astype(jnp.bfloat16)
        dx_here = out_dx.reshape(-1, FF)[target].astype(jnp.bfloat16)
        return (total + part_grad, (y_here, dx_here))
    start_total = jnp.zeros((EXPERTS, FF, D), jnp.float32)
    grad, outputs = lax.scan(replica, start_total, (route.reshape(N_REP, ROWS_REP), x_rows.reshape(N_REP, ROWS_REP, FF), y_cot.reshape(N_REP, ROWS_REP, D)))
    y_rows = outputs[0].reshape(ROWS_ALL, D)
    x_grad = outputs[1].reshape(ROWS_ALL, FF)
    master_next, m_code_next, m_scale_next, v_code_next, v_scale_next = adam_update(master_weight, grad, m_code, m_scale, v_code, v_scale)
    return (y_rows, x_grad, master_next, m_code_next, m_scale_next, v_code_next, v_scale_next)
```

```python
import functools

import jax
import jax.numpy as jnp
from jax import lax
from jax.experimental import pallas as pl
from jax.experimental.pallas import tpu as pltpu
from jax.sharding import PartitionSpec as P

BLOCK = 128
ADAM_STEP = 100

beta_one = 0.9
beta_two = 0.95
learn_rate = 0.01

VMEM_LIMIT = 40 * 1024 * 1024
F32 = jnp.float32
BF16 = jnp.bfloat16


def cost(flops, nbytes):
    return pl.CostEstimate(flops=int(flops), bytes_accessed=int(nbytes), transcendentals=0)


def params(*semantics):
    if semantics:
        return pltpu.CompilerParams(vmem_limit_bytes=VMEM_LIMIT, dimension_semantics=semantics)
    return pltpu.CompilerParams(vmem_limit_bytes=VMEM_LIMIT)


def row_targets(route_row, placement_col, capacity):
    expert_count = placement_col.shape[0]
    row_count = route_row.shape[1]
    hot = (placement_col == route_row).astype(F32)
    earlier = lax.broadcasted_iota(jnp.int32, (row_count, row_count), 0)
    later = lax.broadcasted_iota(jnp.int32, (row_count, row_count), 1)
    before = (earlier < later).astype(F32).astype(BF16)
    position = jnp.dot(hot.astype(BF16), before, preferred_element_type=F32)
    start = lax.broadcasted_iota(jnp.int32, (expert_count, row_count), 0) * capacity
    return jnp.sum(hot * (start.astype(F32) + position), axis=0, keepdims=True).astype(jnp.int32)


def place_matrix(target, places):
    slots = lax.broadcasted_iota(jnp.int32, (places, target.shape[1]), 0)
    return (slots == target).astype(F32).astype(BF16)


def dispatch_x_kernel(capacity, route_ref, placement_ref, x_ref, sent_ref, target_ref):
    target = row_targets(route_ref[...], placement_ref[...], capacity)
    target_ref[...] = target
    places = place_matrix(target, sent_ref.shape[0])
    sent_ref[...] = jnp.dot(places, x_ref[...], preferred_element_type=F32).astype(BF16)


def dispatch_x(route, placement, x_rows, capacity):
    row_count, hidden = x_rows.shape
    places = placement.shape[0] * capacity
    return pl.pallas_call(
        functools.partial(dispatch_x_kernel, capacity),
        out_shape=(
            jax.ShapeDtypeStruct((places, hidden), BF16),
            jax.ShapeDtypeStruct((1, row_count), jnp.int32),
        ),
        compiler_params=params(),
        cost_estimate=cost(2 * places * row_count * hidden, 2 * (places + row_count) * hidden),
    )(route.reshape(1, row_count), placement.reshape(-1, 1), x_rows)


def dispatch_g_kernel(target_ref, g_ref, sent_ref):
    places = place_matrix(target_ref[...], sent_ref.shape[0])
    sent_ref[...] = jnp.dot(places, g_ref[...], preferred_element_type=F32).astype(BF16)


def dispatch_g(target, y_cot, places):
    row_count, width = y_cot.shape
    tile = min(width, 512)
    return pl.pallas_call(
        dispatch_g_kernel,
        grid=(width // tile,),
        in_specs=[
            pl.BlockSpec((1, row_count), lambda j: (0, 0)),
            pl.BlockSpec((row_count, tile), lambda j: (0, j)),
        ],
        out_specs=pl.BlockSpec((places, tile), lambda j: (0, j)),
        out_shape=jax.ShapeDtypeStruct((places, width), BF16),
        compiler_params=params("arbitrary"),
        cost_estimate=cost(2 * places * row_count * width, 2 * (places + row_count) * width),
    )(target, y_cot)


def collect_kernel(target_ref, home_ref, out_ref):
    places = place_matrix(target_ref[...], home_ref.shape[0])
    out_ref[...] = lax.dot_general(
        places, home_ref[...], (((0,), (0,)), ((), ())), preferred_element_type=F32
    ).astype(BF16)


def collect(target, home):
    places, width = home.shape
    row_count = target.shape[1]
    tile = min(width, 512)
    return pl.pallas_call(
        collect_kernel,
        grid=(width // tile,),
        in_specs=[
            pl.BlockSpec((1, row_count), lambda j: (0, 0)),
            pl.BlockSpec((places, tile), lambda j: (0, j)),
        ],
        out_specs=pl.BlockSpec((row_count, tile), lambda j: (0, j)),
        out_shape=jax.ShapeDtypeStruct((row_count, width), BF16),
        compiler_params=params("arbitrary"),
        cost_estimate=cost(2 * places * row_count * width, 2 * (places + row_count) * width),
    )(target, home)


def member_rows(rows, capacity, local_count):
    index = lax.broadcasted_iota(jnp.int32, (rows, 1), 0)
    return lax.rem(index, capacity * local_count) // capacity


def spread(x, capacity, local_count):
    member = member_rows(x.shape[0], capacity, local_count)
    zero = jnp.zeros_like(x)
    return jnp.concatenate([jnp.where(member == e, x, zero) for e in range(local_count)], axis=1)


def forward_kernel(capacity, local_count, x_ref, w_ref, y_ref):
    wide = spread(x_ref[...], capacity, local_count)
    weight = w_ref[...].reshape(wide.shape[1], w_ref.shape[-1])
    y_ref[...] = jnp.dot(wide, weight, preferred_element_type=F32).astype(BF16)


def forward(x, weight, capacity):
    rows, hidden = x.shape
    local_count, _, width = weight.shape
    tile = min(width, 512)
    return pl.pallas_call(
        functools.partial(forward_kernel, capacity, local_count),
        grid=(width // tile,),
        in_specs=[
            pl.BlockSpec((rows, hidden), lambda j: (0, 0)),
            pl.BlockSpec((local_count, hidden, tile), lambda j: (0, 0, j)),
        ],
        out_specs=pl.BlockSpec((rows, tile), lambda j: (0, j)),
        out_shape=jax.ShapeDtypeStruct((rows, width), BF16),
        compiler_params=params("arbitrary"),
        cost_estimate=cost(
            2 * rows * local_count * hidden * width,
            2 * (local_count * hidden + rows) * width,
        ),
    )(x, weight)


def gradient_kernel(capacity, local_count, factor, x_ref, g_ref, out_ref):
    wide = spread(x_ref[...], capacity, local_count)
    outer = lax.dot_general(
        wide, g_ref[...], (((0,), (0,)), ((), ())), preferred_element_type=F32
    )
    out_ref[...] = (outer * factor).astype(BF16).reshape(out_ref.shape)


def gradient(x, g, capacity, local_count, factor):
    rows, hidden = x.shape
    width = g.shape[1]
    tile = min(width, 512)
    return pl.pallas_call(
        functools.partial(gradient_kernel, capacity, local_count, factor),
        grid=(width // tile,),
        in_specs=[
            pl.BlockSpec((rows, hidden), lambda j: (0, 0)),
            pl.BlockSpec((rows, tile), lambda j: (0, j)),
        ],
        out_specs=pl.BlockSpec((local_count, hidden, tile), lambda j: (0, 0, j)),
        out_shape=jax.ShapeDtypeStruct((local_count, hidden, width), BF16),
        compiler_params=params("arbitrary"),
        cost_estimate=cost(
            2 * rows * local_count * hidden * width,
            2 * (local_count * hidden + rows) * width,
        ),
    )(x, g)


def backward_kernel(capacity, local_count, g_ref, w_ref, dx_ref, total_ref):
    step = pl.program_id(0)
    hidden = dx_ref.shape[1]
    weight = w_ref[...].reshape(local_count * hidden, w_ref.shape[-1])
    part = lax.dot_general(
        g_ref[...], weight, (((1,), (1,)), ((), ())), preferred_element_type=F32
    )

    @pl.when(step == 0)
    def _():
        total_ref[...] = part

    @pl.when(step > 0)
    def _():
        total_ref[...] += part

    @pl.when(step == pl.num_programs(0) - 1)
    def _():
        member = member_rows(dx_ref.shape[0], capacity, local_count)
        picked = total_ref[:, :hidden]
        for e in range(1, local_count):
            picked = jnp.where(member == e, total_ref[:, e * hidden : (e + 1) * hidden], picked)
        dx_ref[...] = picked.astype(BF16)


def backward(g, weight, capacity):
    rows, width = g.shape
    local_count, hidden, _ = weight.shape
    tile = min(width, 512)
    return pl.pallas_call(
        functools.partial(backward_kernel, capacity, local_count),
        grid=(width // tile,),
        in_specs=[
            pl.BlockSpec((rows, tile), lambda j: (0, j)),
            pl.BlockSpec((local_count, hidden, tile), lambda j: (0, 0, j)),
        ],
        out_specs=pl.BlockSpec((rows, hidden), lambda j: (0, 0)),
        out_shape=jax.ShapeDtypeStruct((rows, hidden), BF16),
        scratch_shapes=[pltpu.VMEM((rows, local_count * hidden), F32)],
        compiler_params=params("arbitrary"),
        cost_estimate=cost(
            2 * rows * local_count * hidden * width,
            2 * (local_count * hidden + rows) * width,
        ),
    )(g, weight)


def adam_kernel(
    master_ref, grad_ref, mc_ref, ms_ref, vc_ref, vs_ref,
    master_out, mc_out, ms_out, vc_out, vs_out,
):
    blocks = ms_ref.shape[-1]
    rows = ms_ref.shape[1]
    corr_one = 1.0 - beta_one**ADAM_STEP
    corr_two = 1.0 - beta_two**ADAM_STEP
    m_scales = ms_ref[0]
    v_scales = vs_ref[0]
    lane = lax.broadcasted_iota(jnp.int32, (rows, blocks), 1)
    m_tops = jnp.zeros((rows, blocks), F32)
    v_tops = jnp.zeros((rows, blocks), F32)
    for b in range(blocks):
        cols = slice(b * BLOCK, (b + 1) * BLOCK)
        grad = grad_ref[0, :, cols].astype(F32)
        m_old = mc_ref[0, :, cols].astype(F32) * m_scales[:, b : b + 1]
        v_old = vc_ref[0, :, cols].astype(F32) * v_scales[:, b : b + 1]
        m_next = beta_one * m_old + (1.0 - beta_one) * grad
        v_next = beta_two * v_old + (1.0 - beta_two) * grad * grad
        step_size = m_next / corr_one / (jnp.sqrt(v_next / corr_two) + 1e-08)
        master_out[0, :, cols] = master_ref[0, :, cols] - learn_rate * step_size
        m_top = jnp.max(jnp.abs(m_next), axis=-1, keepdims=True) + 1e-06
        v_top = jnp.max(v_next, axis=-1, keepdims=True) + 1e-06
        mc_out[0, :, cols] = (m_next * (1.0 / m_top)).astype(BF16)
        vc_out[0, :, cols] = (v_next * (1.0 / v_top)).astype(BF16)
        m_tops = jnp.where(lane == b, m_top, m_tops)
        v_tops = jnp.where(lane == b, v_top, v_tops)
    ms_out[0] = m_tops
    vs_out[0] = v_tops


def adam(master_weight, grad, m_code, m_scale, v_code, v_scale):
    members, rows, width = master_weight.shape
    blocks = m_scale.shape[-1]
    tile = rows // 3 if rows % 48 == 0 else rows
    big = pl.BlockSpec((1, tile, width), lambda e, i: (e, i, 0))
    small = pl.BlockSpec((1, tile, blocks), lambda e, i: (e, i, 0))
    return pl.pallas_call(
        adam_kernel,
        grid=(members, rows // tile),
        in_specs=[big, big, big, small, big, small],
        out_specs=(big, big, small, big, small),
        out_shape=(
            jax.ShapeDtypeStruct(master_weight.shape, F32),
            jax.ShapeDtypeStruct(master_weight.shape, BF16),
            jax.ShapeDtypeStruct(m_scale.shape, F32),
            jax.ShapeDtypeStruct(master_weight.shape, BF16),
            jax.ShapeDtypeStruct(m_scale.shape, F32),
        ),
        compiler_params=params("arbitrary", "arbitrary"),
        cost_estimate=cost(40 * master_weight.size, 18 * master_weight.size),
    )(master_weight, grad, m_code, m_scale, v_code, v_scale)


def exchange(buffer, groups):
    places, width = buffer.shape
    parts = buffer.reshape(groups, places // groups, width)
    moved = lax.all_to_all(parts, "grp", split_axis=0, concat_axis=0, tiled=True)
    return moved.reshape(places, width)


def per_device(master_weight, m_code, m_scale, v_code, v_scale, placement, route, x_rows, y_cot):
    local_count = master_weight.shape[0]
    row_count = x_rows.shape[0]
    expert_count = placement.shape[0]
    groups = lax.axis_size("grp")
    replicas = lax.axis_size("rep")
    grad_factor = float(row_count * groups * replicas // expert_count) ** (-0.5)
    capacity = max(2, (3 * row_count + 2 * expert_count - 1) // (2 * expert_count))
    places = expert_count * capacity

    weight_slice = master_weight.astype(BF16)
    weight = lax.all_gather(weight_slice, "rep", axis=1, tiled=True)

    send_x, target = dispatch_x(route, placement, x_rows, capacity)
    send_g = dispatch_g(target, y_cot, places)
    local_x = exchange(send_x, groups)
    local_g = exchange(send_g, groups)

    back_y = forward(local_x, weight, capacity)
    home_y = exchange(back_y, groups)

    part_grad = gradient(local_x, local_g, capacity, local_count, grad_factor)
    grad = lax.psum_scatter(part_grad, "rep", scatter_dimension=1, tiled=True)
    back_dx = backward(local_g, weight, capacity)
    home_dx = exchange(back_dx, groups)

    x_grad = collect(target, home_dx)
    updated = adam(master_weight, grad, m_code, m_scale, v_code, v_scale)
    y_rows = collect(target, home_y)
    return (y_rows, x_grad) + tuple(updated)


def solution(mesh):
    return jax.shard_map(
        per_device,
        mesh=mesh,
        in_specs=(
            P("grp", "rep", None),
            P("grp", "rep", None),
            P("grp", "rep", None),
            P("grp", "rep", None),
            P("grp", "rep", None),
            P(),
            P(("rep", "grp")),
            P(("rep", "grp"), None),
            P(("rep", "grp"), None),
        ),
        out_specs=(
            P(("rep", "grp"), None),
            P(("rep", "grp"), None),
            P("grp", "rep", None),
            P("grp", "rep", None),
            P("grp", "rep", None),
            P("grp", "rep", None),
            P("grp", "rep", None),
        ),
        check_vma=False,
    )
```

```python
import functools

import jax
import jax.numpy as jnp
from jax import lax
from jax.experimental import pallas as pl
from jax.experimental.pallas import tpu as pltpu
from jax.sharding import PartitionSpec as P

BLOCK = 128
ADAM_STEP = 100

beta_one = 0.9
beta_two = 0.95
learn_rate = 0.01

VMEM_LIMIT = 40 * 1024 * 1024
F32 = jnp.float32
BF16 = jnp.bfloat16


def cost(flops, nbytes):
    return pl.CostEstimate(flops=int(flops), bytes_accessed=int(nbytes), transcendentals=0)


def params(*semantics):
    if semantics:
        return pltpu.CompilerParams(vmem_limit_bytes=VMEM_LIMIT, dimension_semantics=semantics)
    return pltpu.CompilerParams(vmem_limit_bytes=VMEM_LIMIT)


def is_power_of_two(n):
    return n & (n - 1) == 0


def row_targets(route_row, placement_col, capacity, local_count, relative):
    expert_count = placement_col.shape[0]
    row_count = route_row.shape[1]
    hot = (placement_col == route_row).astype(F32)
    earlier = lax.broadcasted_iota(jnp.int32, (row_count, row_count), 0)
    later = lax.broadcasted_iota(jnp.int32, (row_count, row_count), 1)
    before = (earlier < later).astype(F32).astype(BF16)
    position = jnp.dot(hot.astype(BF16), before, preferred_element_type=F32)
    slot = lax.broadcasted_iota(jnp.int32, (expert_count, row_count), 0)
    chunk = slot // local_count
    if relative:
        chunk = jnp.bitwise_xor(chunk, lax.axis_index("grp"))
    start = (chunk * local_count + lax.rem(slot, local_count)) * capacity
    return jnp.sum(hot * (start.astype(F32) + position), axis=0, keepdims=True).astype(jnp.int32)


def place_matrix(target, places):
    slots = lax.broadcasted_iota(jnp.int32, (places, target.shape[1]), 0)
    return (slots == target).astype(F32).astype(BF16)


def write_chunks(refs, value):
    rows = refs[0].shape[0]
    for k, ref in enumerate(refs):
        ref[...] = value[k * rows : (k + 1) * rows]


def read_chunks(refs):
    if len(refs) == 1:
        return refs[0][...]
    return jnp.concatenate([ref[...] for ref in refs], axis=0)


def dispatch_x_kernel(capacity, local_count, relative, route_ref, placement_ref, x_ref, *out_refs):
    target_ref, chunk_refs = out_refs[0], out_refs[1:]
    target = row_targets(route_ref[...], placement_ref[...], capacity, local_count, relative)
    target_ref[...] = target
    places = place_matrix(target, len(chunk_refs) * chunk_refs[0].shape[0])
    write_chunks(
        chunk_refs, jnp.dot(places, x_ref[...], preferred_element_type=F32).astype(BF16)
    )


def dispatch_x(route, placement, x_rows, capacity, local_count, chunks):
    row_count, hidden = x_rows.shape
    places = placement.shape[0] * capacity
    out = pl.pallas_call(
        functools.partial(dispatch_x_kernel, capacity, local_count, chunks > 1),
        out_shape=(jax.ShapeDtypeStruct((1, row_count), jnp.int32),)
        + (jax.ShapeDtypeStruct((places // chunks, hidden), BF16),) * chunks,
        compiler_params=params(),
        cost_estimate=cost(2 * places * row_count * hidden, 2 * (places + row_count) * hidden),
        name="dispatch_x",
    )(route.reshape(1, row_count), placement.reshape(-1, 1), x_rows)
    return out[0], list(out[1:])


def dispatch_g_kernel(target_ref, g_ref, *chunk_refs):
    places = place_matrix(target_ref[...], len(chunk_refs) * chunk_refs[0].shape[0])
    write_chunks(
        chunk_refs, jnp.dot(places, g_ref[...], preferred_element_type=F32).astype(BF16)
    )


def dispatch_g(target, y_cot, places, chunks):
    row_count, width = y_cot.shape
    tile = min(width, 512)
    rows = places // chunks
    return list(pl.pallas_call(
        dispatch_g_kernel,
        grid=(width // tile,),
        in_specs=[
            pl.BlockSpec((1, row_count), lambda j: (0, 0)),
            pl.BlockSpec((row_count, tile), lambda j: (0, j)),
        ],
        out_specs=(pl.BlockSpec((rows, tile), lambda j: (0, j)),) * chunks,
        out_shape=(jax.ShapeDtypeStruct((rows, width), BF16),) * chunks,
        compiler_params=params("arbitrary"),
        cost_estimate=cost(2 * places * row_count * width, 2 * (places + row_count) * width),
        name="dispatch_g",
    )(target, y_cot))


def collect_kernel(target_ref, *refs):
    chunk_refs, out_ref = refs[:-1], refs[-1]
    home = read_chunks(chunk_refs)
    places = place_matrix(target_ref[...], home.shape[0])
    out_ref[...] = lax.dot_general(
        places, home, (((0,), (0,)), ((), ())), preferred_element_type=F32
    ).astype(BF16)


def collect(target, home, name):
    rows, width = home[0].shape
    places = rows * len(home)
    row_count = target.shape[1]
    tile = min(width, 512)
    return pl.pallas_call(
        collect_kernel,
        grid=(width // tile,),
        in_specs=[pl.BlockSpec((1, row_count), lambda j: (0, 0))]
        + [pl.BlockSpec((rows, tile), lambda j: (0, j))] * len(home),
        out_specs=pl.BlockSpec((row_count, tile), lambda j: (0, j)),
        out_shape=jax.ShapeDtypeStruct((row_count, width), BF16),
        compiler_params=params("arbitrary"),
        cost_estimate=cost(2 * places * row_count * width, 2 * (places + row_count) * width),
        name=name,
    )(target, *home)


def member_rows(rows, capacity, local_count):
    index = lax.broadcasted_iota(jnp.int32, (rows, 1), 0)
    return lax.rem(index, capacity * local_count) // capacity


def spread(x, capacity, local_count):
    member = member_rows(x.shape[0], capacity, local_count)
    zero = jnp.zeros_like(x)
    return jnp.concatenate([jnp.where(member == e, x, zero) for e in range(local_count)], axis=1)


def join_weight(piece_refs, joined_ref):
    local_count, rows, width = piece_refs[0].shape
    if len(piece_refs) == 1:
        return piece_refs[0][...].reshape(local_count * rows, width)
    here = lax.axis_index("rep")
    for i, ref in enumerate(piece_refs):
        owner = jnp.bitwise_xor(here, i)
        for e in range(local_count):
            joined_ref[e, owner] = ref[e]
    return joined_ref[...].reshape(local_count * len(piece_refs) * rows, width)


def joined_scratch(pieces, tile):
    local_count, rows, _ = pieces[0].shape
    return pltpu.VMEM((local_count, len(pieces), rows, tile), BF16)


def forward_kernel(capacity, local_count, chunks, pieces, *refs):
    x_refs, w_refs = refs[:chunks], refs[chunks : chunks + pieces]
    y_refs, joined_ref = refs[chunks + pieces : -1], refs[-1]
    wide = spread(read_chunks(x_refs), capacity, local_count)
    weight = join_weight(w_refs, joined_ref)
    write_chunks(y_refs, jnp.dot(wide, weight, preferred_element_type=F32).astype(BF16))


def forward(x, weight, capacity):
    rows, hidden = x[0].shape
    local_count, slice_rows, width = weight[0].shape
    tile = min(width, 512)
    total = rows * len(x)
    return list(pl.pallas_call(
        functools.partial(forward_kernel, capacity, local_count, len(x), len(weight)),
        grid=(width // tile,),
        in_specs=[pl.BlockSpec((rows, hidden), lambda j: (0, 0))] * len(x)
        + [pl.BlockSpec((local_count, slice_rows, tile), lambda j: (0, 0, j))] * len(weight),
        out_specs=(pl.BlockSpec((rows, tile), lambda j: (0, j)),) * len(x),
        out_shape=(jax.ShapeDtypeStruct((rows, width), BF16),) * len(x),
        scratch_shapes=[joined_scratch(weight, tile)],
        compiler_params=params("arbitrary"),
        cost_estimate=cost(
            2 * total * local_count * hidden * width,
            2 * (local_count * hidden + total) * width,
        ),
        name="forward",
    )(*x, *weight))


def gradient_kernel(capacity, local_count, chunks, parts, factor, *refs):
    x_refs, g_refs = refs[:chunks], refs[chunks : 2 * chunks]
    wide = spread(read_chunks(x_refs), capacity, local_count)
    outer = lax.dot_general(
        wide, read_chunks(g_refs), (((0,), (0,)), ((), ())), preferred_element_type=F32
    )
    low = (outer * factor).astype(BF16)
    if parts == 1:
        out_ref = refs[-1]
        out_ref[...] = low.reshape(out_ref.shape)
        return
    out_refs, split_ref = refs[2 * chunks : -1], refs[-1]
    split_ref[...] = low.reshape(split_ref.shape)
    here = lax.axis_index("rep")
    for i, out_ref in enumerate(out_refs):
        owner = jnp.bitwise_xor(here, i)
        for e in range(local_count):
            out_ref[e] = split_ref[e, owner]


def gradient(x, g, capacity, local_count, parts, factor):
    rows, hidden = x[0].shape
    width = g[0].shape[1]
    tile = min(width, 512)
    total = rows * len(x)
    slice_rows = hidden // parts
    return list(pl.pallas_call(
        functools.partial(gradient_kernel, capacity, local_count, len(x), parts, factor),
        grid=(width // tile,),
        in_specs=[pl.BlockSpec((rows, hidden), lambda j: (0, 0))] * len(x)
        + [pl.BlockSpec((rows, tile), lambda j: (0, j))] * len(g),
        out_specs=(pl.BlockSpec((local_count, slice_rows, tile), lambda j: (0, 0, j)),) * parts,
        out_shape=(jax.ShapeDtypeStruct((local_count, slice_rows, width), BF16),) * parts,
        scratch_shapes=[pltpu.VMEM((local_count, parts, slice_rows, tile), BF16)]
        if parts > 1
        else [],
        compiler_params=params("arbitrary"),
        cost_estimate=cost(
            2 * total * local_count * hidden * width,
            2 * (local_count * hidden + total) * width,
        ),
        name="gradient",
    )(*x, *g))


def backward_kernel(capacity, local_count, chunks, pieces, *refs):
    g_refs, w_refs = refs[:chunks], refs[chunks : chunks + pieces]
    dx_refs, joined_ref, total_ref = refs[chunks + pieces : -2], refs[-2], refs[-1]
    step = pl.program_id(0)
    hidden = dx_refs[0].shape[1]
    part = lax.dot_general(
        read_chunks(g_refs), join_weight(w_refs, joined_ref), (((1,), (1,)), ((), ())),
        preferred_element_type=F32,
    )

    @pl.when(step == 0)
    def _():
        total_ref[...] = part

    @pl.when(step > 0)
    def _():
        total_ref[...] += part

    @pl.when(step == pl.num_programs(0) - 1)
    def _():
        member = member_rows(total_ref.shape[0], capacity, local_count)
        picked = total_ref[:, :hidden]
        for e in range(1, local_count):
            picked = jnp.where(member == e, total_ref[:, e * hidden : (e + 1) * hidden], picked)
        write_chunks(dx_refs, picked.astype(BF16))


def backward(g, weight, capacity):
    rows, width = g[0].shape
    local_count, slice_rows, _ = weight[0].shape
    hidden = slice_rows * len(weight)
    tile = min(width, 512)
    total = rows * len(g)
    return list(pl.pallas_call(
        functools.partial(backward_kernel, capacity, local_count, len(g), len(weight)),
        grid=(width // tile,),
        in_specs=[pl.BlockSpec((rows, tile), lambda j: (0, j))] * len(g)
        + [pl.BlockSpec((local_count, slice_rows, tile), lambda j: (0, 0, j))] * len(weight),
        out_specs=(pl.BlockSpec((rows, hidden), lambda j: (0, 0)),) * len(g),
        out_shape=(jax.ShapeDtypeStruct((rows, hidden), BF16),) * len(g),
        scratch_shapes=[
            joined_scratch(weight, tile),
            pltpu.VMEM((total, local_count * hidden), F32),
        ],
        compiler_params=params("arbitrary"),
        cost_estimate=cost(
            2 * total * local_count * hidden * width,
            2 * (local_count * hidden + total) * width,
        ),
        name="backward",
    )(*g, *weight))


def cast_kernel(w_ref, out_ref):
    out_ref[...] = w_ref[...].astype(BF16)


def cast_weight(weight):
    members, rows, width = weight.shape
    tile = min(width, 512)
    spec = pl.BlockSpec((members, rows, tile), lambda j: (0, 0, j))
    return pl.pallas_call(
        cast_kernel,
        grid=(width // tile,),
        in_specs=[spec],
        out_specs=spec,
        out_shape=jax.ShapeDtypeStruct(weight.shape, BF16),
        compiler_params=params("arbitrary"),
        cost_estimate=cost(weight.size, 6 * weight.size),
        name="cast_weight",
    )(weight)


def add_kernel(a_ref, b_ref, out_ref):
    out_ref[...] = (a_ref[...].astype(F32) + b_ref[...].astype(F32)).astype(BF16)


def add_parts(a, b):
    members, rows, width = a.shape
    tile = min(width, 1024)
    spec = pl.BlockSpec((members, rows, tile), lambda j: (0, 0, j))
    return pl.pallas_call(
        add_kernel,
        grid=(width // tile,),
        in_specs=[spec, spec],
        out_specs=spec,
        out_shape=jax.ShapeDtypeStruct(a.shape, BF16),
        compiler_params=params("arbitrary"),
        cost_estimate=cost(a.size, 6 * a.size),
        name="add_parts",
    )(a, b)


def adam_kernel(
    parts, master_ref, mc_ref, ms_ref, vc_ref, vs_ref, *refs
):
    grad_refs = refs[:parts]
    master_out, mc_out, ms_out, vc_out, vs_out = refs[parts:]
    blocks = ms_ref.shape[1]
    rows = ms_ref.shape[2]
    corr_one = 1.0 - beta_one**ADAM_STEP
    corr_two = 1.0 - beta_two**ADAM_STEP
    m_scales = (ms_ref[0] * beta_one).T
    v_scales = (vs_ref[0] * beta_two).T
    lane = lax.broadcasted_iota(jnp.int32, (rows, blocks), 1)
    m_tops = jnp.zeros((rows, blocks), F32)
    v_tops = jnp.zeros((rows, blocks), F32)
    for b in range(blocks):
        cols = slice(b * BLOCK, (b + 1) * BLOCK)
        grad = grad_refs[0][0, :, cols].astype(F32)
        for ref in grad_refs[1:]:
            grad = grad + ref[0, :, cols].astype(F32)
        m_next = mc_ref[0, :, cols].astype(F32) * m_scales[:, b : b + 1] + (1.0 - beta_one) * grad
        v_next = vc_ref[0, :, cols].astype(F32) * v_scales[:, b : b + 1] + (
            1.0 - beta_two
        ) * (grad * grad)
        v_hat = v_next * (1.0 / corr_two)
        root = v_hat * lax.rsqrt(v_hat) + 1e-08
        master_out[0, :, cols] = master_ref[0, :, cols] - (learn_rate / corr_one) * m_next / root
        m_top = jnp.max(jnp.abs(m_next), axis=-1, keepdims=True) + 1e-06
        v_top = jnp.max(v_next, axis=-1, keepdims=True) + 1e-06
        mc_out[0, :, cols] = (m_next * (1.0 / m_top)).astype(BF16)
        vc_out[0, :, cols] = (v_next * (1.0 / v_top)).astype(BF16)
        m_tops = jnp.where(lane == b, m_top, m_tops)
        v_tops = jnp.where(lane == b, v_top, v_tops)
    ms_out[0] = m_tops.T
    vs_out[0] = v_tops.T


def adam(master_weight, grads, m_code, m_scale, v_code, v_scale):
    members, rows, width = master_weight.shape
    blocks = m_scale.shape[-1]
    count = 8 if blocks % 8 == 0 else blocks
    big = pl.BlockSpec((1, rows, count * BLOCK), lambda e, j: (e, 0, j))
    small = pl.BlockSpec((1, count, rows), lambda e, j: (e, j, 0))
    scales = jax.ShapeDtypeStruct((members, blocks, rows), F32)
    master_next, m_code_next, m_scale_next, v_code_next, v_scale_next = pl.pallas_call(
        functools.partial(adam_kernel, len(grads)),
        grid=(members, blocks // count),
        in_specs=[big, big, small, big, small] + [big] * len(grads),
        out_specs=(big, big, small, big, small),
        out_shape=(
            jax.ShapeDtypeStruct(master_weight.shape, F32),
            jax.ShapeDtypeStruct(master_weight.shape, BF16),
            scales,
            jax.ShapeDtypeStruct(master_weight.shape, BF16),
            scales,
        ),
        compiler_params=params("arbitrary", "arbitrary"),
        cost_estimate=cost(40 * master_weight.size, 18 * master_weight.size),
        name="adam",
    )(master_weight, m_code, jnp.swapaxes(m_scale, 1, 2), v_code, jnp.swapaxes(v_scale, 1, 2), *grads)
    return (
        master_next,
        m_code_next,
        jnp.swapaxes(m_scale_next, 1, 2),
        v_code_next,
        jnp.swapaxes(v_scale_next, 1, 2),
    )


def swap(array, axis, offset):
    size = lax.axis_size(axis)
    return lax.ppermute(array, axis, [(i, i ^ offset) for i in range(size)])


def exchange(chunks, groups):
    if len(chunks) > 1:
        order = sorted(range(1, len(chunks)), reverse=True)
        moved = {k: swap(chunks[k], "grp", k) for k in order}
        return [chunks[0]] + [moved[k] for k in range(1, len(chunks))]
    places, width = chunks[0].shape
    parts = chunks[0].reshape(groups, places // groups, width)
    moved = lax.all_to_all(parts, "grp", split_axis=0, concat_axis=0, tiled=True)
    return [moved.reshape(places, width)]


def gather_weight(weight_slice, replicas):
    if replicas != 4:
        return [lax.all_gather(weight_slice, "rep", axis=1, tiled=True)]
    far = swap(weight_slice, "rep", 2)
    near = swap(weight_slice, "rep", 1)
    return [weight_slice, near, far, swap(far, "rep", 1)]


def sum_gradient(parts):
    if len(parts) != 4:
        return [lax.psum_scatter(parts[0], "rep", scatter_dimension=1, tiled=True)]
    far = swap(parts[3], "rep", 1)
    near = swap(parts[1], "rep", 1)
    return [parts[0], near, swap(add_parts(parts[2], far), "rep", 2)]


def per_device(master_weight, m_code, m_scale, v_code, v_scale, placement, route, x_rows, y_cot):
    local_count, slice_rows, _ = master_weight.shape
    row_count = x_rows.shape[0]
    expert_count = placement.shape[0]
    groups = lax.axis_size("grp")
    replicas = lax.axis_size("rep")
    grad_factor = float(row_count * groups * replicas // expert_count) ** (-0.5)
    capacity = max(2, (3 * row_count + 2 * expert_count - 1) // (2 * expert_count))
    places = expert_count * capacity
    chunks = groups if is_power_of_two(groups) and (places // groups) % 16 == 0 else 1

    target, send_x = dispatch_x(route, placement, x_rows, capacity, local_count, chunks)
    local_x = exchange(send_x, groups)
    send_g = dispatch_g(target, y_cot, places, chunks)
    local_g = exchange(send_g, groups)
    weight = gather_weight(cast_weight(master_weight), replicas)

    back_y = forward(local_x, weight, capacity)
    home_y = exchange(back_y, groups)

    parts = replicas if replicas == 4 else 1
    grads = sum_gradient(gradient(local_x, local_g, capacity, local_count, parts, grad_factor))
    back_dx = backward(local_g, weight, capacity)
    home_dx = exchange(back_dx, groups)

    updated = adam(master_weight, grads, m_code, m_scale, v_code, v_scale)
    x_grad = collect(target, home_dx, "collect_dx")
    y_rows = collect(target, home_y, "collect_y")
    return (y_rows, x_grad) + tuple(updated)


def solution(mesh):
    return jax.shard_map(
        per_device,
        mesh=mesh,
        in_specs=(
            P("grp", "rep", None),
            P("grp", "rep", None),
            P("grp", "rep", None),
            P("grp", "rep", None),
            P("grp", "rep", None),
            P(),
            P(("rep", "grp")),
            P(("rep", "grp"), None),
            P(("rep", "grp"), None),
        ),
        out_specs=(
            P(("rep", "grp"), None),
            P(("rep", "grp"), None),
            P("grp", "rep", None),
            P("grp", "rep", None),
            P("grp", "rep", None),
            P("grp", "rep", None),
            P("grp", "rep", None),
        ),
        check_vma=False,
    )
```

```python
import functools

import jax
import jax.numpy as jnp
from jax import lax
from jax.experimental import pallas as pl
from jax.experimental.pallas import tpu as pltpu
from jax.sharding import PartitionSpec as P

BLOCK = 128
ADAM_STEP = 100

beta_one = 0.9
beta_two = 0.95
learn_rate = 0.01

VMEM_LIMIT = 40 * 1024 * 1024
LARGE_LIMIT = 56 * 1024 * 1024
F32 = jnp.float32
BF16 = jnp.bfloat16


def cost(flops, nbytes):
    return pl.CostEstimate(flops=int(flops), bytes_accessed=int(nbytes), transcendentals=0)


def params(*semantics):
    if semantics:
        return pltpu.CompilerParams(vmem_limit_bytes=VMEM_LIMIT, dimension_semantics=semantics)
    return pltpu.CompilerParams(vmem_limit_bytes=VMEM_LIMIT)


def row_targets(route_row, placement_row, capacity):
    expert_count = placement_row.shape[1]
    row_count = route_row.shape[1]
    diagonal = lax.broadcasted_iota(jnp.int32, (expert_count, expert_count), 0) == (
        lax.broadcasted_iota(jnp.int32, (expert_count, expert_count), 1)
    )
    placement_col = jnp.sum(
        jnp.where(diagonal, placement_row, 0).astype(F32), axis=1, keepdims=True
    )
    hot = (placement_col == route_row.astype(F32)).astype(F32)
    earlier = lax.broadcasted_iota(jnp.int32, (row_count, row_count), 0)
    later = lax.broadcasted_iota(jnp.int32, (row_count, row_count), 1)
    before = (earlier < later).astype(F32).astype(BF16)
    position = jnp.dot(hot.astype(BF16), before, preferred_element_type=F32)
    slot = lax.broadcasted_iota(jnp.int32, (expert_count, row_count), 0)
    start = (slot * capacity).astype(F32)
    return jnp.sum(hot * (start + position), axis=0, keepdims=True).astype(jnp.int32)


def place_matrix(target, places):
    slots = lax.broadcasted_iota(jnp.int32, (places, target.shape[1]), 0)
    return (slots == target).astype(F32).astype(BF16)


def dispatch_kernel(
    capacity, route_ref, placement_ref, x_hbm, g_hbm, sent_hbm, target_ref,
    x_ref, g_ref, sent_ref, in_sems, out_sems,
):
    tiles, _, tile = g_ref.shape
    width = tiles * tile
    hidden = x_ref.shape[1]
    loads = [
        pltpu.make_async_copy(
            g_hbm.at[:, pl.ds(j * tile, tile)], g_ref.at[j], in_sems.at[j]
        )
        for j in range(tiles)
    ]
    loads.append(pltpu.make_async_copy(x_hbm, x_ref, in_sems.at[tiles]))
    for load in loads:
        load.start()
    target = row_targets(route_ref[...], placement_ref[...], capacity)
    target_ref[...] = target
    places = place_matrix(target, sent_ref.shape[0])
    stores = []
    for j in range(tiles + 1):
        loads[j].wait()
        columns = pl.ds(j * tile, tile if j < tiles else hidden)
        rows = g_ref[j] if j < tiles else x_ref[...]
        sent_ref[:, columns] = jnp.dot(places, rows, preferred_element_type=F32).astype(BF16)
        store = pltpu.make_async_copy(
            sent_ref.at[:, columns], sent_hbm.at[:, columns], out_sems.at[j]
        )
        store.start()
        stores.append(store)
    for store in stores:
        store.wait()


def dispatch(route, placement, x_rows, y_cot, capacity):
    row_count, hidden = x_rows.shape
    width = y_cot.shape[1]
    tile = min(width, 512)
    tiles = width // tile
    places = placement.shape[0] * capacity
    whole = pl.BlockSpec(memory_space=pltpu.VMEM)
    hbm = pl.BlockSpec(memory_space=pl.ANY)
    return pl.pallas_call(
        functools.partial(dispatch_kernel, capacity),
        in_specs=[whole, whole, hbm, hbm],
        out_specs=(hbm, whole),
        out_shape=(
            jax.ShapeDtypeStruct((places, width + hidden), BF16),
            jax.ShapeDtypeStruct((1, row_count), jnp.int32),
        ),
        scratch_shapes=[
            pltpu.VMEM((row_count, hidden), BF16),
            pltpu.VMEM((tiles, row_count, tile), BF16),
            pltpu.VMEM((places, width + hidden), BF16),
            pltpu.SemaphoreType.DMA((tiles + 1,)),
            pltpu.SemaphoreType.DMA((tiles + 1,)),
        ],
        compiler_params=pltpu.CompilerParams(vmem_limit_bytes=LARGE_LIMIT),
        cost_estimate=cost(
            2 * places * row_count * (hidden + width), 2 * (places + row_count) * (hidden + width)
        ),
        name="dispatch",
    )(route.reshape(1, row_count), placement.reshape(1, -1), x_rows, y_cot)


def home_places_kernel(target_ref, out_ref):
    target = target_ref[...]
    slots = lax.broadcasted_iota(jnp.int32, (out_ref.shape[1], target.shape[1]), 0)
    out_ref[...] = (slots == target).astype(F32).T.astype(BF16)


def home_places(target, places):
    return pl.pallas_call(
        home_places_kernel,
        out_shape=jax.ShapeDtypeStruct((target.shape[1], places), BF16),
        compiler_params=params(),
        cost_estimate=cost(places * target.shape[1], 2 * places * target.shape[1]),
        name="home_places",
    )(target)


def hidden_specs(rows, hidden, width):
    return [
        pl.BlockSpec((rows, BLOCK), functools.partial(lambda k, j: (0, k), width // BLOCK + i))
        for i in range(hidden // BLOCK)
    ]


def read_columns(refs):
    return jnp.concatenate([ref[...] for ref in refs], axis=1)


def collect_kernel(places_ref, home_ref, *refs):
    hidden_refs, y_ref, dx_ref = refs[:-2], refs[-2], refs[-1]
    places = places_ref[...]
    y_ref[...] = jnp.dot(places, home_ref[...], preferred_element_type=F32).astype(BF16)

    @pl.when(pl.program_id(0) == 0)
    def _():
        dx_ref[...] = jnp.dot(
            places, read_columns(hidden_refs), preferred_element_type=F32
        ).astype(BF16)


def collect(places, home, hidden):
    total, width = home.shape
    width -= hidden
    row_count = places.shape[0]
    tile = min(width, 512)
    specs = hidden_specs(total, hidden, width)
    return pl.pallas_call(
        collect_kernel,
        grid=(width // tile,),
        in_specs=[
            pl.BlockSpec((row_count, total), lambda j: (0, 0)),
            pl.BlockSpec((total, tile), lambda j: (0, j)),
        ]
        + specs,
        out_specs=(
            pl.BlockSpec((row_count, tile), lambda j: (0, j)),
            pl.BlockSpec((row_count, hidden), lambda j: (0, 0)),
        ),
        out_shape=(
            jax.ShapeDtypeStruct((row_count, width), BF16),
            jax.ShapeDtypeStruct((row_count, hidden), BF16),
        ),
        compiler_params=params("arbitrary"),
        cost_estimate=cost(
            2 * total * row_count * (hidden + width), 2 * (total + row_count) * (hidden + width)
        ),
        name="collect",
    )(places, *([home] * (1 + len(specs))))


def member_rows(rows, capacity, local_count):
    index = lax.broadcasted_iota(jnp.int32, (rows, 1), 0)
    return lax.rem(index, capacity * local_count) // capacity


def spread(x, capacity, local_count):
    member = member_rows(x.shape[0], capacity, local_count)
    zero = jnp.zeros_like(x)
    return jnp.concatenate([jnp.where(member == e, x, zero) for e in range(local_count)], axis=1)


def products_kernel(capacity, local_count, g_ref, w_ref, *refs):
    x_refs, out_ref, wide_ref, total_ref = refs[:-3], refs[-3], refs[-2], refs[-1]
    step = pl.program_id(0)
    tile = g_ref.shape[1]
    width = tile * pl.num_programs(0)
    weight = w_ref[...].reshape(wide_ref.shape[1], tile)

    @pl.when(step == 0)
    def _():
        wide_ref[...] = spread(read_columns(x_refs), capacity, local_count)
        total_ref[...] = jnp.zeros_like(total_ref)

    columns = pl.ds(pl.multiple_of(step * tile, tile), tile)
    out_ref[:, columns] = jnp.dot(
        wide_ref[...], weight, preferred_element_type=F32
    ).astype(BF16)
    total_ref[...] += lax.dot_general(
        g_ref[...], weight, (((1,), (1,)), ((), ())), preferred_element_type=F32
    )

    @pl.when(step == pl.num_programs(0) - 1)
    def _():
        hidden = wide_ref.shape[1] // local_count
        member = member_rows(total_ref.shape[0], capacity, local_count)
        picked = total_ref[:, :hidden]
        for e in range(1, local_count):
            picked = jnp.where(member == e, total_ref[:, e * hidden : (e + 1) * hidden], picked)
        out_ref[:, out_ref.shape[1] - hidden :] = picked.astype(BF16)


def products(local, weight, capacity):
    local_count, hidden, width = weight.shape
    total = local.shape[0]
    tile = min(width, 512)
    specs = hidden_specs(total, hidden, width)
    return pl.pallas_call(
        functools.partial(products_kernel, capacity, local_count),
        grid=(width // tile,),
        in_specs=[
            pl.BlockSpec((total, tile), lambda j: (0, j)),
            pl.BlockSpec((local_count, hidden, tile), lambda j: (0, 0, j)),
        ]
        + specs,
        out_specs=pl.BlockSpec(local.shape, lambda j: (0, 0)),
        out_shape=jax.ShapeDtypeStruct(local.shape, BF16),
        scratch_shapes=[
            pltpu.VMEM((total, local_count * hidden), BF16),
            pltpu.VMEM((total, local_count * hidden), F32),
        ],
        compiler_params=params("arbitrary"),
        cost_estimate=cost(
            4 * total * local_count * hidden * width,
            2 * (local_count * hidden + 2 * total) * width,
        ),
        name="products",
    )(local, weight, *([local] * len(specs)))


def gradient_kernel(capacity, local_count, parts, factor, g_ref, *refs):
    blocks = len(refs) - 2 - (parts if parts > 1 else 0)
    x_refs, wide_ref = refs[:blocks], refs[-1]
    out_refs = refs[blocks:-2] if parts > 1 else refs[blocks:-1]

    @pl.when(pl.program_id(0) == 0)
    def _():
        wide_ref[...] = spread(read_columns(x_refs), capacity, local_count)

    outer = lax.dot_general(
        wide_ref[...], g_ref[...], (((0,), (0,)), ((), ())), preferred_element_type=F32
    )
    low = (outer * factor).astype(BF16)
    if parts == 1:
        out_refs[0][...] = low.reshape(out_refs[0].shape)
        return
    split_ref = refs[-2]
    split_ref[...] = low.reshape(split_ref.shape)
    here = lax.axis_index("rep")
    for i, out_ref in enumerate(out_refs):
        owner = jnp.bitwise_xor(here, i)
        for e in range(local_count):
            out_ref[e] = split_ref[e, owner]


def gradient(local, hidden, capacity, local_count, parts, factor):
    total, width = local.shape
    width -= hidden
    tile = min(width, 512)
    slice_rows = hidden // parts
    specs = hidden_specs(total, hidden, width)
    split = [pltpu.VMEM((local_count, parts, slice_rows, tile), BF16)] if parts > 1 else []
    return list(pl.pallas_call(
        functools.partial(gradient_kernel, capacity, local_count, parts, factor),
        grid=(width // tile,),
        in_specs=[pl.BlockSpec((total, tile), lambda j: (0, j))] + specs,
        out_specs=(pl.BlockSpec((local_count, slice_rows, tile), lambda j: (0, 0, j)),) * parts,
        out_shape=(jax.ShapeDtypeStruct((local_count, slice_rows, width), BF16),) * parts,
        scratch_shapes=split + [pltpu.VMEM((total, local_count * hidden), BF16)],
        compiler_params=params("arbitrary"),
        cost_estimate=cost(
            2 * total * local_count * hidden * width,
            2 * (local_count * hidden + total) * width,
        ),
        name="gradient",
    )(*([local] * (1 + len(specs)))))


def join_kernel(*refs):
    piece_refs, out_ref = refs[:-1], refs[-1]
    here = lax.axis_index("rep")
    for i, ref in enumerate(piece_refs):
        owner = jnp.bitwise_xor(here, i)
        for e in range(out_ref.shape[0]):
            out_ref[e, owner] = ref[e]


def join_weight(pieces):
    if len(pieces) == 1:
        return pieces[0]
    local_count, rows, width = pieces[0].shape
    count = len(pieces)
    tile = min(width, 512)
    joined = pl.pallas_call(
        join_kernel,
        grid=(width // tile,),
        in_specs=[pl.BlockSpec((local_count, rows, tile), lambda j: (0, 0, j))] * count,
        out_specs=pl.BlockSpec((local_count, count, rows, tile), lambda j: (0, 0, 0, j)),
        out_shape=jax.ShapeDtypeStruct((local_count, count, rows, width), BF16),
        compiler_params=params("arbitrary"),
        cost_estimate=cost(0, 4 * local_count * count * rows * width),
        name="join_weight",
    )(*pieces)
    return joined.reshape(local_count, count * rows, width)


def cast_kernel(w_ref, out_ref):
    out_ref[...] = w_ref[...].astype(BF16)


def cast_weight(weight):
    members, rows, width = weight.shape
    tile = min(width, 512)
    spec = pl.BlockSpec((members, rows, tile), lambda j: (0, 0, j))
    return pl.pallas_call(
        cast_kernel,
        grid=(width // tile,),
        in_specs=[spec],
        out_specs=spec,
        out_shape=jax.ShapeDtypeStruct(weight.shape, BF16),
        compiler_params=params("arbitrary"),
        cost_estimate=cost(weight.size, 6 * weight.size),
        name="cast_weight",
    )(weight)


def add_kernel(a_ref, b_ref, out_ref):
    out_ref[...] = (a_ref[...].astype(F32) + b_ref[...].astype(F32)).astype(BF16)


def add_parts(a, b):
    members, rows, width = a.shape
    tile = min(width, 1024)
    spec = pl.BlockSpec((members, rows, tile), lambda j: (0, 0, j))
    return pl.pallas_call(
        add_kernel,
        grid=(width // tile,),
        in_specs=[spec, spec],
        out_specs=spec,
        out_shape=jax.ShapeDtypeStruct(a.shape, BF16),
        compiler_params=params("arbitrary"),
        cost_estimate=cost(a.size, 6 * a.size),
        name="add_parts",
    )(a, b)


def adam_kernel(
    parts, master_ref, mc_ref, ms_ref, vc_ref, vs_ref, *refs
):
    grad_refs = refs[:parts]
    master_out, mc_out, ms_out, vc_out, vs_out = refs[parts:]
    blocks = ms_ref.shape[1]
    rows = ms_ref.shape[2]
    corr_one = 1.0 - beta_one**ADAM_STEP
    corr_two = 1.0 - beta_two**ADAM_STEP
    m_scales = (ms_ref[0] * beta_one).T
    v_scales = (vs_ref[0] * beta_two).T
    lane = lax.broadcasted_iota(jnp.int32, (rows, blocks), 1)
    m_tops = jnp.zeros((rows, blocks), F32)
    v_tops = jnp.zeros((rows, blocks), F32)
    for b in range(blocks):
        cols = slice(b * BLOCK, (b + 1) * BLOCK)
        grad = grad_refs[0][0, :, cols].astype(F32)
        for ref in grad_refs[1:]:
            grad = grad + ref[0, :, cols].astype(F32)
        m_next = mc_ref[0, :, cols].astype(F32) * m_scales[:, b : b + 1] + (1.0 - beta_one) * grad
        v_next = vc_ref[0, :, cols].astype(F32) * v_scales[:, b : b + 1] + (
            1.0 - beta_two
        ) * (grad * grad)
        v_hat = v_next * (1.0 / corr_two)
        root = v_hat * lax.rsqrt(v_hat) + 1e-08
        master_out[0, :, cols] = master_ref[0, :, cols] - (learn_rate / corr_one) * m_next / root
        m_top = jnp.max(jnp.abs(m_next), axis=-1, keepdims=True) + 1e-06
        v_top = jnp.max(v_next, axis=-1, keepdims=True) + 1e-06
        mc_out[0, :, cols] = (m_next * (1.0 / m_top)).astype(BF16)
        vc_out[0, :, cols] = (v_next * (1.0 / v_top)).astype(BF16)
        m_tops = jnp.where(lane == b, m_top, m_tops)
        v_tops = jnp.where(lane == b, v_top, v_tops)
    ms_out[0] = m_tops.T
    vs_out[0] = v_tops.T


def adam(master_weight, grads, m_code, m_scale, v_code, v_scale):
    members, rows, width = master_weight.shape
    blocks = m_scale.shape[-1]
    count = 8 if blocks % 8 == 0 else blocks
    big = pl.BlockSpec((1, rows, count * BLOCK), lambda e, j: (e, 0, j))
    small = pl.BlockSpec((1, count, rows), lambda e, j: (e, j, 0))
    scales = jax.ShapeDtypeStruct((members, blocks, rows), F32)
    master_next, m_code_next, m_scale_next, v_code_next, v_scale_next = pl.pallas_call(
        functools.partial(adam_kernel, len(grads)),
        grid=(members, blocks // count),
        in_specs=[big, big, small, big, small] + [big] * len(grads),
        out_specs=(big, big, small, big, small),
        out_shape=(
            jax.ShapeDtypeStruct(master_weight.shape, F32),
            jax.ShapeDtypeStruct(master_weight.shape, BF16),
            scales,
            jax.ShapeDtypeStruct(master_weight.shape, BF16),
            scales,
        ),
        compiler_params=params("arbitrary", "arbitrary"),
        cost_estimate=cost(40 * master_weight.size, 18 * master_weight.size),
        name="adam",
    )(master_weight, m_code, jnp.swapaxes(m_scale, 1, 2), v_code, jnp.swapaxes(v_scale, 1, 2), *grads)
    return (
        master_next,
        m_code_next,
        jnp.swapaxes(m_scale_next, 1, 2),
        v_code_next,
        jnp.swapaxes(v_scale_next, 1, 2),
    )


def swap(array, axis, offset):
    size = lax.axis_size(axis)
    return lax.ppermute(array, axis, [(i, i ^ offset) for i in range(size)])


def exchange(buffer, groups):
    places, width = buffer.shape
    parts = buffer.reshape(groups, places // groups, width)
    moved = lax.all_to_all(parts, "grp", split_axis=0, concat_axis=0, tiled=True)
    return moved.reshape(places, width)


def gather_weight(weight_slice, replicas):
    if replicas != 4:
        return [lax.all_gather(weight_slice, "rep", axis=1, tiled=True)]
    far = swap(weight_slice, "rep", 2)
    near = swap(weight_slice, "rep", 1)
    return [weight_slice, near, far, swap(far, "rep", 1)]


def sum_gradient(parts):
    if len(parts) != 4:
        return [lax.psum_scatter(parts[0], "rep", scatter_dimension=1, tiled=True)]
    far = swap(parts[3], "rep", 1)
    near = swap(parts[1], "rep", 1)
    return [parts[0], near, swap(add_parts(parts[2], far), "rep", 2)]


def per_device(master_weight, m_code, m_scale, v_code, v_scale, placement, route, x_rows, y_cot):
    local_count = master_weight.shape[0]
    row_count = x_rows.shape[0]
    expert_count = placement.shape[0]
    groups = lax.axis_size("grp")
    replicas = lax.axis_size("rep")
    grad_factor = float(row_count * groups * replicas // expert_count) ** (-0.5)
    capacity = max(2, (3 * row_count + 2 * expert_count - 1) // (2 * expert_count))
    places = expert_count * capacity
    sent, target = dispatch(route, placement, x_rows, y_cot, capacity)
    local = exchange(sent, groups)
    early_master, target = lax.optimization_barrier((master_weight, target))
    weight = join_weight(gather_weight(cast_weight(early_master), replicas))
    results = products(local, weight, capacity)
    local, results = lax.optimization_barrier((local, results))
    home = exchange(results, groups)

    parts = replicas if replicas == 4 else 1
    hidden = x_rows.shape[1]
    grads = sum_gradient(gradient(local, hidden, capacity, local_count, parts, grad_factor))
    updated = adam(master_weight, grads, m_code, m_scale, v_code, v_scale)
    y_rows, x_grad = collect(home_places(target, places), home, hidden)
    return (y_rows, x_grad) + tuple(updated)


def solution(mesh):
    return jax.shard_map(
        per_device,
        mesh=mesh,
        in_specs=(
            P("grp", "rep", None),
            P("grp", "rep", None),
            P("grp", "rep", None),
            P("grp", "rep", None),
            P("grp", "rep", None),
            P(),
            P(("rep", "grp")),
            P(("rep", "grp"), None),
            P(("rep", "grp"), None),
        ),
        out_specs=(
            P(("rep", "grp"), None),
            P(("rep", "grp"), None),
            P("grp", "rep", None),
            P("grp", "rep", None),
            P("grp", "rep", None),
            P("grp", "rep", None),
            P("grp", "rep", None),
        ),
        check_vma=False,
    )
```

```python
import functools

import jax
import jax.numpy as jnp
from jax import lax
from jax.experimental import pallas as pl
from jax.experimental.pallas import tpu as pltpu
from jax.sharding import PartitionSpec as P

BLOCK = 128
ADAM_STEP = 100

beta_one = 0.9
beta_two = 0.95
learn_rate = 0.01

VMEM_LIMIT = 40 * 1024 * 1024
LARGE_LIMIT = 56 * 1024 * 1024
F32 = jnp.float32
BF16 = jnp.bfloat16


def cost(flops, nbytes):
    return pl.CostEstimate(flops=int(flops), bytes_accessed=int(nbytes), transcendentals=0)


def params(*semantics):
    if semantics:
        return pltpu.CompilerParams(vmem_limit_bytes=VMEM_LIMIT, dimension_semantics=semantics)
    return pltpu.CompilerParams(vmem_limit_bytes=VMEM_LIMIT)


def row_targets(route_row, placement_row, capacity):
    expert_count = placement_row.shape[1]
    row_count = route_row.shape[1]
    diagonal = lax.broadcasted_iota(jnp.int32, (expert_count, expert_count), 0) == (
        lax.broadcasted_iota(jnp.int32, (expert_count, expert_count), 1)
    )
    placement_col = jnp.sum(
        jnp.where(diagonal, placement_row, 0).astype(F32), axis=1, keepdims=True
    )
    hot = (placement_col == route_row.astype(F32)).astype(F32)
    earlier = lax.broadcasted_iota(jnp.int32, (row_count, row_count), 0)
    later = lax.broadcasted_iota(jnp.int32, (row_count, row_count), 1)
    before = (earlier < later).astype(F32).astype(BF16)
    position = jnp.dot(hot.astype(BF16), before, preferred_element_type=F32)
    slot = lax.broadcasted_iota(jnp.int32, (expert_count, row_count), 0)
    start = (slot * capacity).astype(F32)
    return jnp.sum(hot * (start + position), axis=0, keepdims=True).astype(jnp.int32)


def place_matrix(target, places):
    slots = lax.broadcasted_iota(jnp.int32, (places, target.shape[1]), 0)
    return (slots == target).astype(F32).astype(BF16)


def dispatch_kernel(
    capacity, route_hbm, placement_hbm, x_hbm, g_hbm, sent_hbm, target_hbm,
    route_ref, placement_ref, target_ref, x_ref, g_ref, sent_ref, key_sems, in_sems, out_sems,
):
    tiles, _, tile = g_ref.shape
    hidden = x_ref.shape[1]
    keys = [
        pltpu.make_async_copy(route_hbm, route_ref, key_sems.at[0]),
        pltpu.make_async_copy(placement_hbm, placement_ref, key_sems.at[1]),
    ]
    loads = [
        pltpu.make_async_copy(
            g_hbm.at[:, pl.ds(j * tile, tile)], g_ref.at[j], in_sems.at[j]
        )
        for j in range(tiles)
    ]
    loads.append(pltpu.make_async_copy(x_hbm, x_ref, in_sems.at[tiles]))
    for load in keys + loads:
        load.start()
    for load in keys:
        load.wait()
    target = row_targets(route_ref[...], placement_ref[...], capacity)
    target_ref[...] = target
    stores = [pltpu.make_async_copy(target_ref, target_hbm, key_sems.at[2])]
    stores[0].start()
    places = place_matrix(target, sent_ref.shape[0])
    for j in range(tiles + 1):
        loads[j].wait()
        columns = pl.ds(j * tile, tile if j < tiles else hidden)
        rows = g_ref[j] if j < tiles else x_ref[...]
        sent_ref[:, columns] = jnp.dot(places, rows, preferred_element_type=F32).astype(BF16)
        store = pltpu.make_async_copy(
            sent_ref.at[:, columns], sent_hbm.at[:, columns], out_sems.at[j]
        )
        store.start()
        stores.append(store)
    for store in stores:
        store.wait()


def dispatch(route, placement, x_rows, y_cot, capacity):
    row_count, hidden = x_rows.shape
    width = y_cot.shape[1]
    expert_count = placement.shape[0]
    tile = min(width, 512)
    tiles = width // tile
    places = expert_count * capacity
    hbm = pl.BlockSpec(memory_space=pl.ANY)
    return pl.pallas_call(
        functools.partial(dispatch_kernel, capacity),
        in_specs=[hbm, hbm, hbm, hbm],
        out_specs=(hbm, hbm),
        out_shape=(
            jax.ShapeDtypeStruct((places, width + hidden), BF16),
            jax.ShapeDtypeStruct((1, row_count), jnp.int32),
        ),
        scratch_shapes=[
            pltpu.VMEM((1, row_count), jnp.int32),
            pltpu.VMEM((1, expert_count), jnp.int32),
            pltpu.VMEM((1, row_count), jnp.int32),
            pltpu.VMEM((row_count, hidden), BF16),
            pltpu.VMEM((tiles, row_count, tile), BF16),
            pltpu.VMEM((places, width + hidden), BF16),
            pltpu.SemaphoreType.DMA((3,)),
            pltpu.SemaphoreType.DMA((tiles + 1,)),
            pltpu.SemaphoreType.DMA((tiles + 1,)),
        ],
        compiler_params=pltpu.CompilerParams(vmem_limit_bytes=LARGE_LIMIT),
        cost_estimate=cost(
            2 * places * row_count * (hidden + width), 2 * (places + row_count) * (hidden + width)
        ),
        name="dispatch",
    )(route.reshape(1, row_count), placement.reshape(1, -1), x_rows, y_cot)


def home_places_kernel(target_ref, out_ref):
    target = target_ref[...]
    slots = lax.broadcasted_iota(jnp.int32, (out_ref.shape[1], target.shape[1]), 0)
    out_ref[...] = (slots == target).astype(F32).T.astype(BF16)


def home_places(target, places):
    return pl.pallas_call(
        home_places_kernel,
        out_shape=jax.ShapeDtypeStruct((target.shape[1], places), BF16),
        compiler_params=params(),
        cost_estimate=cost(places * target.shape[1], 2 * places * target.shape[1]),
        name="home_places",
    )(target)


def hidden_specs(rows, hidden, width):
    return [
        pl.BlockSpec((rows, BLOCK), functools.partial(lambda k, j: (0, k), width // BLOCK + i))
        for i in range(hidden // BLOCK)
    ]


def read_columns(refs):
    return jnp.concatenate([ref[...] for ref in refs], axis=1)


def collect_kernel(
    places_ref, home_hbm, y_hbm, dx_hbm, home_ref, y_ref, dx_ref, in_sems, out_sems
):
    hidden = dx_ref.shape[1]
    width = y_ref.shape[1]
    tiles = in_sems.shape[0] - 1
    tile = width // tiles
    spans = [pl.ds(j * tile, tile) for j in range(tiles)] + [pl.ds(width, hidden)]
    loads = [
        pltpu.make_async_copy(home_hbm.at[:, span], home_ref.at[:, span], in_sems.at[j])
        for j, span in enumerate(spans)
    ]
    for load in loads:
        load.start()
    places = places_ref[...]
    stores = []
    for j, span in enumerate(spans):
        loads[j].wait()
        rows = jnp.dot(places, home_ref[:, span], preferred_element_type=F32).astype(BF16)
        if j < tiles:
            y_ref[:, span] = rows
            store = pltpu.make_async_copy(y_ref.at[:, span], y_hbm.at[:, span], out_sems.at[j])
        else:
            dx_ref[...] = rows
            store = pltpu.make_async_copy(dx_ref, dx_hbm, out_sems.at[j])
        store.start()
        stores.append(store)
    for store in stores:
        store.wait()


def collect(places, home, hidden):
    total, width = home.shape
    width -= hidden
    row_count = places.shape[0]
    tiles = width // min(width, 512)
    whole = pl.BlockSpec(memory_space=pltpu.VMEM)
    hbm = pl.BlockSpec(memory_space=pl.ANY)
    return pl.pallas_call(
        collect_kernel,
        in_specs=[whole, hbm],
        out_specs=(hbm, hbm),
        out_shape=(
            jax.ShapeDtypeStruct((row_count, width), BF16),
            jax.ShapeDtypeStruct((row_count, hidden), BF16),
        ),
        scratch_shapes=[
            pltpu.VMEM((total, width + hidden), BF16),
            pltpu.VMEM((row_count, width), BF16),
            pltpu.VMEM((row_count, hidden), BF16),
            pltpu.SemaphoreType.DMA((tiles + 1,)),
            pltpu.SemaphoreType.DMA((tiles + 1,)),
        ],
        compiler_params=params(),
        cost_estimate=cost(
            2 * total * row_count * (hidden + width), 2 * (total + row_count) * (hidden + width)
        ),
        name="collect",
    )(places, home)


def member_rows(rows, capacity, local_count):
    index = lax.broadcasted_iota(jnp.int32, (rows, 1), 0)
    return lax.rem(index, capacity * local_count) // capacity


def spread(x, capacity, local_count):
    member = member_rows(x.shape[0], capacity, local_count)
    zero = jnp.zeros_like(x)
    return jnp.concatenate([jnp.where(member == e, x, zero) for e in range(local_count)], axis=1)


def products_kernel(capacity, pieces, local_hbm, *refs):
    w_hbm, out_hbm = refs[:pieces], refs[pieces]
    x_ref, g_ref, w_ref, out_ref, x_sem, g_sems, w_sems, out_sems = refs[pieces + 1 :]
    tiles, local_count, _, _, tile = w_ref.shape
    total, hidden = x_ref.shape
    width = tiles * tile
    here = lax.axis_index("rep") if pieces > 1 else 0
    x_load = pltpu.make_async_copy(local_hbm.at[:, pl.ds(width, hidden)], x_ref, x_sem)
    x_load.start()
    loads = []
    for j in range(tiles):
        span = pl.ds(j * tile, tile)
        loads.append([])
        for i, piece in enumerate(w_hbm):
            owner = jnp.bitwise_xor(here, i) if pieces > 1 else 0
            for e in range(local_count):
                loads[j].append(
                    pltpu.make_async_copy(
                        piece.at[e, :, span], w_ref.at[j, e, owner], w_sems.at[j, i, e]
                    )
                )
        loads[j].append(
            pltpu.make_async_copy(local_hbm.at[:, span], g_ref.at[j], g_sems.at[j])
        )
        for load in loads[j]:
            load.start()
    x_load.wait()
    wide = spread(x_ref[...], capacity, local_count)
    sums = None
    stores = []
    for j in range(tiles):
        span = pl.ds(j * tile, tile)
        for load in loads[j]:
            load.wait()
        weight = w_ref[j].reshape(local_count * hidden, tile)
        out_ref[:, span] = jnp.dot(wide, weight, preferred_element_type=F32).astype(BF16)
        store = pltpu.make_async_copy(out_ref.at[:, span], out_hbm.at[:, span], out_sems.at[j])
        store.start()
        stores.append(store)
        part = lax.dot_general(
            g_ref[j], weight, (((1,), (1,)), ((), ())), preferred_element_type=F32
        )
        sums = part if sums is None else sums + part
    member = member_rows(total, capacity, local_count)
    picked = sums[:, :hidden]
    for e in range(1, local_count):
        picked = jnp.where(member == e, sums[:, e * hidden : (e + 1) * hidden], picked)
    span = pl.ds(width, hidden)
    out_ref[:, span] = picked.astype(BF16)
    store = pltpu.make_async_copy(out_ref.at[:, span], out_hbm.at[:, span], out_sems.at[tiles])
    store.start()
    stores.append(store)
    for store in stores:
        store.wait()


def products(local, weight, capacity):
    local_count, slice_rows, width = weight[0].shape
    pieces = len(weight)
    hidden = slice_rows * pieces
    total = local.shape[0]
    tile = min(width, 512)
    tiles = width // tile
    hbm = pl.BlockSpec(memory_space=pl.ANY)
    return pl.pallas_call(
        functools.partial(products_kernel, capacity, pieces),
        in_specs=[hbm] * (1 + pieces),
        out_specs=hbm,
        out_shape=jax.ShapeDtypeStruct(local.shape, BF16),
        scratch_shapes=[
            pltpu.VMEM((total, hidden), BF16),
            pltpu.VMEM((tiles, total, tile), BF16),
            pltpu.VMEM((tiles, local_count, pieces, slice_rows, tile), BF16),
            pltpu.VMEM(local.shape, BF16),
            pltpu.SemaphoreType.DMA,
            pltpu.SemaphoreType.DMA((tiles,)),
            pltpu.SemaphoreType.DMA((tiles, pieces, local_count)),
            pltpu.SemaphoreType.DMA((tiles + 1,)),
        ],
        compiler_params=pltpu.CompilerParams(vmem_limit_bytes=LARGE_LIMIT),
        cost_estimate=cost(
            4 * total * local_count * hidden * width,
            2 * (local_count * hidden + 2 * total) * width,
        ),
        name="products",
    )(local, *weight)


def gradient_kernel(capacity, local_count, parts, factor, g_ref, *refs):
    blocks = len(refs) - 2 - (parts if parts > 1 else 0)
    x_refs, wide_ref = refs[:blocks], refs[-1]
    out_refs = refs[blocks:-2] if parts > 1 else refs[blocks:-1]

    @pl.when(pl.program_id(0) == 0)
    def _():
        wide_ref[...] = spread(read_columns(x_refs), capacity, local_count)

    outer = lax.dot_general(
        wide_ref[...], g_ref[...], (((0,), (0,)), ((), ())), preferred_element_type=F32
    )
    low = (outer * factor).astype(BF16)
    if parts == 1:
        out_refs[0][...] = low.reshape(out_refs[0].shape)
        return
    split_ref = refs[-2]
    split_ref[...] = low.reshape(split_ref.shape)
    here = lax.axis_index("rep")
    for i, out_ref in enumerate(out_refs):
        owner = jnp.bitwise_xor(here, i)
        for e in range(local_count):
            out_ref[e] = split_ref[e, owner]


def gradient(local, hidden, capacity, local_count, parts, factor):
    total, width = local.shape
    width -= hidden
    tile = min(width, 512)
    slice_rows = hidden // parts
    specs = hidden_specs(total, hidden, width)
    split = [pltpu.VMEM((local_count, parts, slice_rows, tile), BF16)] if parts > 1 else []
    return list(pl.pallas_call(
        functools.partial(gradient_kernel, capacity, local_count, parts, factor),
        grid=(width // tile,),
        in_specs=[pl.BlockSpec((total, tile), lambda j: (0, j))] + specs,
        out_specs=(pl.BlockSpec((local_count, slice_rows, tile), lambda j: (0, 0, j)),) * parts,
        out_shape=(jax.ShapeDtypeStruct((local_count, slice_rows, width), BF16),) * parts,
        scratch_shapes=split + [pltpu.VMEM((total, local_count * hidden), BF16)],
        compiler_params=params("arbitrary"),
        cost_estimate=cost(
            2 * total * local_count * hidden * width,
            2 * (local_count * hidden + total) * width,
        ),
        name="gradient",
    )(*([local] * (1 + len(specs)))))


def cast_kernel(w_ref, out_ref):
    out_ref[...] = w_ref[...].astype(BF16)


def cast_weight(weight):
    members, rows, width = weight.shape
    tile = min(width, 512)
    spec = pl.BlockSpec((members, rows, tile), lambda j: (0, 0, j))
    return pl.pallas_call(
        cast_kernel,
        grid=(width // tile,),
        in_specs=[spec],
        out_specs=spec,
        out_shape=jax.ShapeDtypeStruct(weight.shape, BF16),
        compiler_params=params("arbitrary"),
        cost_estimate=cost(weight.size, 6 * weight.size),
        name="cast_weight",
    )(weight)


def add_kernel(a_ref, b_ref, out_ref):
    out_ref[...] = (a_ref[...].astype(F32) + b_ref[...].astype(F32)).astype(BF16)


def add_parts(a, b):
    members, rows, width = a.shape
    tile = min(width, 1024)
    spec = pl.BlockSpec((members, rows, tile), lambda j: (0, 0, j))
    return pl.pallas_call(
        add_kernel,
        grid=(width // tile,),
        in_specs=[spec, spec],
        out_specs=spec,
        out_shape=jax.ShapeDtypeStruct(a.shape, BF16),
        compiler_params=params("arbitrary"),
        cost_estimate=cost(a.size, 6 * a.size),
        name="add_parts",
    )(a, b)


def adam_kernel(
    parts, master_ref, mc_ref, ms_ref, vc_ref, vs_ref, *refs
):
    grad_refs = refs[:parts]
    master_out, mc_out, ms_out, vc_out, vs_out = refs[parts:]
    blocks = ms_ref.shape[1]
    rows = ms_ref.shape[2]
    corr_one = 1.0 - beta_one**ADAM_STEP
    corr_two = 1.0 - beta_two**ADAM_STEP
    m_scales = (ms_ref[0] * beta_one).T
    v_scales = (vs_ref[0] * beta_two).T
    lane = lax.broadcasted_iota(jnp.int32, (rows, blocks), 1)
    m_tops = jnp.zeros((rows, blocks), F32)
    v_tops = jnp.zeros((rows, blocks), F32)
    for b in range(blocks):
        cols = slice(b * BLOCK, (b + 1) * BLOCK)
        grad = grad_refs[0][0, :, cols].astype(F32)
        for ref in grad_refs[1:]:
            grad = grad + ref[0, :, cols].astype(F32)
        m_next = mc_ref[0, :, cols].astype(F32) * m_scales[:, b : b + 1] + (1.0 - beta_one) * grad
        v_next = vc_ref[0, :, cols].astype(F32) * v_scales[:, b : b + 1] + (
            1.0 - beta_two
        ) * (grad * grad)
        v_hat = v_next * (1.0 / corr_two)
        root = v_hat * lax.rsqrt(v_hat) + 1e-08
        master_out[0, :, cols] = master_ref[0, :, cols] - (learn_rate / corr_one) * m_next / root
        m_top = jnp.max(jnp.abs(m_next), axis=-1, keepdims=True) + 1e-06
        v_top = jnp.max(v_next, axis=-1, keepdims=True) + 1e-06
        mc_out[0, :, cols] = (m_next * (1.0 / m_top)).astype(BF16)
        vc_out[0, :, cols] = (v_next * (1.0 / v_top)).astype(BF16)
        m_tops = jnp.where(lane == b, m_top, m_tops)
        v_tops = jnp.where(lane == b, v_top, v_tops)
    ms_out[0] = m_tops.T
    vs_out[0] = v_tops.T


def adam(master_weight, grads, m_code, m_scale, v_code, v_scale):
    members, rows, width = master_weight.shape
    blocks = m_scale.shape[-1]
    count = 8 if blocks % 8 == 0 else blocks
    big = pl.BlockSpec((1, rows, count * BLOCK), lambda e, j: (e, 0, j))
    small = pl.BlockSpec((1, count, rows), lambda e, j: (e, j, 0))
    scales = jax.ShapeDtypeStruct((members, blocks, rows), F32)
    master_next, m_code_next, m_scale_next, v_code_next, v_scale_next = pl.pallas_call(
        functools.partial(adam_kernel, len(grads)),
        grid=(members, blocks // count),
        in_specs=[big, big, small, big, small] + [big] * len(grads),
        out_specs=(big, big, small, big, small),
        out_shape=(
            jax.ShapeDtypeStruct(master_weight.shape, F32),
            jax.ShapeDtypeStruct(master_weight.shape, BF16),
            scales,
            jax.ShapeDtypeStruct(master_weight.shape, BF16),
            scales,
        ),
        compiler_params=params("arbitrary", "arbitrary"),
        cost_estimate=cost(40 * master_weight.size, 18 * master_weight.size),
        name="adam",
    )(master_weight, m_code, jnp.swapaxes(m_scale, 1, 2), v_code, jnp.swapaxes(v_scale, 1, 2), *grads)
    return (
        master_next,
        m_code_next,
        jnp.swapaxes(m_scale_next, 1, 2),
        v_code_next,
        jnp.swapaxes(v_scale_next, 1, 2),
    )


def swap(array, axis, offset):
    size = lax.axis_size(axis)
    return lax.ppermute(array, axis, [(i, i ^ offset) for i in range(size)])


def exchange(buffer, groups):
    places, width = buffer.shape
    parts = buffer.reshape(groups, places // groups, width)
    moved = lax.all_to_all(parts, "grp", split_axis=0, concat_axis=0, tiled=True)
    return moved.reshape(places, width)


def gather_weight(weight_slice, replicas):
    if replicas != 4:
        return [lax.all_gather(weight_slice, "rep", axis=1, tiled=True)]
    far = swap(weight_slice, "rep", 2)
    near = swap(weight_slice, "rep", 1)
    return [weight_slice, near, far, swap(far, "rep", 1)]


def sum_gradient(parts):
    if len(parts) != 4:
        return [lax.psum_scatter(parts[0], "rep", scatter_dimension=1, tiled=True)]
    far = swap(parts[3], "rep", 1)
    near = swap(parts[1], "rep", 1)
    return [parts[0], near, swap(add_parts(parts[2], far), "rep", 2)]


def per_device(master_weight, m_code, m_scale, v_code, v_scale, placement, route, x_rows, y_cot):
    local_count = master_weight.shape[0]
    row_count = x_rows.shape[0]
    expert_count = placement.shape[0]
    groups = lax.axis_size("grp")
    replicas = lax.axis_size("rep")
    grad_factor = float(row_count * groups * replicas // expert_count) ** (-0.5)
    capacity = max(2, (3 * row_count + 2 * expert_count - 1) // (2 * expert_count))
    places = expert_count * capacity
    sent, target = dispatch(route, placement, x_rows, y_cot, capacity)
    local = exchange(sent, groups)
    early_master, target = lax.optimization_barrier((master_weight, target))
    weight = gather_weight(cast_weight(early_master), replicas)
    results = products(local, weight, capacity)
    local, results = lax.optimization_barrier((local, results))
    home = exchange(results, groups)

    parts = replicas if replicas == 4 else 1
    hidden = x_rows.shape[1]
    grads = sum_gradient(gradient(local, hidden, capacity, local_count, parts, grad_factor))
    updated = adam(master_weight, grads, m_code, m_scale, v_code, v_scale)
    y_rows, x_grad = collect(home_places(target, places), home, hidden)
    return (y_rows, x_grad) + tuple(updated)


def solution(mesh):
    return jax.shard_map(
        per_device,
        mesh=mesh,
        in_specs=(
            P("grp", "rep", None),
            P("grp", "rep", None),
            P("grp", "rep", None),
            P("grp", "rep", None),
            P("grp", "rep", None),
            P(),
            P(("rep", "grp")),
            P(("rep", "grp"), None),
            P(("rep", "grp"), None),
        ),
        out_specs=(
            P(("rep", "grp"), None),
            P(("rep", "grp"), None),
            P("grp", "rep", None),
            P("grp", "rep", None),
            P("grp", "rep", None),
            P("grp", "rep", None),
            P("grp", "rep", None),
        ),
        check_vma=False,
    )
```

```python
import functools

import jax
import jax.numpy as jnp
from jax import lax
from jax.experimental import pallas as pl
from jax.experimental.pallas import tpu as pltpu
from jax.sharding import PartitionSpec as P

BLOCK = 128
ADAM_STEP = 100

beta_one = 0.9
beta_two = 0.95
learn_rate = 0.01

VMEM_LIMIT = 40 * 1024 * 1024
LARGE_LIMIT = 56 * 1024 * 1024
F32 = jnp.float32
BF16 = jnp.bfloat16


def cost(flops, nbytes):
    return pl.CostEstimate(flops=int(flops), bytes_accessed=int(nbytes), transcendentals=0)


def params(*semantics):
    if semantics:
        return pltpu.CompilerParams(vmem_limit_bytes=VMEM_LIMIT, dimension_semantics=semantics)
    return pltpu.CompilerParams(vmem_limit_bytes=VMEM_LIMIT)


def row_targets(route_row, placement_row, capacity):
    expert_count = placement_row.shape[1]
    row_count = route_row.shape[1]
    diagonal = lax.broadcasted_iota(jnp.int32, (expert_count, expert_count), 0) == (
        lax.broadcasted_iota(jnp.int32, (expert_count, expert_count), 1)
    )
    placement_col = jnp.sum(
        jnp.where(diagonal, placement_row, 0).astype(F32), axis=1, keepdims=True
    )
    hot = (placement_col == route_row.astype(F32)).astype(F32)
    earlier = lax.broadcasted_iota(jnp.int32, (row_count, row_count), 0)
    later = lax.broadcasted_iota(jnp.int32, (row_count, row_count), 1)
    before = (earlier < later).astype(F32).astype(BF16)
    position = jnp.dot(hot.astype(BF16), before, preferred_element_type=F32)
    slot = lax.broadcasted_iota(jnp.int32, (expert_count, row_count), 0)
    start = (slot * capacity).astype(F32)
    return jnp.sum(hot * (start + position), axis=0, keepdims=True).astype(jnp.int32)


def place_matrix(target, places):
    slots = lax.broadcasted_iota(jnp.int32, (places, target.shape[1]), 0)
    return (slots == target).astype(F32).astype(BF16)


def dispatch_kernel(
    capacity, route_hbm, placement_hbm, g_hbm, sent_hbm, target_hbm,
    route_ref, placement_ref, target_ref, g_ref, sent_ref, key_sems, in_sems, out_sems,
):
    tiles, _, tile = g_ref.shape
    keys = [
        pltpu.make_async_copy(route_hbm, route_ref, key_sems.at[0]),
        pltpu.make_async_copy(placement_hbm, placement_ref, key_sems.at[1]),
    ]
    loads = [
        pltpu.make_async_copy(
            g_hbm.at[:, pl.ds(j * tile, tile)], g_ref.at[j], in_sems.at[j]
        )
        for j in range(tiles)
    ]
    for load in keys + loads:
        load.start()
    for load in keys:
        load.wait()
    target = row_targets(route_ref[...], placement_ref[...], capacity)
    target_ref[...] = target
    stores = [pltpu.make_async_copy(target_ref, target_hbm, key_sems.at[2])]
    stores[0].start()
    places = place_matrix(target, sent_ref.shape[0])
    for j in range(tiles):
        loads[j].wait()
        span = pl.ds(j * tile, tile)
        sent_ref[:, span] = jnp.dot(places, g_ref[j], preferred_element_type=F32).astype(BF16)
        store = pltpu.make_async_copy(sent_ref.at[:, span], sent_hbm.at[:, span], out_sems.at[j])
        store.start()
        stores.append(store)
    for store in stores:
        store.wait()


def dispatch(route, placement, y_cot, capacity):
    row_count, width = y_cot.shape
    expert_count = placement.shape[0]
    tile = min(width, 512)
    tiles = width // tile
    places = expert_count * capacity
    hbm = pl.BlockSpec(memory_space=pl.ANY)
    return pl.pallas_call(
        functools.partial(dispatch_kernel, capacity),
        in_specs=[hbm, hbm, hbm],
        out_specs=(hbm, hbm),
        out_shape=(
            jax.ShapeDtypeStruct((places, width), BF16),
            jax.ShapeDtypeStruct((1, row_count), jnp.int32),
        ),
        scratch_shapes=[
            pltpu.VMEM((1, row_count), jnp.int32),
            pltpu.VMEM((1, expert_count), jnp.int32),
            pltpu.VMEM((1, row_count), jnp.int32),
            pltpu.VMEM((tiles, row_count, tile), BF16),
            pltpu.VMEM((places, width), BF16),
            pltpu.SemaphoreType.DMA((3,)),
            pltpu.SemaphoreType.DMA((tiles,)),
            pltpu.SemaphoreType.DMA((tiles,)),
        ],
        compiler_params=pltpu.CompilerParams(vmem_limit_bytes=LARGE_LIMIT),
        cost_estimate=cost(2 * places * row_count * width, 2 * (places + row_count) * width),
        name="dispatch",
    )(route.reshape(1, row_count), placement.reshape(1, -1), y_cot)


def chunk_owner(k):
    return jnp.bitwise_xor(lax.axis_index("grp"), k)


def split_chunks(refs, rows, held_ref):
    if len(refs) == 1:
        refs[0][...] = rows
        return
    held_ref[...] = rows.reshape(held_ref.shape)
    for k, ref in enumerate(refs):
        ref[...] = held_ref[chunk_owner(k)]


def join_chunks(refs, held_ref):
    if len(refs) == 1:
        return refs[0][...]
    for k, ref in enumerate(refs):
        held_ref[chunk_owner(k)] = ref[...]
    return held_ref[...].reshape(len(refs) * refs[0].shape[0], refs[0].shape[1])


def held_scratch(chunks, rows, hidden):
    return pltpu.VMEM((chunks, rows, hidden), BF16)


def dispatch_x_kernel(chunks, target_ref, x_ref, *refs):
    places = place_matrix(target_ref[...], chunks * refs[0].shape[0])
    rows = jnp.dot(places, x_ref[...], preferred_element_type=F32).astype(BF16)
    split_chunks(refs[:chunks], rows, refs[-1])


def dispatch_x(target, x_rows, places, chunks):
    row_count, hidden = x_rows.shape
    rows = places // chunks
    return list(pl.pallas_call(
        functools.partial(dispatch_x_kernel, chunks),
        out_shape=(jax.ShapeDtypeStruct((rows, hidden), BF16),) * chunks,
        scratch_shapes=[held_scratch(chunks, rows, hidden)],
        compiler_params=params(),
        cost_estimate=cost(2 * places * row_count * hidden, 2 * (places + row_count) * hidden),
        name="dispatch_x",
    )(target, x_rows))


def home_places_kernel(target_ref, out_ref):
    target = target_ref[...]
    slots = lax.broadcasted_iota(jnp.int32, (out_ref.shape[1], target.shape[1]), 0)
    out_ref[...] = (slots == target).astype(F32).T.astype(BF16)


def home_places(target, places):
    return pl.pallas_call(
        home_places_kernel,
        out_shape=jax.ShapeDtypeStruct((target.shape[1], places), BF16),
        compiler_params=params(),
        cost_estimate=cost(places * target.shape[1], 2 * places * target.shape[1]),
        name="home_places",
    )(target)


def collect_kernel(chunks, places_ref, home_hbm, *refs):
    dx_refs, y_hbm, x_grad_hbm = refs[:chunks], refs[chunks], refs[chunks + 1]
    home_ref, held_ref, y_ref, x_grad_ref, in_sems, out_sems = refs[chunks + 2 :]
    tiles = in_sems.shape[0]
    tile = y_ref.shape[1] // tiles
    spans = [pl.ds(j * tile, tile) for j in range(tiles)]
    loads = [
        pltpu.make_async_copy(home_hbm.at[:, span], home_ref.at[:, span], in_sems.at[j])
        for j, span in enumerate(spans)
    ]
    for load in loads:
        load.start()
    places = places_ref[...]
    x_grad_ref[...] = jnp.dot(
        places, join_chunks(dx_refs, held_ref), preferred_element_type=F32
    ).astype(BF16)
    stores = [pltpu.make_async_copy(x_grad_ref, x_grad_hbm, out_sems.at[tiles])]
    stores[0].start()
    for j, span in enumerate(spans):
        loads[j].wait()
        y_ref[:, span] = jnp.dot(
            places, home_ref[:, span], preferred_element_type=F32
        ).astype(BF16)
        store = pltpu.make_async_copy(y_ref.at[:, span], y_hbm.at[:, span], out_sems.at[j])
        store.start()
        stores.append(store)
    for store in stores:
        store.wait()


def collect(places, home_y, home_dx):
    total, width = home_y.shape
    rows, hidden = home_dx[0].shape
    chunks = len(home_dx)
    row_count = places.shape[0]
    tiles = width // min(width, 512)
    whole = pl.BlockSpec(memory_space=pltpu.VMEM)
    hbm = pl.BlockSpec(memory_space=pl.ANY)
    return pl.pallas_call(
        functools.partial(collect_kernel, chunks),
        in_specs=[whole, hbm] + [whole] * chunks,
        out_specs=(hbm, hbm),
        out_shape=(
            jax.ShapeDtypeStruct((row_count, width), BF16),
            jax.ShapeDtypeStruct((row_count, hidden), BF16),
        ),
        scratch_shapes=[
            pltpu.VMEM((total, width), BF16),
            held_scratch(chunks, rows, hidden),
            pltpu.VMEM((row_count, width), BF16),
            pltpu.VMEM((row_count, hidden), BF16),
            pltpu.SemaphoreType.DMA((tiles,)),
            pltpu.SemaphoreType.DMA((tiles + 1,)),
        ],
        compiler_params=params(),
        cost_estimate=cost(
            2 * total * row_count * (hidden + width), 2 * (total + row_count) * (hidden + width)
        ),
        name="collect",
    )(places, home_y, *home_dx)


def member_rows(rows, capacity, local_count):
    index = lax.broadcasted_iota(jnp.int32, (rows, 1), 0)
    return lax.rem(index, capacity * local_count) // capacity


def spread(x, capacity, local_count):
    member = member_rows(x.shape[0], capacity, local_count)
    zero = jnp.zeros_like(x)
    return jnp.concatenate([jnp.where(member == e, x, zero) for e in range(local_count)], axis=1)


def join_weight(piece_refs, joined_ref):
    local_count, rows, width = piece_refs[0].shape
    if len(piece_refs) == 1:
        return piece_refs[0][...].reshape(local_count * rows, width)
    here = lax.axis_index("rep")
    for i, ref in enumerate(piece_refs):
        owner = jnp.bitwise_xor(here, i)
        for e in range(local_count):
            joined_ref[e, owner] = ref[e]
    return joined_ref[...].reshape(local_count * len(piece_refs) * rows, width)


def joined_scratch(pieces, tile):
    local_count, rows, _ = pieces[0].shape
    return pltpu.VMEM((local_count, len(pieces), rows, tile), BF16)


def forward_kernel(capacity, local_count, chunks, pieces, *refs):
    x_refs, w_refs = refs[:chunks], refs[chunks : chunks + pieces]
    y_ref, wide_ref, held_ref, joined_ref = refs[chunks + pieces :]

    @pl.when(pl.program_id(0) == 0)
    def _():
        wide_ref[...] = spread(join_chunks(x_refs, held_ref), capacity, local_count)

    y_ref[...] = jnp.dot(
        wide_ref[...], join_weight(w_refs, joined_ref), preferred_element_type=F32
    ).astype(BF16)


def forward(x, weight, capacity):
    rows, hidden = x[0].shape
    local_count, slice_rows, width = weight[0].shape
    tile = min(width, 512)
    total = rows * len(x)
    wide = local_count * hidden
    return pl.pallas_call(
        functools.partial(forward_kernel, capacity, local_count, len(x), len(weight)),
        grid=(width // tile,),
        in_specs=[pl.BlockSpec((rows, hidden), lambda j: (0, 0))] * len(x)
        + [pl.BlockSpec((local_count, slice_rows, tile), lambda j: (0, 0, j))] * len(weight),
        out_specs=(
            pl.BlockSpec((total, tile), lambda j: (0, j)),
            pl.BlockSpec((total, wide), lambda j: (0, 0)),
        ),
        out_shape=(
            jax.ShapeDtypeStruct((total, width), BF16),
            jax.ShapeDtypeStruct((total, wide), BF16),
        ),
        scratch_shapes=[held_scratch(len(x), rows, hidden), joined_scratch(weight, tile)],
        compiler_params=params("arbitrary"),
        cost_estimate=cost(2 * total * wide * width, 2 * (wide + total) * width),
        name="forward",
    )(*x, *weight)


def backward_kernel(capacity, local_count, chunks, pieces, g_ref, *refs):
    w_refs, dx_refs = refs[:pieces], refs[pieces : pieces + chunks]
    held_ref, joined_ref, total_ref = refs[pieces + chunks :]
    step = pl.program_id(0)
    hidden = dx_refs[0].shape[1]
    part = lax.dot_general(
        g_ref[...], join_weight(w_refs, joined_ref), (((1,), (1,)), ((), ())),
        preferred_element_type=F32,
    )

    @pl.when(step == 0)
    def _():
        total_ref[...] = part

    @pl.when(step > 0)
    def _():
        total_ref[...] += part

    @pl.when(step == pl.num_programs(0) - 1)
    def _():
        member = member_rows(total_ref.shape[0], capacity, local_count)
        picked = total_ref[:, :hidden]
        for e in range(1, local_count):
            picked = jnp.where(member == e, total_ref[:, e * hidden : (e + 1) * hidden], picked)
        split_chunks(dx_refs, picked.astype(BF16), held_ref)


def backward(g, weight, capacity, chunks):
    total, width = g.shape
    local_count, slice_rows, _ = weight[0].shape
    hidden = slice_rows * len(weight)
    rows = total // chunks
    tile = min(width, 512)
    return list(pl.pallas_call(
        functools.partial(backward_kernel, capacity, local_count, chunks, len(weight)),
        grid=(width // tile,),
        in_specs=[pl.BlockSpec((total, tile), lambda j: (0, j))]
        + [pl.BlockSpec((local_count, slice_rows, tile), lambda j: (0, 0, j))] * len(weight),
        out_specs=(pl.BlockSpec((rows, hidden), lambda j: (0, 0)),) * chunks,
        out_shape=(jax.ShapeDtypeStruct((rows, hidden), BF16),) * chunks,
        scratch_shapes=[
            held_scratch(chunks, rows, hidden),
            joined_scratch(weight, tile),
            pltpu.VMEM((total, local_count * hidden), F32),
        ],
        compiler_params=params("arbitrary"),
        cost_estimate=cost(
            2 * total * local_count * hidden * width,
            2 * (local_count * hidden + total) * width,
        ),
        name="backward",
    )(g, *weight))


def gradient_kernel(parts, factor, wide_ref, g_ref, *refs):
    outer = lax.dot_general(
        wide_ref[...], g_ref[...], (((0,), (0,)), ((), ())), preferred_element_type=F32
    )
    low = (outer * factor).astype(BF16)
    if parts == 1:
        refs[0][...] = low.reshape(refs[0].shape)
        return
    out_refs, split_ref = refs[:-1], refs[-1]
    split_ref[...] = low.reshape(split_ref.shape)
    here = lax.axis_index("rep")
    for i, out_ref in enumerate(out_refs):
        owner = jnp.bitwise_xor(here, i)
        for e in range(split_ref.shape[0]):
            out_ref[e] = split_ref[e, owner]


def gradient(wide, g, local_count, parts, factor):
    total, width = g.shape
    tile = min(width, 512)
    columns = wide.shape[1]
    slice_rows = columns // local_count // parts
    split = [pltpu.VMEM((local_count, parts, slice_rows, tile), BF16)] if parts > 1 else []
    return list(pl.pallas_call(
        functools.partial(gradient_kernel, parts, factor),
        grid=(width // tile,),
        in_specs=[
            pl.BlockSpec((total, columns), lambda j: (0, 0)),
            pl.BlockSpec((total, tile), lambda j: (0, j)),
        ],
        out_specs=(pl.BlockSpec((local_count, slice_rows, tile), lambda j: (0, 0, j)),) * parts,
        out_shape=(jax.ShapeDtypeStruct((local_count, slice_rows, width), BF16),) * parts,
        scratch_shapes=split,
        compiler_params=params("arbitrary"),
        cost_estimate=cost(2 * total * columns * width, 2 * (columns + total) * width),
        name="gradient",
    )(wide, g))


def cast_kernel(w_ref, out_ref):
    out_ref[...] = w_ref[...].astype(BF16)


def cast_weight(weight):
    members, rows, width = weight.shape
    tile = min(width, 512)
    spec = pl.BlockSpec((members, rows, tile), lambda j: (0, 0, j))
    return pl.pallas_call(
        cast_kernel,
        grid=(width // tile,),
        in_specs=[spec],
        out_specs=spec,
        out_shape=jax.ShapeDtypeStruct(weight.shape, BF16),
        compiler_params=params("arbitrary"),
        cost_estimate=cost(weight.size, 6 * weight.size),
        name="cast_weight",
    )(weight)


def add_kernel(a_ref, b_ref, out_ref):
    out_ref[...] = (a_ref[...].astype(F32) + b_ref[...].astype(F32)).astype(BF16)


def add_parts(a, b):
    members, rows, width = a.shape
    tile = min(width, 1024)
    spec = pl.BlockSpec((members, rows, tile), lambda j: (0, 0, j))
    return pl.pallas_call(
        add_kernel,
        grid=(width // tile,),
        in_specs=[spec, spec],
        out_specs=spec,
        out_shape=jax.ShapeDtypeStruct(a.shape, BF16),
        compiler_params=params("arbitrary"),
        cost_estimate=cost(a.size, 6 * a.size),
        name="add_parts",
    )(a, b)


def adam_kernel(
    parts, master_ref, mc_ref, ms_ref, vc_ref, vs_ref, *refs
):
    grad_refs = refs[:parts]
    master_out, mc_out, ms_out, vc_out, vs_out = refs[parts:]
    blocks = ms_ref.shape[1]
    rows = ms_ref.shape[2]
    corr_one = 1.0 - beta_one**ADAM_STEP
    corr_two = 1.0 - beta_two**ADAM_STEP
    m_scales = (ms_ref[0] * beta_one).T
    v_scales = (vs_ref[0] * beta_two).T
    lane = lax.broadcasted_iota(jnp.int32, (rows, blocks), 1)
    m_tops = jnp.zeros((rows, blocks), F32)
    v_tops = jnp.zeros((rows, blocks), F32)
    for b in range(blocks):
        cols = slice(b * BLOCK, (b + 1) * BLOCK)
        grad = grad_refs[0][0, :, cols].astype(F32)
        for ref in grad_refs[1:]:
            grad = grad + ref[0, :, cols].astype(F32)
        m_next = mc_ref[0, :, cols].astype(F32) * m_scales[:, b : b + 1] + (1.0 - beta_one) * grad
        v_next = vc_ref[0, :, cols].astype(F32) * v_scales[:, b : b + 1] + (
            1.0 - beta_two
        ) * (grad * grad)
        v_hat = v_next * (1.0 / corr_two)
        root = v_hat * lax.rsqrt(v_hat) + 1e-08
        master_out[0, :, cols] = master_ref[0, :, cols] - (learn_rate / corr_one) * m_next / root
        m_top = jnp.max(jnp.abs(m_next), axis=-1, keepdims=True) + 1e-06
        v_top = jnp.max(v_next, axis=-1, keepdims=True) + 1e-06
        mc_out[0, :, cols] = (m_next * (1.0 / m_top)).astype(BF16)
        vc_out[0, :, cols] = (v_next * (1.0 / v_top)).astype(BF16)
        m_tops = jnp.where(lane == b, m_top, m_tops)
        v_tops = jnp.where(lane == b, v_top, v_tops)
    ms_out[0] = m_tops.T
    vs_out[0] = v_tops.T


def adam(master_weight, grads, m_code, m_scale, v_code, v_scale):
    members, rows, width = master_weight.shape
    blocks = m_scale.shape[-1]
    count = 8 if blocks % 8 == 0 else blocks
    big = pl.BlockSpec((1, rows, count * BLOCK), lambda e, j: (e, 0, j))
    small = pl.BlockSpec((1, count, rows), lambda e, j: (e, j, 0))
    scales = jax.ShapeDtypeStruct((members, blocks, rows), F32)
    master_next, m_code_next, m_scale_next, v_code_next, v_scale_next = pl.pallas_call(
        functools.partial(adam_kernel, len(grads)),
        grid=(members, blocks // count),
        in_specs=[big, big, small, big, small] + [big] * len(grads),
        out_specs=(big, big, small, big, small),
        out_shape=(
            jax.ShapeDtypeStruct(master_weight.shape, F32),
            jax.ShapeDtypeStruct(master_weight.shape, BF16),
            scales,
            jax.ShapeDtypeStruct(master_weight.shape, BF16),
            scales,
        ),
        compiler_params=params("arbitrary", "arbitrary"),
        cost_estimate=cost(40 * master_weight.size, 18 * master_weight.size),
        name="adam",
    )(master_weight, m_code, jnp.swapaxes(m_scale, 1, 2), v_code, jnp.swapaxes(v_scale, 1, 2), *grads)
    return (
        master_next,
        m_code_next,
        jnp.swapaxes(m_scale_next, 1, 2),
        v_code_next,
        jnp.swapaxes(v_scale_next, 1, 2),
    )


def swap(array, axis, offset):
    size = lax.axis_size(axis)
    return lax.ppermute(array, axis, [(i, i ^ offset) for i in range(size)])


def exchange(buffer, groups):
    places, width = buffer.shape
    parts = buffer.reshape(groups, places // groups, width)
    moved = lax.all_to_all(parts, "grp", split_axis=0, concat_axis=0, tiled=True)
    return moved.reshape(places, width)


def exchange_chunks(chunks, groups):
    if len(chunks) == 1:
        return [exchange(chunks[0], groups)]
    return [chunks[0]] + [swap(chunk, "grp", k) for k, chunk in enumerate(chunks) if k > 0]


def gather_weight(weight_slice, replicas):
    if replicas != 4:
        return [lax.all_gather(weight_slice, "rep", axis=1, tiled=True)]
    far = swap(weight_slice, "rep", 2)
    near = swap(weight_slice, "rep", 1)
    return [weight_slice, near, far, swap(far, "rep", 1)]


def sum_gradient(parts):
    if len(parts) != 4:
        return [lax.psum_scatter(parts[0], "rep", scatter_dimension=1, tiled=True)]
    far = swap(parts[3], "rep", 1)
    near = swap(parts[1], "rep", 1)
    return [parts[0], near, swap(add_parts(parts[2], far), "rep", 2)]


def per_device(master_weight, m_code, m_scale, v_code, v_scale, placement, route, x_rows, y_cot):
    local_count = master_weight.shape[0]
    row_count = x_rows.shape[0]
    expert_count = placement.shape[0]
    groups = lax.axis_size("grp")
    replicas = lax.axis_size("rep")
    grad_factor = float(row_count * groups * replicas // expert_count) ** (-0.5)
    capacity = max(2, (3 * row_count + 2 * expert_count - 1) // (2 * expert_count))
    places = expert_count * capacity
    few = groups <= 8 and groups & (groups - 1) == 0 and places // groups % 16 == 0
    chunks = groups if few else 1
    parts = replicas if replicas == 4 else 1

    sent_g, target = dispatch(route, placement, y_cot, capacity)
    local_g = exchange(sent_g, groups)

    early_master, early_x, target = lax.optimization_barrier((master_weight, x_rows, target))
    weight = gather_weight(cast_weight(early_master), replicas)
    local_x = exchange_chunks(dispatch_x(target, early_x, places, chunks), groups)
    back_y, wide = forward(local_x, weight, capacity)
    home_y = exchange(back_y, groups)

    grads = sum_gradient(gradient(wide, local_g, local_count, parts, grad_factor))
    home_dx = exchange_chunks(backward(local_g, weight, capacity, chunks), groups)
    updated = adam(master_weight, grads, m_code, m_scale, v_code, v_scale)
    y_rows, x_grad = collect(home_places(target, places), home_y, home_dx)
    return (y_rows, x_grad) + tuple(updated)


def solution(mesh):
    return jax.shard_map(
        per_device,
        mesh=mesh,
        in_specs=(
            P("grp", "rep", None),
            P("grp", "rep", None),
            P("grp", "rep", None),
            P("grp", "rep", None),
            P("grp", "rep", None),
            P(),
            P(("rep", "grp")),
            P(("rep", "grp"), None),
            P(("rep", "grp"), None),
        ),
        out_specs=(
            P(("rep", "grp"), None),
            P(("rep", "grp"), None),
            P("grp", "rep", None),
            P("grp", "rep", None),
            P("grp", "rep", None),
            P("grp", "rep", None),
            P("grp", "rep", None),
        ),
        check_vma=False,
    )
```

```python
import functools

import jax
import jax.numpy as jnp
from jax import lax
from jax.experimental import pallas as pl
from jax.experimental.pallas import tpu as pltpu
from jax.sharding import PartitionSpec as P

BLOCK = 128
ADAM_STEP = 100

beta_one = 0.9
beta_two = 0.95
learn_rate = 0.01

VMEM_LIMIT = 60 * 1024 * 1024
F32 = jnp.float32
BF16 = jnp.bfloat16


def cost(flops, nbytes):
    return pl.CostEstimate(flops=int(flops), bytes_accessed=int(nbytes), transcendentals=0)


def params(*semantics):
    if semantics:
        return pltpu.CompilerParams(vmem_limit_bytes=VMEM_LIMIT, dimension_semantics=semantics)
    return pltpu.CompilerParams(vmem_limit_bytes=VMEM_LIMIT)


def row_targets(route_row, placement_row, capacity):
    expert_count = placement_row.shape[1]
    row_count = route_row.shape[1]
    diagonal = lax.broadcasted_iota(jnp.int32, (expert_count, expert_count), 0) == (
        lax.broadcasted_iota(jnp.int32, (expert_count, expert_count), 1)
    )
    placement_col = jnp.sum(
        jnp.where(diagonal, placement_row, 0).astype(F32), axis=1, keepdims=True
    )
    hot = (placement_col == route_row.astype(F32)).astype(F32)
    earlier = lax.broadcasted_iota(jnp.int32, (row_count, row_count), 0)
    later = lax.broadcasted_iota(jnp.int32, (row_count, row_count), 1)
    before = (earlier < later).astype(F32).astype(BF16)
    position = jnp.dot(hot.astype(BF16), before, preferred_element_type=F32)
    slot = lax.broadcasted_iota(jnp.int32, (expert_count, row_count), 0)
    start = (slot * capacity).astype(F32)
    return jnp.sum(hot * (start + position), axis=0, keepdims=True).astype(jnp.int32)


def place_matrix(target, places):
    slots = lax.broadcasted_iota(jnp.int32, (places, target.shape[1]), 0)
    return (slots == target).astype(F32).astype(BF16)


def dispatch_kernel(
    capacity, route_hbm, placement_hbm, g_hbm, sent_hbm, target_hbm,
    route_ref, placement_ref, target_ref, g_ref, sent_ref, key_sems, in_sems, out_sems,
):
    tiles, _, tile = g_ref.shape
    keys = [
        pltpu.make_async_copy(route_hbm, route_ref, key_sems.at[0]),
        pltpu.make_async_copy(placement_hbm, placement_ref, key_sems.at[1]),
    ]
    loads = [
        pltpu.make_async_copy(
            g_hbm.at[:, pl.ds(j * tile, tile)], g_ref.at[j], in_sems.at[j]
        )
        for j in range(tiles)
    ]
    for load in keys + loads:
        load.start()
    for load in keys:
        load.wait()
    target = row_targets(route_ref[...], placement_ref[...], capacity)
    target_ref[...] = target
    stores = [pltpu.make_async_copy(target_ref, target_hbm, key_sems.at[2])]
    stores[0].start()
    places = place_matrix(target, sent_ref.shape[0])
    for j in range(tiles):
        loads[j].wait()
        span = pl.ds(j * tile, tile)
        sent_ref[:, span] = jnp.dot(places, g_ref[j], preferred_element_type=F32).astype(BF16)
        store = pltpu.make_async_copy(sent_ref.at[:, span], sent_hbm.at[:, span], out_sems.at[j])
        store.start()
        stores.append(store)
    for store in stores:
        store.wait()


def dispatch(route, placement, y_cot, capacity):
    row_count, width = y_cot.shape
    expert_count = placement.shape[0]
    tile = min(width, 512)
    tiles = width // tile
    places = expert_count * capacity
    hbm = pl.BlockSpec(memory_space=pl.ANY)
    return pl.pallas_call(
        functools.partial(dispatch_kernel, capacity),
        in_specs=[hbm, hbm, hbm],
        out_specs=(hbm, hbm),
        out_shape=(
            jax.ShapeDtypeStruct((places, width), BF16),
            jax.ShapeDtypeStruct((1, row_count), jnp.int32),
        ),
        scratch_shapes=[
            pltpu.VMEM((1, row_count), jnp.int32),
            pltpu.VMEM((1, expert_count), jnp.int32),
            pltpu.VMEM((1, row_count), jnp.int32),
            pltpu.VMEM((tiles, row_count, tile), BF16),
            pltpu.VMEM((places, width), BF16),
            pltpu.SemaphoreType.DMA((3,)),
            pltpu.SemaphoreType.DMA((tiles,)),
            pltpu.SemaphoreType.DMA((tiles,)),
        ],
        compiler_params=pltpu.CompilerParams(vmem_limit_bytes=VMEM_LIMIT),
        cost_estimate=cost(2 * places * row_count * width, 2 * (places + row_count) * width),
        name="dispatch",
    )(route.reshape(1, row_count), placement.reshape(1, -1), y_cot)


def chunk_owner(k):
    return jnp.bitwise_xor(lax.axis_index("grp"), k)


def split_chunks(refs, rows, held_ref):
    if len(refs) == 1:
        refs[0][...] = rows
        return
    held_ref[...] = rows.reshape(held_ref.shape)
    for k, ref in enumerate(refs):
        ref[...] = held_ref[chunk_owner(k)]


def join_chunks(refs, held_ref):
    if len(refs) == 1:
        return refs[0][...]
    for k, ref in enumerate(refs):
        held_ref[chunk_owner(k)] = ref[...]
    return held_ref[...].reshape(len(refs) * refs[0].shape[0], refs[0].shape[1])


def held_scratch(chunks, rows, hidden):
    return pltpu.VMEM((chunks, rows, hidden), BF16)


def dispatch_x_kernel(chunks, target_ref, x_ref, *refs):
    places = place_matrix(target_ref[...], chunks * refs[0].shape[0])
    rows = jnp.dot(places, x_ref[...], preferred_element_type=F32).astype(BF16)
    split_chunks(refs[:chunks], rows, refs[-1])


def dispatch_x(target, x_rows, places, chunks):
    row_count, hidden = x_rows.shape
    rows = places // chunks
    return list(pl.pallas_call(
        functools.partial(dispatch_x_kernel, chunks),
        out_shape=(jax.ShapeDtypeStruct((rows, hidden), BF16),) * chunks,
        scratch_shapes=[held_scratch(chunks, rows, hidden)],
        compiler_params=params(),
        cost_estimate=cost(2 * places * row_count * hidden, 2 * (places + row_count) * hidden),
        name="dispatch_x",
    )(target, x_rows))


def home_places_kernel(target_ref, out_ref):
    target = target_ref[...]
    slots = lax.broadcasted_iota(jnp.int32, (out_ref.shape[1], target.shape[1]), 0)
    out_ref[...] = (slots == target).astype(F32).T.astype(BF16)


def home_places(target, places):
    return pl.pallas_call(
        home_places_kernel,
        out_shape=jax.ShapeDtypeStruct((target.shape[1], places), BF16),
        compiler_params=params(),
        cost_estimate=cost(places * target.shape[1], 2 * places * target.shape[1]),
        name="home_places",
    )(target)


def collect_kernel(chunks, places_ref, home_hbm, *refs):
    dx_refs, y_hbm, x_grad_hbm = refs[:chunks], refs[chunks], refs[chunks + 1]
    home_ref, held_ref, y_ref, x_grad_ref, in_sems, chunk_sems, out_sems = refs[chunks + 2 :]
    tiles = in_sems.shape[0]
    tile = y_ref.shape[1] // tiles
    spans = [pl.ds(j * tile, tile) for j in range(tiles)]
    loads = [
        pltpu.make_async_copy(home_hbm.at[:, span], home_ref.at[:, span], in_sems.at[j])
        for j, span in enumerate(spans)
    ]
    chunk_loads = [
        pltpu.make_async_copy(
            ref, held_ref.at[chunk_owner(k) if chunks > 1 else 0], chunk_sems.at[k]
        )
        for k, ref in enumerate(dx_refs)
    ]
    for load in chunk_loads + loads:
        load.start()
    places = places_ref[...]
    for load in chunk_loads:
        load.wait()
    home_dx = held_ref[...].reshape(places.shape[1], x_grad_ref.shape[1])
    x_grad_ref[...] = jnp.dot(places, home_dx, preferred_element_type=F32).astype(BF16)
    stores = [pltpu.make_async_copy(x_grad_ref, x_grad_hbm, out_sems.at[tiles])]
    stores[0].start()
    for j, span in enumerate(spans):
        loads[j].wait()
        y_ref[:, span] = jnp.dot(
            places, home_ref[:, span], preferred_element_type=F32
        ).astype(BF16)
        store = pltpu.make_async_copy(y_ref.at[:, span], y_hbm.at[:, span], out_sems.at[j])
        store.start()
        stores.append(store)
    for store in stores:
        store.wait()


def collect(places, home_y, home_dx):
    total, width = home_y.shape
    rows, hidden = home_dx[0].shape
    chunks = len(home_dx)
    row_count = places.shape[0]
    tiles = width // min(width, 512)
    whole = pl.BlockSpec(memory_space=pltpu.VMEM)
    hbm = pl.BlockSpec(memory_space=pl.ANY)
    return pl.pallas_call(
        functools.partial(collect_kernel, chunks),
        in_specs=[whole, hbm] + [hbm] * chunks,
        out_specs=(hbm, hbm),
        out_shape=(
            jax.ShapeDtypeStruct((row_count, width), BF16),
            jax.ShapeDtypeStruct((row_count, hidden), BF16),
        ),
        scratch_shapes=[
            pltpu.VMEM((total, width), BF16),
            held_scratch(chunks, rows, hidden),
            pltpu.VMEM((row_count, width), BF16),
            pltpu.VMEM((row_count, hidden), BF16),
            pltpu.SemaphoreType.DMA((tiles,)),
            pltpu.SemaphoreType.DMA((chunks,)),
            pltpu.SemaphoreType.DMA((tiles + 1,)),
        ],
        compiler_params=params(),
        cost_estimate=cost(
            2 * total * row_count * (hidden + width), 2 * (total + row_count) * (hidden + width)
        ),
        name="collect",
    )(places, home_y, *home_dx)


def member_rows(rows, capacity, local_count):
    index = lax.broadcasted_iota(jnp.int32, (rows, 1), 0)
    return lax.rem(index, capacity * local_count) // capacity


def spread(x, capacity, local_count):
    member = member_rows(x.shape[0], capacity, local_count)
    zero = jnp.zeros_like(x)
    return jnp.concatenate([jnp.where(member == e, x, zero) for e in range(local_count)], axis=1)


def join_weight(piece_refs, joined_ref):
    local_count, rows, width = piece_refs[0].shape
    if len(piece_refs) == 1:
        return piece_refs[0][...].reshape(local_count * rows, width)
    here = lax.axis_index("rep")
    for i, ref in enumerate(piece_refs):
        owner = jnp.bitwise_xor(here, i)
        for e in range(local_count):
            joined_ref[e, owner] = ref[e]
    return joined_ref[...].reshape(local_count * len(piece_refs) * rows, width)


def joined_scratch(pieces, tile):
    local_count, rows, _ = pieces[0].shape
    return pltpu.VMEM((local_count, len(pieces), rows, tile), BF16)


def forward_kernel(capacity, local_count, chunks, pieces, *refs):
    x_refs, w_refs = refs[:chunks], refs[chunks : chunks + pieces]
    y_ref, wide_ref, held_ref, joined_ref = refs[chunks + pieces :]

    @pl.when(pl.program_id(0) == 0)
    def _():
        wide_ref[...] = spread(join_chunks(x_refs, held_ref), capacity, local_count)

    y_ref[...] = jnp.dot(
        wide_ref[...], join_weight(w_refs, joined_ref), preferred_element_type=F32
    ).astype(BF16)


def forward(x, weight, capacity):
    rows, hidden = x[0].shape
    local_count, slice_rows, width = weight[0].shape
    tile = min(width, 512)
    total = rows * len(x)
    wide = local_count * hidden
    return pl.pallas_call(
        functools.partial(forward_kernel, capacity, local_count, len(x), len(weight)),
        grid=(width // tile,),
        in_specs=[pl.BlockSpec((rows, hidden), lambda j: (0, 0))] * len(x)
        + [pl.BlockSpec((local_count, slice_rows, tile), lambda j: (0, 0, j))] * len(weight),
        out_specs=(
            pl.BlockSpec((total, tile), lambda j: (0, j)),
            pl.BlockSpec((total, wide), lambda j: (0, 0)),
        ),
        out_shape=(
            jax.ShapeDtypeStruct((total, width), BF16),
            jax.ShapeDtypeStruct((total, wide), BF16),
        ),
        scratch_shapes=[held_scratch(len(x), rows, hidden), joined_scratch(weight, tile)],
        compiler_params=params("arbitrary"),
        cost_estimate=cost(2 * total * wide * width, 2 * (wide + total) * width),
        name="forward",
    )(*x, *weight)


def backward_kernel(capacity, local_count, chunks, pieces, g_ref, *refs):
    w_refs, dx_refs = refs[:pieces], refs[pieces : pieces + chunks]
    held_ref, joined_ref, total_ref = refs[pieces + chunks :]
    step = pl.program_id(0)
    hidden = dx_refs[0].shape[1]
    part = lax.dot_general(
        g_ref[...], join_weight(w_refs, joined_ref), (((1,), (1,)), ((), ())),
        preferred_element_type=F32,
    )

    @pl.when(step == 0)
    def _():
        total_ref[...] = part

    @pl.when(step > 0)
    def _():
        total_ref[...] += part

    @pl.when(step == pl.num_programs(0) - 1)
    def _():
        member = member_rows(total_ref.shape[0], capacity, local_count)
        picked = total_ref[:, :hidden]
        for e in range(1, local_count):
            picked = jnp.where(member == e, total_ref[:, e * hidden : (e + 1) * hidden], picked)
        split_chunks(dx_refs, picked.astype(BF16), held_ref)


def backward(g, weight, capacity, chunks):
    total, width = g.shape
    local_count, slice_rows, _ = weight[0].shape
    hidden = slice_rows * len(weight)
    rows = total // chunks
    tile = min(width, 512)
    return list(pl.pallas_call(
        functools.partial(backward_kernel, capacity, local_count, chunks, len(weight)),
        grid=(width // tile,),
        in_specs=[pl.BlockSpec((total, tile), lambda j: (0, j))]
        + [pl.BlockSpec((local_count, slice_rows, tile), lambda j: (0, 0, j))] * len(weight),
        out_specs=(pl.BlockSpec((rows, hidden), lambda j: (0, 0)),) * chunks,
        out_shape=(jax.ShapeDtypeStruct((rows, hidden), BF16),) * chunks,
        scratch_shapes=[
            held_scratch(chunks, rows, hidden),
            joined_scratch(weight, tile),
            pltpu.VMEM((total, local_count * hidden), F32),
        ],
        compiler_params=params("arbitrary"),
        cost_estimate=cost(
            2 * total * local_count * hidden * width,
            2 * (local_count * hidden + total) * width,
        ),
        name="backward",
    )(g, *weight))


def gradient_kernel(parts, factor, wide_ref, g_ref, *refs):
    outer = lax.dot_general(
        wide_ref[...], g_ref[...], (((0,), (0,)), ((), ())), preferred_element_type=F32
    )
    low = (outer * factor).astype(BF16)
    if parts == 1:
        refs[0][...] = low.reshape(refs[0].shape)
        return
    out_refs, split_ref = refs[:-1], refs[-1]
    split_ref[...] = low.reshape(split_ref.shape)
    here = lax.axis_index("rep")
    for i, out_ref in enumerate(out_refs):
        owner = jnp.bitwise_xor(here, i)
        for e in range(split_ref.shape[0]):
            out_ref[e] = split_ref[e, owner]


def gradient(wide, g, local_count, parts, factor):
    total, width = g.shape
    tile = min(width, 512)
    columns = wide.shape[1]
    slice_rows = columns // local_count // parts
    split = [pltpu.VMEM((local_count, parts, slice_rows, tile), BF16)] if parts > 1 else []
    return list(pl.pallas_call(
        functools.partial(gradient_kernel, parts, factor),
        grid=(width // tile,),
        in_specs=[
            pl.BlockSpec((total, columns), lambda j: (0, 0)),
            pl.BlockSpec((total, tile), lambda j: (0, j)),
        ],
        out_specs=(pl.BlockSpec((local_count, slice_rows, tile), lambda j: (0, 0, j)),) * parts,
        out_shape=(jax.ShapeDtypeStruct((local_count, slice_rows, width), BF16),) * parts,
        scratch_shapes=split,
        compiler_params=params("arbitrary"),
        cost_estimate=cost(2 * total * columns * width, 2 * (columns + total) * width),
        name="gradient",
    )(wide, g))


def cast_kernel(w_ref, out_ref):
    out_ref[...] = w_ref[...].astype(BF16)


def cast_weight(weight):
    members, rows, width = weight.shape
    tile = min(width, 512)
    spec = pl.BlockSpec((members, rows, tile), lambda j: (0, 0, j))
    return pl.pallas_call(
        cast_kernel,
        grid=(width // tile,),
        in_specs=[spec],
        out_specs=spec,
        out_shape=jax.ShapeDtypeStruct(weight.shape, BF16),
        compiler_params=params("arbitrary"),
        cost_estimate=cost(weight.size, 6 * weight.size),
        name="cast_weight",
    )(weight)


def add_kernel(a_ref, b_ref, out_ref):
    out_ref[...] = (a_ref[...].astype(F32) + b_ref[...].astype(F32)).astype(BF16)


def add_parts(a, b):
    members, rows, width = a.shape
    tile = min(width, 1024)
    spec = pl.BlockSpec((members, rows, tile), lambda j: (0, 0, j))
    return pl.pallas_call(
        add_kernel,
        grid=(width // tile,),
        in_specs=[spec, spec],
        out_specs=spec,
        out_shape=jax.ShapeDtypeStruct(a.shape, BF16),
        compiler_params=params("arbitrary"),
        cost_estimate=cost(a.size, 6 * a.size),
        name="add_parts",
    )(a, b)


def adam_kernel(
    parts, master_ref, mc_ref, ms_ref, vc_ref, vs_ref, *refs
):
    grad_refs = refs[:parts]
    master_out, mc_out, ms_out, vc_out, vs_out = refs[parts:]
    blocks = ms_ref.shape[1]
    rows = ms_ref.shape[2]
    corr_one = 1.0 - beta_one**ADAM_STEP
    corr_two = 1.0 - beta_two**ADAM_STEP
    m_scales = (ms_ref[0] * beta_one).T
    v_scales = (vs_ref[0] * beta_two).T
    lane = lax.broadcasted_iota(jnp.int32, (rows, blocks), 1)
    m_tops = jnp.zeros((rows, blocks), F32)
    v_tops = jnp.zeros((rows, blocks), F32)
    for b in range(blocks):
        cols = slice(b * BLOCK, (b + 1) * BLOCK)
        grad = grad_refs[0][0, :, cols].astype(F32)
        for ref in grad_refs[1:]:
            grad = grad + ref[0, :, cols].astype(F32)
        m_next = mc_ref[0, :, cols].astype(F32) * m_scales[:, b : b + 1] + (1.0 - beta_one) * grad
        v_next = vc_ref[0, :, cols].astype(F32) * v_scales[:, b : b + 1] + (
            1.0 - beta_two
        ) * (grad * grad)
        v_hat = v_next * (1.0 / corr_two)
        root = v_hat * lax.rsqrt(v_hat) + 1e-08
        master_out[0, :, cols] = master_ref[0, :, cols] - (learn_rate / corr_one) * m_next / root
        m_top = jnp.max(jnp.abs(m_next), axis=-1, keepdims=True) + 1e-06
        v_top = jnp.max(v_next, axis=-1, keepdims=True) + 1e-06
        mc_out[0, :, cols] = (m_next * (1.0 / m_top)).astype(BF16)
        vc_out[0, :, cols] = (v_next * (1.0 / v_top)).astype(BF16)
        m_tops = jnp.where(lane == b, m_top, m_tops)
        v_tops = jnp.where(lane == b, v_top, v_tops)
    ms_out[0] = m_tops.T
    vs_out[0] = v_tops.T


def adam(master_weight, grads, m_code, m_scale, v_code, v_scale):
    members, rows, width = master_weight.shape
    blocks = m_scale.shape[-1]
    count = 8 if blocks % 8 == 0 else blocks
    big = pl.BlockSpec((1, rows, count * BLOCK), lambda e, j: (e, 0, j))
    small = pl.BlockSpec((1, count, rows), lambda e, j: (e, j, 0))
    scales = jax.ShapeDtypeStruct((members, blocks, rows), F32)
    master_next, m_code_next, m_scale_next, v_code_next, v_scale_next = pl.pallas_call(
        functools.partial(adam_kernel, len(grads)),
        grid=(members, blocks // count),
        in_specs=[big, big, small, big, small] + [big] * len(grads),
        out_specs=(big, big, small, big, small),
        out_shape=(
            jax.ShapeDtypeStruct(master_weight.shape, F32),
            jax.ShapeDtypeStruct(master_weight.shape, BF16),
            scales,
            jax.ShapeDtypeStruct(master_weight.shape, BF16),
            scales,
        ),
        compiler_params=params("arbitrary", "arbitrary"),
        cost_estimate=cost(40 * master_weight.size, 18 * master_weight.size),
        name="adam",
    )(master_weight, m_code, jnp.swapaxes(m_scale, 1, 2), v_code, jnp.swapaxes(v_scale, 1, 2), *grads)
    return (
        master_next,
        m_code_next,
        jnp.swapaxes(m_scale_next, 1, 2),
        v_code_next,
        jnp.swapaxes(v_scale_next, 1, 2),
    )


def swap(array, axis, offset):
    size = lax.axis_size(axis)
    return lax.ppermute(array, axis, [(i, i ^ offset) for i in range(size)])


def exchange(buffer, groups):
    places, width = buffer.shape
    parts = buffer.reshape(groups, places // groups, width)
    moved = lax.all_to_all(parts, "grp", split_axis=0, concat_axis=0, tiled=True)
    return moved.reshape(places, width)


def exchange_chunks(chunks, groups):
    if len(chunks) == 1:
        return [exchange(chunks[0], groups)]
    return [chunks[0]] + [swap(chunk, "grp", k) for k, chunk in enumerate(chunks) if k > 0]


def gather_weight(weight_slice, replicas, send_between):
    if replicas != 4:
        between = send_between()
        return [lax.all_gather(weight_slice, "rep", axis=1, tiled=True)], between
    near = swap(weight_slice, "rep", 1)
    far = swap(weight_slice, "rep", 2)
    between = send_between()
    far, between = lax.optimization_barrier((far, between))
    return [weight_slice, near, far, swap(far, "rep", 1)], between


def sum_gradient(parts):
    if len(parts) != 4:
        return [lax.psum_scatter(parts[0], "rep", scatter_dimension=1, tiled=True)]
    far = swap(parts[3], "rep", 1)
    near = swap(parts[1], "rep", 1)
    return [parts[0], near, swap(add_parts(parts[2], far), "rep", 2)]


def per_device(master_weight, m_code, m_scale, v_code, v_scale, placement, route, x_rows, y_cot):
    local_count = master_weight.shape[0]
    row_count = x_rows.shape[0]
    expert_count = placement.shape[0]
    groups = lax.axis_size("grp")
    replicas = lax.axis_size("rep")
    grad_factor = float(row_count * groups * replicas // expert_count) ** (-0.5)
    capacity = max(2, (3 * row_count + 2 * expert_count - 1) // (2 * expert_count))
    places = expert_count * capacity
    few = groups <= 8 and groups & (groups - 1) == 0 and places // groups % 16 == 0
    chunks = groups if few else 1
    parts = replicas if replicas == 4 else 1

    sent_g, target = dispatch(route, placement, y_cot, capacity)
    local_g = exchange(sent_g, groups)

    early_master, early_x, target = lax.optimization_barrier((master_weight, x_rows, target))

    def send_x():
        return exchange_chunks(dispatch_x(target, early_x, places, chunks), groups)

    weight, local_x = gather_weight(cast_weight(early_master), replicas, send_x)
    back_y, wide = forward(local_x, weight, capacity)
    home_y = exchange(back_y, groups)

    grads = sum_gradient(gradient(wide, local_g, local_count, parts, grad_factor))
    home_dx = exchange_chunks(backward(local_g, weight, capacity, chunks), groups)
    updated = adam(master_weight, grads, m_code, m_scale, v_code, v_scale)
    y_rows, x_grad = collect(home_places(target, places), home_y, home_dx)
    return (y_rows, x_grad) + tuple(updated)


def solution(mesh):
    return jax.shard_map(
        per_device,
        mesh=mesh,
        in_specs=(
            P("grp", "rep", None),
            P("grp", "rep", None),
            P("grp", "rep", None),
            P("grp", "rep", None),
            P("grp", "rep", None),
            P(),
            P(("rep", "grp")),
            P(("rep", "grp"), None),
            P(("rep", "grp"), None),
        ),
        out_specs=(
            P(("rep", "grp"), None),
            P(("rep", "grp"), None),
            P("grp", "rep", None),
            P("grp", "rep", None),
            P("grp", "rep", None),
            P("grp", "rep", None),
            P("grp", "rep", None),
        ),
        check_vma=False,
    )
```

```python
import functools

import jax
import jax.numpy as jnp
from jax import lax
from jax.experimental import pallas as pl
from jax.experimental.pallas import tpu as pltpu
from jax.sharding import PartitionSpec as P

BLOCK = 128
ADAM_STEP = 100

beta_one = 0.9
beta_two = 0.95
learn_rate = 0.01

VMEM_LIMIT = 40 * 1024 * 1024
LARGE_LIMIT = 56 * 1024 * 1024
F32 = jnp.float32
BF16 = jnp.bfloat16


def cost(flops, nbytes):
    return pl.CostEstimate(flops=int(flops), bytes_accessed=int(nbytes), transcendentals=0)


def params(*semantics):
    if semantics:
        return pltpu.CompilerParams(vmem_limit_bytes=VMEM_LIMIT, dimension_semantics=semantics)
    return pltpu.CompilerParams(vmem_limit_bytes=VMEM_LIMIT)


def order_of(device, groups):
    if groups % 2:
        return device
    half = groups // 2
    return device % half * 2 + device // half


def row_targets(route_row, placement_row, capacity, groups):
    expert_count = placement_row.shape[1]
    row_count = route_row.shape[1]
    diagonal = lax.broadcasted_iota(jnp.int32, (expert_count, expert_count), 0) == (
        lax.broadcasted_iota(jnp.int32, (expert_count, expert_count), 1)
    )
    placement_col = jnp.sum(
        jnp.where(diagonal, placement_row, 0).astype(F32), axis=1, keepdims=True
    )
    hot = (placement_col == route_row.astype(F32)).astype(F32)
    earlier = lax.broadcasted_iota(jnp.int32, (row_count, row_count), 0)
    later = lax.broadcasted_iota(jnp.int32, (row_count, row_count), 1)
    before = (earlier < later).astype(F32).astype(BF16)
    position = jnp.dot(hot.astype(BF16), before, preferred_element_type=F32)
    slot = lax.broadcasted_iota(jnp.int32, (expert_count, row_count), 0)
    local_count = expert_count // groups
    order = order_of(slot // local_count, groups)
    start = ((order * local_count + slot % local_count) * capacity).astype(F32)
    return jnp.sum(hot * (start + position), axis=0, keepdims=True).astype(jnp.int32)


def place_matrix(target, places):
    slots = lax.broadcasted_iota(jnp.int32, (places, target.shape[1]), 0)
    return (slots == target).astype(F32).astype(BF16)


def dispatch_kernel(
    capacity, groups, route_hbm, placement_hbm, x_hbm, g_hbm, sent_hbm, target_hbm,
    route_ref, placement_ref, target_ref, x_ref, g_ref, sent_ref, key_sems, in_sems, out_sems,
):
    tiles, _, tile = g_ref.shape
    hidden = x_ref.shape[1]
    keys = [
        pltpu.make_async_copy(route_hbm, route_ref, key_sems.at[0]),
        pltpu.make_async_copy(placement_hbm, placement_ref, key_sems.at[1]),
    ]
    loads = [
        pltpu.make_async_copy(
            g_hbm.at[:, pl.ds(j * tile, tile)], g_ref.at[j], in_sems.at[j]
        )
        for j in range(tiles)
    ]
    loads.append(pltpu.make_async_copy(x_hbm, x_ref, in_sems.at[tiles]))
    for load in keys + loads:
        load.start()
    for load in keys:
        load.wait()
    target = row_targets(route_ref[...], placement_ref[...], capacity, groups)
    target_ref[...] = target
    stores = [pltpu.make_async_copy(target_ref, target_hbm, key_sems.at[2])]
    stores[0].start()
    places = place_matrix(target, sent_ref.shape[0])
    for j in range(tiles + 1):
        loads[j].wait()
        columns = pl.ds(j * tile, tile if j < tiles else hidden)
        rows = g_ref[j] if j < tiles else x_ref[...]
        sent_ref[:, columns] = jnp.dot(places, rows, preferred_element_type=F32).astype(BF16)
        store = pltpu.make_async_copy(
            sent_ref.at[:, columns], sent_hbm.at[:, columns], out_sems.at[j]
        )
        store.start()
        stores.append(store)
    for store in stores:
        store.wait()


def dispatch(route, placement, x_rows, y_cot, capacity, groups):
    row_count, hidden = x_rows.shape
    width = y_cot.shape[1]
    expert_count = placement.shape[0]
    tile = min(width, 512)
    tiles = width // tile
    places = expert_count * capacity
    hbm = pl.BlockSpec(memory_space=pl.ANY)
    return pl.pallas_call(
        functools.partial(dispatch_kernel, capacity, groups),
        in_specs=[hbm, hbm, hbm, hbm],
        out_specs=(hbm, hbm),
        out_shape=(
            jax.ShapeDtypeStruct((places, width + hidden), BF16),
            jax.ShapeDtypeStruct((1, row_count), jnp.int32),
        ),
        scratch_shapes=[
            pltpu.VMEM((1, row_count), jnp.int32),
            pltpu.VMEM((1, expert_count), jnp.int32),
            pltpu.VMEM((1, row_count), jnp.int32),
            pltpu.VMEM((row_count, hidden), BF16),
            pltpu.VMEM((tiles, row_count, tile), BF16),
            pltpu.VMEM((places, width + hidden), BF16),
            pltpu.SemaphoreType.DMA((3,)),
            pltpu.SemaphoreType.DMA((tiles + 1,)),
            pltpu.SemaphoreType.DMA((tiles + 1,)),
        ],
        compiler_params=pltpu.CompilerParams(vmem_limit_bytes=LARGE_LIMIT),
        cost_estimate=cost(
            2 * places * row_count * (hidden + width), 2 * (places + row_count) * (hidden + width)
        ),
        name="dispatch",
    )(route.reshape(1, row_count), placement.reshape(1, -1), x_rows, y_cot)


def home_places_kernel(target_ref, out_ref):
    target = target_ref[...]
    slots = lax.broadcasted_iota(jnp.int32, (out_ref.shape[1], target.shape[1]), 0)
    out_ref[...] = (slots == target).astype(F32).T.astype(BF16)


def home_places(target, places):
    return pl.pallas_call(
        home_places_kernel,
        out_shape=jax.ShapeDtypeStruct((target.shape[1], places), BF16),
        compiler_params=params(),
        cost_estimate=cost(places * target.shape[1], 2 * places * target.shape[1]),
        name="home_places",
    )(target)


def hidden_specs(rows, hidden, width):
    return [
        pl.BlockSpec((rows, BLOCK), functools.partial(lambda k, j: (0, k), width // BLOCK + i))
        for i in range(hidden // BLOCK)
    ]


def read_columns(refs):
    return jnp.concatenate([ref[...] for ref in refs], axis=1)


def collect_kernel(
    places_ref, home_hbm, y_hbm, dx_hbm, home_ref, y_ref, dx_ref, in_sems, out_sems
):
    hidden = dx_ref.shape[1]
    width = y_ref.shape[1]
    tiles = in_sems.shape[0] - 1
    tile = width // tiles
    spans = [pl.ds(j * tile, tile) for j in range(tiles)] + [pl.ds(width, hidden)]
    loads = [
        pltpu.make_async_copy(home_hbm.at[:, span], home_ref.at[:, span], in_sems.at[j])
        for j, span in enumerate(spans)
    ]
    for load in loads:
        load.start()
    places = places_ref[...]
    stores = []
    for j, span in enumerate(spans):
        loads[j].wait()
        rows = jnp.dot(places, home_ref[:, span], preferred_element_type=F32).astype(BF16)
        if j < tiles:
            y_ref[:, span] = rows
            store = pltpu.make_async_copy(y_ref.at[:, span], y_hbm.at[:, span], out_sems.at[j])
        else:
            dx_ref[...] = rows
            store = pltpu.make_async_copy(dx_ref, dx_hbm, out_sems.at[j])
        store.start()
        stores.append(store)
    for store in stores:
        store.wait()


def collect(places, home, hidden):
    total, width = home.shape
    width -= hidden
    row_count = places.shape[0]
    tiles = width // min(width, 512)
    whole = pl.BlockSpec(memory_space=pltpu.VMEM)
    hbm = pl.BlockSpec(memory_space=pl.ANY)
    return pl.pallas_call(
        collect_kernel,
        in_specs=[whole, hbm],
        out_specs=(hbm, hbm),
        out_shape=(
            jax.ShapeDtypeStruct((row_count, width), BF16),
            jax.ShapeDtypeStruct((row_count, hidden), BF16),
        ),
        scratch_shapes=[
            pltpu.VMEM((total, width + hidden), BF16),
            pltpu.VMEM((row_count, width), BF16),
            pltpu.VMEM((row_count, hidden), BF16),
            pltpu.SemaphoreType.DMA((tiles + 1,)),
            pltpu.SemaphoreType.DMA((tiles + 1,)),
        ],
        compiler_params=params(),
        cost_estimate=cost(
            2 * total * row_count * (hidden + width), 2 * (total + row_count) * (hidden + width)
        ),
        name="collect",
    )(places, home)


def member_rows(rows, capacity, local_count):
    index = lax.broadcasted_iota(jnp.int32, (rows, 1), 0)
    return lax.rem(index, capacity * local_count) // capacity


def spread(x, capacity, local_count):
    member = member_rows(x.shape[0], capacity, local_count)
    zero = jnp.zeros_like(x)
    return jnp.concatenate([jnp.where(member == e, x, zero) for e in range(local_count)], axis=1)


def join_weight(piece_refs, joined_ref):
    local_count, rows, width = piece_refs[0].shape
    if len(piece_refs) == 1:
        return piece_refs[0][...].reshape(local_count * rows, width)
    here = lax.axis_index("rep")
    for i, ref in enumerate(piece_refs):
        owner = jnp.bitwise_xor(here, i)
        for e in range(local_count):
            joined_ref[e, owner] = ref[e]
    return joined_ref[...].reshape(local_count * len(piece_refs) * rows, width)


def products_kernel(capacity, local_count, pieces, g_ref, *refs):
    w_refs = refs[:pieces]
    x_refs, out_hbm = refs[pieces:-6], refs[-6]
    joined_ref, wide_ref, total_ref, out_ref, out_sems = refs[-5:]
    step = pl.program_id(0)
    steps = out_sems.shape[0] - 1
    tile = g_ref.shape[1]
    hidden = wide_ref.shape[1] // local_count
    columns = pl.ds(pl.multiple_of(step * tile, tile), tile)

    @pl.when(step == 0)
    def _():
        wide_ref[...] = spread(read_columns(x_refs), capacity, local_count)
        total_ref[...] = jnp.zeros_like(total_ref)

    weight = join_weight(w_refs, joined_ref)
    out_ref[:, columns] = jnp.dot(
        wide_ref[...], weight, preferred_element_type=F32
    ).astype(BF16)
    pltpu.make_async_copy(
        out_ref.at[:, columns], out_hbm.at[:, columns], out_sems.at[step]
    ).start()
    total_ref[...] += lax.dot_general(
        g_ref[...], weight, (((1,), (1,)), ((), ())), preferred_element_type=F32
    )

    @pl.when(step == steps - 1)
    def _():
        member = member_rows(total_ref.shape[0], capacity, local_count)
        picked = total_ref[:, :hidden]
        for e in range(1, local_count):
            picked = jnp.where(member == e, total_ref[:, e * hidden : (e + 1) * hidden], picked)
        last = pl.ds(steps * tile, hidden)
        out_ref[:, last] = picked.astype(BF16)
        final = pltpu.make_async_copy(out_ref.at[:, last], out_hbm.at[:, last], out_sems.at[steps])
        final.start()
        for j in range(steps):
            span = pl.ds(j * tile, tile)
            pltpu.make_async_copy(out_ref.at[:, span], out_hbm.at[:, span], out_sems.at[j]).wait()
        final.wait()


def products(local, weight, capacity):
    local_count, slice_rows, width = weight[0].shape
    pieces = len(weight)
    hidden = slice_rows * pieces
    total = local.shape[0]
    tile = min(width, 512)
    tiles = width // tile
    specs = hidden_specs(total, hidden, width)
    return pl.pallas_call(
        functools.partial(products_kernel, capacity, local_count, pieces),
        grid=(tiles,),
        in_specs=[pl.BlockSpec((total, tile), lambda j: (0, j))]
        + [pl.BlockSpec((local_count, slice_rows, tile), lambda j: (0, 0, j))] * pieces
        + specs,
        out_specs=pl.BlockSpec(memory_space=pl.ANY),
        out_shape=jax.ShapeDtypeStruct(local.shape, BF16),
        scratch_shapes=[
            pltpu.VMEM((local_count, pieces, slice_rows, tile), BF16),
            pltpu.VMEM((total, local_count * hidden), BF16),
            pltpu.VMEM((total, local_count * hidden), F32),
            pltpu.VMEM(local.shape, BF16),
            pltpu.SemaphoreType.DMA((tiles + 1,)),
        ],
        compiler_params=pltpu.CompilerParams(
            vmem_limit_bytes=LARGE_LIMIT, dimension_semantics=("arbitrary",)
        ),
        cost_estimate=cost(
            4 * total * local_count * hidden * width,
            2 * (local_count * hidden + 2 * total) * width,
        ),
        name="products",
    )(local, *weight, *([local] * len(specs)))


def gradient_kernel(capacity, local_count, parts, factor, g_ref, *refs):
    blocks = len(refs) - 2 - (parts if parts > 1 else 0)
    x_refs, wide_ref = refs[:blocks], refs[-1]
    out_refs = refs[blocks:-2] if parts > 1 else refs[blocks:-1]

    @pl.when(pl.program_id(0) == 0)
    def _():
        wide_ref[...] = spread(read_columns(x_refs), capacity, local_count)

    outer = lax.dot_general(
        wide_ref[...], g_ref[...], (((0,), (0,)), ((), ())), preferred_element_type=F32
    )
    low = (outer * factor).astype(BF16)
    if parts == 1:
        out_refs[0][...] = low.reshape(out_refs[0].shape)
        return
    split_ref = refs[-2]
    split_ref[...] = low.reshape(split_ref.shape)
    here = lax.axis_index("rep")
    for i, out_ref in enumerate(out_refs):
        owner = jnp.bitwise_xor(here, i)
        for e in range(local_count):
            out_ref[e] = split_ref[e, owner]


def gradient(local, hidden, capacity, local_count, parts, factor):
    total, width = local.shape
    width -= hidden
    tile = min(width, 512)
    slice_rows = hidden // parts
    specs = hidden_specs(total, hidden, width)
    split = [pltpu.VMEM((local_count, parts, slice_rows, tile), BF16)] if parts > 1 else []
    return list(pl.pallas_call(
        functools.partial(gradient_kernel, capacity, local_count, parts, factor),
        grid=(width // tile,),
        in_specs=[pl.BlockSpec((total, tile), lambda j: (0, j))] + specs,
        out_specs=(pl.BlockSpec((local_count, slice_rows, tile), lambda j: (0, 0, j)),) * parts,
        out_shape=(jax.ShapeDtypeStruct((local_count, slice_rows, width), BF16),) * parts,
        scratch_shapes=split + [pltpu.VMEM((total, local_count * hidden), BF16)],
        compiler_params=pltpu.CompilerParams(
            vmem_limit_bytes=LARGE_LIMIT, dimension_semantics=("arbitrary",)
        ),
        cost_estimate=cost(
            2 * total * local_count * hidden * width,
            2 * (local_count * hidden + total) * width,
        ),
        name="gradient",
    )(*([local] * (1 + len(specs)))))


def cast_kernel(w_ref, out_ref):
    out_ref[...] = w_ref[...].astype(BF16)


def cast_weight(weight):
    members, rows, width = weight.shape
    tile = min(width, 512)
    spec = pl.BlockSpec((members, rows, tile), lambda j: (0, 0, j))
    return pl.pallas_call(
        cast_kernel,
        grid=(width // tile,),
        in_specs=[spec],
        out_specs=spec,
        out_shape=jax.ShapeDtypeStruct(weight.shape, BF16),
        compiler_params=params("arbitrary"),
        cost_estimate=cost(weight.size, 6 * weight.size),
        name="cast_weight",
    )(weight)


def add_kernel(a_ref, b_ref, out_ref):
    out_ref[...] = (a_ref[...].astype(F32) + b_ref[...].astype(F32)).astype(BF16)


def add_parts(a, b):
    members, rows, width = a.shape
    tile = min(width, 1024)
    spec = pl.BlockSpec((members, rows, tile), lambda j: (0, 0, j))
    return pl.pallas_call(
        add_kernel,
        grid=(width // tile,),
        in_specs=[spec, spec],
        out_specs=spec,
        out_shape=jax.ShapeDtypeStruct(a.shape, BF16),
        compiler_params=params("arbitrary"),
        cost_estimate=cost(a.size, 6 * a.size),
        name="add_parts",
    )(a, b)


def adam_kernel(
    parts, master_ref, mc_ref, ms_ref, vc_ref, vs_ref, *refs
):
    grad_refs = refs[:parts]
    master_out, mc_out, ms_out, vc_out, vs_out = refs[parts:]
    blocks = ms_ref.shape[1]
    rows = ms_ref.shape[2]
    corr_one = 1.0 - beta_one**ADAM_STEP
    corr_two = 1.0 - beta_two**ADAM_STEP
    m_scales = (ms_ref[0] * beta_one).T
    v_scales = (vs_ref[0] * beta_two).T
    lane = lax.broadcasted_iota(jnp.int32, (rows, blocks), 1)
    m_tops = jnp.zeros((rows, blocks), F32)
    v_tops = jnp.zeros((rows, blocks), F32)
    for b in range(blocks):
        cols = slice(b * BLOCK, (b + 1) * BLOCK)
        grad = grad_refs[0][0, :, cols].astype(F32)
        for ref in grad_refs[1:]:
            grad = grad + ref[0, :, cols].astype(F32)
        m_next = mc_ref[0, :, cols].astype(F32) * m_scales[:, b : b + 1] + (1.0 - beta_one) * grad
        v_next = vc_ref[0, :, cols].astype(F32) * v_scales[:, b : b + 1] + (
            1.0 - beta_two
        ) * (grad * grad)
        v_hat = v_next * (1.0 / corr_two)
        root = v_hat * lax.rsqrt(v_hat) + 1e-08
        master_out[0, :, cols] = master_ref[0, :, cols] - (learn_rate / corr_one) * m_next / root
        m_top = jnp.max(jnp.abs(m_next), axis=-1, keepdims=True) + 1e-06
        v_top = jnp.max(v_next, axis=-1, keepdims=True) + 1e-06
        mc_out[0, :, cols] = (m_next * (1.0 / m_top)).astype(BF16)
        vc_out[0, :, cols] = (v_next * (1.0 / v_top)).astype(BF16)
        m_tops = jnp.where(lane == b, m_top, m_tops)
        v_tops = jnp.where(lane == b, v_top, v_tops)
    ms_out[0] = m_tops.T
    vs_out[0] = v_tops.T


def adam(master_weight, grads, m_code, m_scale, v_code, v_scale):
    members, rows, width = master_weight.shape
    blocks = m_scale.shape[-1]
    count = 8 if blocks % 8 == 0 else blocks
    big = pl.BlockSpec((1, rows, count * BLOCK), lambda e, j: (e, 0, j))
    small = pl.BlockSpec((1, count, rows), lambda e, j: (e, j, 0))
    scales = jax.ShapeDtypeStruct((members, blocks, rows), F32)
    master_next, m_code_next, m_scale_next, v_code_next, v_scale_next = pl.pallas_call(
        functools.partial(adam_kernel, len(grads)),
        grid=(members, blocks // count),
        in_specs=[big, big, small, big, small] + [big] * len(grads),
        out_specs=(big, big, small, big, small),
        out_shape=(
            jax.ShapeDtypeStruct(master_weight.shape, F32),
            jax.ShapeDtypeStruct(master_weight.shape, BF16),
            scales,
            jax.ShapeDtypeStruct(master_weight.shape, BF16),
            scales,
        ),
        compiler_params=params("arbitrary", "arbitrary"),
        cost_estimate=cost(40 * master_weight.size, 18 * master_weight.size),
        name="adam",
    )(master_weight, m_code, jnp.swapaxes(m_scale, 1, 2), v_code, jnp.swapaxes(v_scale, 1, 2), *grads)
    return (
        master_next,
        m_code_next,
        jnp.swapaxes(m_scale_next, 1, 2),
        v_code_next,
        jnp.swapaxes(v_scale_next, 1, 2),
    )


def swap(array, axis, offset):
    size = lax.axis_size(axis)
    return lax.ppermute(array, axis, [(i, i ^ offset) for i in range(size)])


def exchange(buffer, groups):
    places, width = buffer.shape
    parts = buffer.reshape(groups, places // groups, width)
    members = sorted(range(groups), key=lambda device: order_of(device, groups))
    moved = lax.all_to_all(
        parts, "grp", split_axis=0, concat_axis=0, tiled=True, axis_index_groups=[members]
    )
    return moved.reshape(places, width)


def gather_weight(weight_slice, replicas):
    if replicas != 4:
        return [lax.all_gather(weight_slice, "rep", axis=1, tiled=True)]
    far = swap(weight_slice, "rep", 2)
    near = swap(weight_slice, "rep", 1)
    return [weight_slice, near, far, swap(far, "rep", 1)]


def sum_gradient(parts):
    if len(parts) != 4:
        return [lax.psum_scatter(parts[0], "rep", scatter_dimension=1, tiled=True)]
    far = swap(parts[3], "rep", 1)
    near = swap(parts[1], "rep", 1)
    return [parts[0], near, swap(add_parts(parts[2], far), "rep", 2)]


def per_device(master_weight, m_code, m_scale, v_code, v_scale, placement, route, x_rows, y_cot):
    local_count = master_weight.shape[0]
    row_count = x_rows.shape[0]
    expert_count = placement.shape[0]
    groups = lax.axis_size("grp")
    replicas = lax.axis_size("rep")
    grad_factor = float(row_count * groups * replicas // expert_count) ** (-0.5)
    capacity = max(2, (3 * row_count + 2 * expert_count - 1) // (2 * expert_count))
    places = expert_count * capacity
    sent, target = dispatch(route, placement, x_rows, y_cot, capacity, groups)
    local = exchange(sent, groups)
    early_master, target = lax.optimization_barrier((master_weight, target))
    weight = gather_weight(cast_weight(early_master), replicas)
    results = products(local, weight, capacity)
    local, results = lax.optimization_barrier((local, results))
    home = exchange(results, groups)

    parts = replicas if replicas == 4 else 1
    hidden = x_rows.shape[1]
    grads = sum_gradient(gradient(local, hidden, capacity, local_count, parts, grad_factor))
    updated = adam(master_weight, grads, m_code, m_scale, v_code, v_scale)
    y_rows, x_grad = collect(home_places(target, places), home, hidden)
    return (y_rows, x_grad) + tuple(updated)


def solution(mesh):
    return jax.shard_map(
        per_device,
        mesh=mesh,
        in_specs=(
            P("grp", "rep", None),
            P("grp", "rep", None),
            P("grp", "rep", None),
            P("grp", "rep", None),
            P("grp", "rep", None),
            P(),
            P(("rep", "grp")),
            P(("rep", "grp"), None),
            P(("rep", "grp"), None),
        ),
        out_specs=(
            P(("rep", "grp"), None),
            P(("rep", "grp"), None),
            P("grp", "rep", None),
            P("grp", "rep", None),
            P("grp", "rep", None),
            P("grp", "rep", None),
            P("grp", "rep", None),
        ),
        check_vma=False,
    )
```

```python
import functools

import jax
import jax.numpy as jnp
from jax import lax
from jax.experimental import pallas as pl
from jax.experimental.pallas import tpu as pltpu
from jax.sharding import PartitionSpec as P

BLOCK = 128
ADAM_STEP = 100

beta_one = 0.9
beta_two = 0.95
learn_rate = 0.01

VMEM_LIMIT = 40 * 1024 * 1024
LARGE_LIMIT = 56 * 1024 * 1024
F32 = jnp.float32
BF16 = jnp.bfloat16


def cost(flops, nbytes):
    return pl.CostEstimate(flops=int(flops), bytes_accessed=int(nbytes), transcendentals=0)


def params(*semantics):
    if semantics:
        return pltpu.CompilerParams(vmem_limit_bytes=VMEM_LIMIT, dimension_semantics=semantics)
    return pltpu.CompilerParams(vmem_limit_bytes=VMEM_LIMIT)


def order_of(device, groups):
    if groups % 2:
        return device
    half = groups // 2
    return device % half * 2 + device // half


def row_targets(route_row, placement_row, capacity, groups):
    expert_count = placement_row.shape[1]
    row_count = route_row.shape[1]
    diagonal = lax.broadcasted_iota(jnp.int32, (expert_count, expert_count), 0) == (
        lax.broadcasted_iota(jnp.int32, (expert_count, expert_count), 1)
    )
    placement_col = jnp.sum(
        jnp.where(diagonal, placement_row, 0).astype(F32), axis=1, keepdims=True
    )
    hot = (placement_col == route_row.astype(F32)).astype(F32)
    earlier = lax.broadcasted_iota(jnp.int32, (row_count, row_count), 0)
    later = lax.broadcasted_iota(jnp.int32, (row_count, row_count), 1)
    before = (earlier < later).astype(F32).astype(BF16)
    position = jnp.dot(hot.astype(BF16), before, preferred_element_type=F32)
    slot = lax.broadcasted_iota(jnp.int32, (expert_count, row_count), 0)
    local_count = expert_count // groups
    order = order_of(slot // local_count, groups)
    start = ((order * local_count + slot % local_count) * capacity).astype(F32)
    return jnp.sum(hot * (start + position), axis=0, keepdims=True).astype(jnp.int32)


def place_matrix(target, places):
    slots = lax.broadcasted_iota(jnp.int32, (places, target.shape[1]), 0)
    return (slots == target).astype(F32).astype(BF16)


def dispatch_kernel(
    capacity, groups, route_hbm, placement_hbm, x_hbm, g_hbm, sent_hbm, target_hbm,
    route_ref, placement_ref, target_ref, x_ref, g_ref, sent_ref, key_sems, in_sems, out_sems,
):
    tiles, _, tile = g_ref.shape
    hidden = x_ref.shape[1]
    keys = [
        pltpu.make_async_copy(route_hbm, route_ref, key_sems.at[0]),
        pltpu.make_async_copy(placement_hbm, placement_ref, key_sems.at[1]),
    ]
    loads = [
        pltpu.make_async_copy(
            g_hbm.at[:, pl.ds(j * tile, tile)], g_ref.at[j], in_sems.at[j]
        )
        for j in range(tiles)
    ]
    loads.append(pltpu.make_async_copy(x_hbm, x_ref, in_sems.at[tiles]))
    for load in keys + loads:
        load.start()
    for load in keys:
        load.wait()
    target = row_targets(route_ref[...], placement_ref[...], capacity, groups)
    target_ref[...] = target
    stores = [pltpu.make_async_copy(target_ref, target_hbm, key_sems.at[2])]
    stores[0].start()
    places = place_matrix(target, sent_ref.shape[0])
    for j in range(tiles + 1):
        loads[j].wait()
        columns = pl.ds(j * tile, tile if j < tiles else hidden)
        rows = g_ref[j] if j < tiles else x_ref[...]
        sent_ref[:, columns] = jnp.dot(places, rows, preferred_element_type=F32).astype(BF16)
        store = pltpu.make_async_copy(
            sent_ref.at[:, columns], sent_hbm.at[:, columns], out_sems.at[j]
        )
        store.start()
        stores.append(store)
    for store in stores:
        store.wait()


def dispatch(route, placement, x_rows, y_cot, capacity, groups):
    row_count, hidden = x_rows.shape
    width = y_cot.shape[1]
    expert_count = placement.shape[0]
    tile = min(width, 512)
    tiles = width // tile
    places = expert_count * capacity
    hbm = pl.BlockSpec(memory_space=pl.ANY)
    return pl.pallas_call(
        functools.partial(dispatch_kernel, capacity, groups),
        in_specs=[hbm, hbm, hbm, hbm],
        out_specs=(hbm, hbm),
        out_shape=(
            jax.ShapeDtypeStruct((places, width + hidden), BF16),
            jax.ShapeDtypeStruct((1, row_count), jnp.int32),
        ),
        scratch_shapes=[
            pltpu.VMEM((1, row_count), jnp.int32),
            pltpu.VMEM((1, expert_count), jnp.int32),
            pltpu.VMEM((1, row_count), jnp.int32),
            pltpu.VMEM((row_count, hidden), BF16),
            pltpu.VMEM((tiles, row_count, tile), BF16),
            pltpu.VMEM((places, width + hidden), BF16),
            pltpu.SemaphoreType.DMA((3,)),
            pltpu.SemaphoreType.DMA((tiles + 1,)),
            pltpu.SemaphoreType.DMA((tiles + 1,)),
        ],
        compiler_params=pltpu.CompilerParams(vmem_limit_bytes=LARGE_LIMIT),
        cost_estimate=cost(
            2 * places * row_count * (hidden + width), 2 * (places + row_count) * (hidden + width)
        ),
        name="dispatch",
    )(route.reshape(1, row_count), placement.reshape(1, -1), x_rows, y_cot)


def home_places_kernel(target_ref, out_ref):
    target = target_ref[...]
    slots = lax.broadcasted_iota(jnp.int32, (out_ref.shape[1], target.shape[1]), 0)
    out_ref[...] = (slots == target).astype(F32).T.astype(BF16)


def home_places(target, places):
    return pl.pallas_call(
        home_places_kernel,
        out_shape=jax.ShapeDtypeStruct((target.shape[1], places), BF16),
        compiler_params=params(),
        cost_estimate=cost(places * target.shape[1], 2 * places * target.shape[1]),
        name="home_places",
    )(target)


def collect_kernel(
    places_hbm, home_hbm, y_hbm, dx_hbm,
    places_ref, home_ref, y_ref, dx_ref, places_sem, in_sems, out_sems,
):
    hidden = dx_ref.shape[1]
    width = y_ref.shape[1]
    tiles = in_sems.shape[0] - 1
    tile = width // tiles
    spans = [pl.ds(j * tile, tile) for j in range(tiles)] + [pl.ds(width, hidden)]
    loads = [
        pltpu.make_async_copy(home_hbm.at[:, span], home_ref.at[:, span], in_sems.at[j])
        for j, span in enumerate(spans)
    ]
    places_load = pltpu.make_async_copy(places_hbm, places_ref, places_sem)
    for load in [places_load] + loads:
        load.start()
    places_load.wait()
    places = places_ref[...]
    stores = []
    for j, span in enumerate(spans):
        loads[j].wait()
        rows = jnp.dot(places, home_ref[:, span], preferred_element_type=F32).astype(BF16)
        if j < tiles:
            y_ref[:, span] = rows
            store = pltpu.make_async_copy(y_ref.at[:, span], y_hbm.at[:, span], out_sems.at[j])
        else:
            dx_ref[...] = rows
            store = pltpu.make_async_copy(dx_ref, dx_hbm, out_sems.at[j])
        store.start()
        stores.append(store)
    for store in stores:
        store.wait()


def collect(places, home, hidden):
    total, width = home.shape
    width -= hidden
    row_count = places.shape[0]
    tiles = width // min(width, 512)
    hbm = pl.BlockSpec(memory_space=pl.ANY)
    return pl.pallas_call(
        collect_kernel,
        in_specs=[hbm, hbm],
        out_specs=(hbm, hbm),
        out_shape=(
            jax.ShapeDtypeStruct((row_count, width), BF16),
            jax.ShapeDtypeStruct((row_count, hidden), BF16),
        ),
        scratch_shapes=[
            pltpu.VMEM(places.shape, BF16),
            pltpu.VMEM((total, width + hidden), BF16),
            pltpu.VMEM((row_count, width), BF16),
            pltpu.VMEM((row_count, hidden), BF16),
            pltpu.SemaphoreType.DMA,
            pltpu.SemaphoreType.DMA((tiles + 1,)),
            pltpu.SemaphoreType.DMA((tiles + 1,)),
        ],
        compiler_params=params(),
        cost_estimate=cost(
            2 * total * row_count * (hidden + width), 2 * (total + row_count) * (hidden + width)
        ),
        name="collect",
    )(places, home)


def member_rows(rows, capacity, local_count):
    index = lax.broadcasted_iota(jnp.int32, (rows, 1), 0)
    return lax.rem(index, capacity * local_count) // capacity


def spread(x, capacity, local_count):
    member = member_rows(x.shape[0], capacity, local_count)
    zero = jnp.zeros_like(x)
    return jnp.concatenate([jnp.where(member == e, x, zero) for e in range(local_count)], axis=1)


def products_kernel(capacity, pieces, local_ref, *refs):
    w_hbm, out_hbm = refs[:pieces], refs[pieces]
    w_ref, wide_ref, total_ref, out_ref, w_sems, out_sems = refs[pieces + 1 :]
    step = pl.program_id(0)
    steps, local_count, _, _, tile = w_ref.shape
    hidden = wide_ref.shape[1] // local_count
    columns = pl.ds(pl.multiple_of(step * tile, tile), tile)
    here = lax.axis_index("rep") if pieces > 1 else 0

    def weight_loads(j, span):
        return [
            pltpu.make_async_copy(
                piece.at[e, :, span],
                w_ref.at[j, e, jnp.bitwise_xor(here, i) if pieces > 1 else 0],
                w_sems.at[j, i, e],
            )
            for i, piece in enumerate(w_hbm)
            for e in range(local_count)
        ]

    @pl.when(step == 0)
    def _():
        for j in range(steps):
            for load in weight_loads(j, pl.ds(j * tile, tile)):
                load.start()
        wide_ref[...] = spread(local_ref[:, steps * tile :], capacity, local_count)
        total_ref[...] = jnp.zeros_like(total_ref)

    for load in weight_loads(step, columns):
        load.wait()
    weight = w_ref[step].reshape(local_count * hidden, tile)
    out_ref[:, columns] = jnp.dot(
        wide_ref[...], weight, preferred_element_type=F32
    ).astype(BF16)
    pltpu.make_async_copy(
        out_ref.at[:, columns], out_hbm.at[:, columns], out_sems.at[step]
    ).start()
    total_ref[...] += lax.dot_general(
        local_ref[:, columns], weight, (((1,), (1,)), ((), ())), preferred_element_type=F32
    )

    @pl.when(step == steps - 1)
    def _():
        member = member_rows(total_ref.shape[0], capacity, local_count)
        picked = total_ref[:, :hidden]
        for e in range(1, local_count):
            picked = jnp.where(member == e, total_ref[:, e * hidden : (e + 1) * hidden], picked)
        last = pl.ds(steps * tile, hidden)
        out_ref[:, last] = picked.astype(BF16)
        final = pltpu.make_async_copy(out_ref.at[:, last], out_hbm.at[:, last], out_sems.at[steps])
        final.start()
        for j in range(steps):
            span = pl.ds(j * tile, tile)
            pltpu.make_async_copy(out_ref.at[:, span], out_hbm.at[:, span], out_sems.at[j]).wait()
        final.wait()


def products(local, weight, capacity):
    local_count, slice_rows, width = weight[0].shape
    pieces = len(weight)
    hidden = slice_rows * pieces
    total = local.shape[0]
    tile = min(width, 512)
    tiles = width // tile
    hbm = pl.BlockSpec(memory_space=pltpu.HBM)
    return pl.pallas_call(
        functools.partial(products_kernel, capacity, pieces),
        grid=(tiles,),
        in_specs=[pl.BlockSpec(memory_space=pltpu.VMEM)] + [hbm] * pieces,
        out_specs=hbm,
        out_shape=jax.ShapeDtypeStruct(local.shape, BF16),
        scratch_shapes=[
            pltpu.VMEM((tiles, local_count, pieces, slice_rows, tile), BF16),
            pltpu.VMEM((total, local_count * hidden), BF16),
            pltpu.VMEM((total, local_count * hidden), F32),
            pltpu.VMEM(local.shape, BF16),
            pltpu.SemaphoreType.DMA((tiles, pieces, local_count)),
            pltpu.SemaphoreType.DMA((tiles + 1,)),
        ],
        compiler_params=params("arbitrary"),
        cost_estimate=cost(
            4 * total * local_count * hidden * width,
            2 * (local_count * hidden + 2 * total) * width,
        ),
        name="products",
    )(local, *weight)


def gradient_kernel(capacity, local_count, parts, factor, local_ref, *refs):
    out_refs, wide_ref = refs[:parts], refs[-1]
    step = pl.program_id(0)
    tile = out_refs[0].shape[-1]
    width = local_ref.shape[1] - wide_ref.shape[1] // local_count

    @pl.when(step == 0)
    def _():
        wide_ref[...] = spread(local_ref[:, width:], capacity, local_count)

    columns = pl.ds(pl.multiple_of(step * tile, tile), tile)
    outer = lax.dot_general(
        wide_ref[...], local_ref[:, columns], (((0,), (0,)), ((), ())),
        preferred_element_type=F32,
    )
    low = (outer * factor).astype(BF16)
    if parts == 1:
        out_refs[0][...] = low.reshape(out_refs[0].shape)
        return
    split_ref = refs[parts]
    split_ref[...] = low.reshape(split_ref.shape)
    here = lax.axis_index("rep")
    for i, out_ref in enumerate(out_refs):
        owner = jnp.bitwise_xor(here, i)
        for e in range(local_count):
            out_ref[e] = split_ref[e, owner]


def gradient(local, hidden, capacity, local_count, parts, factor):
    total, width = local.shape
    width -= hidden
    tile = min(width, 512)
    slice_rows = hidden // parts
    split = [pltpu.VMEM((local_count, parts, slice_rows, tile), BF16)] if parts > 1 else []
    return list(pl.pallas_call(
        functools.partial(gradient_kernel, capacity, local_count, parts, factor),
        grid=(width // tile,),
        in_specs=[pl.BlockSpec(memory_space=pltpu.VMEM)],
        out_specs=(pl.BlockSpec((local_count, slice_rows, tile), lambda j: (0, 0, j)),) * parts,
        out_shape=(jax.ShapeDtypeStruct((local_count, slice_rows, width), BF16),) * parts,
        scratch_shapes=split + [pltpu.VMEM((total, local_count * hidden), BF16)],
        compiler_params=params("arbitrary"),
        cost_estimate=cost(
            2 * total * local_count * hidden * width,
            2 * (local_count * hidden + total) * width,
        ),
        name="gradient",
    )(local))


def cast_kernel(w_ref, out_ref):
    out_ref[...] = w_ref[...].astype(BF16)


def cast_weight(weight):
    members, rows, width = weight.shape
    tile = min(width, 512)
    spec = pl.BlockSpec((members, rows, tile), lambda j: (0, 0, j))
    return pl.pallas_call(
        cast_kernel,
        grid=(width // tile,),
        in_specs=[spec],
        out_specs=spec,
        out_shape=jax.ShapeDtypeStruct(weight.shape, BF16),
        compiler_params=params("arbitrary"),
        cost_estimate=cost(weight.size, 6 * weight.size),
        name="cast_weight",
    )(weight)


def add_kernel(a_ref, b_ref, out_ref):
    out_ref[...] = (a_ref[...].astype(F32) + b_ref[...].astype(F32)).astype(BF16)


def add_parts(a, b):
    members, rows, width = a.shape
    tile = min(width, 1024)
    spec = pl.BlockSpec((members, rows, tile), lambda j: (0, 0, j))
    return pl.pallas_call(
        add_kernel,
        grid=(width // tile,),
        in_specs=[spec, spec],
        out_specs=spec,
        out_shape=jax.ShapeDtypeStruct(a.shape, BF16),
        compiler_params=params("arbitrary"),
        cost_estimate=cost(a.size, 6 * a.size),
        name="add_parts",
    )(a, b)


def adam_kernel(
    parts, master_ref, mc_ref, ms_ref, vc_ref, vs_ref, *refs
):
    grad_refs = refs[:parts]
    master_out, mc_out, ms_out, vc_out, vs_out = refs[parts:]
    blocks = ms_ref.shape[1]
    rows = ms_ref.shape[2]
    corr_one = 1.0 - beta_one**ADAM_STEP
    corr_two = 1.0 - beta_two**ADAM_STEP
    m_scales = (ms_ref[0] * beta_one).T
    v_scales = (vs_ref[0] * beta_two).T
    lane = lax.broadcasted_iota(jnp.int32, (rows, blocks), 1)
    m_tops = jnp.zeros((rows, blocks), F32)
    v_tops = jnp.zeros((rows, blocks), F32)
    for b in range(blocks):
        cols = slice(b * BLOCK, (b + 1) * BLOCK)
        grad = grad_refs[0][0, :, cols].astype(F32)
        for ref in grad_refs[1:]:
            grad = grad + ref[0, :, cols].astype(F32)
        m_next = mc_ref[0, :, cols].astype(F32) * m_scales[:, b : b + 1] + (1.0 - beta_one) * grad
        v_next = vc_ref[0, :, cols].astype(F32) * v_scales[:, b : b + 1] + (
            1.0 - beta_two
        ) * (grad * grad)
        v_hat = v_next * (1.0 / corr_two)
        root = v_hat * lax.rsqrt(v_hat) + 1e-08
        master_out[0, :, cols] = master_ref[0, :, cols] - (learn_rate / corr_one) * m_next / root
        m_top = jnp.max(jnp.abs(m_next), axis=-1, keepdims=True) + 1e-06
        v_top = jnp.max(v_next, axis=-1, keepdims=True) + 1e-06
        mc_out[0, :, cols] = (m_next * (1.0 / m_top)).astype(BF16)
        vc_out[0, :, cols] = (v_next * (1.0 / v_top)).astype(BF16)
        m_tops = jnp.where(lane == b, m_top, m_tops)
        v_tops = jnp.where(lane == b, v_top, v_tops)
    ms_out[0] = m_tops.T
    vs_out[0] = v_tops.T


def adam(master_weight, grads, m_code, m_scale, v_code, v_scale):
    members, rows, width = master_weight.shape
    blocks = m_scale.shape[-1]
    count = 8 if blocks % 8 == 0 else blocks
    big = pl.BlockSpec((1, rows, count * BLOCK), lambda e, j: (e, 0, j))
    small = pl.BlockSpec((1, count, rows), lambda e, j: (e, j, 0))
    scales = jax.ShapeDtypeStruct((members, blocks, rows), F32)
    master_next, m_code_next, m_scale_next, v_code_next, v_scale_next = pl.pallas_call(
        functools.partial(adam_kernel, len(grads)),
        grid=(members, blocks // count),
        in_specs=[big, big, small, big, small] + [big] * len(grads),
        out_specs=(big, big, small, big, small),
        out_shape=(
            jax.ShapeDtypeStruct(master_weight.shape, F32),
            jax.ShapeDtypeStruct(master_weight.shape, BF16),
            scales,
            jax.ShapeDtypeStruct(master_weight.shape, BF16),
            scales,
        ),
        compiler_params=params("arbitrary", "arbitrary"),
        cost_estimate=cost(40 * master_weight.size, 18 * master_weight.size),
        name="adam",
    )(master_weight, m_code, jnp.swapaxes(m_scale, 1, 2), v_code, jnp.swapaxes(v_scale, 1, 2), *grads)
    return (
        master_next,
        m_code_next,
        jnp.swapaxes(m_scale_next, 1, 2),
        v_code_next,
        jnp.swapaxes(v_scale_next, 1, 2),
    )


def swap(array, axis, offset):
    size = lax.axis_size(axis)
    return lax.ppermute(array, axis, [(i, i ^ offset) for i in range(size)])


def exchange(buffer, groups):
    places, width = buffer.shape
    parts = buffer.reshape(groups, places // groups, width)
    members = sorted(range(groups), key=lambda device: order_of(device, groups))
    moved = lax.all_to_all(
        parts, "grp", split_axis=0, concat_axis=0, tiled=True, axis_index_groups=[members]
    )
    return moved.reshape(places, width)


def gather_weight(weight_slice, replicas):
    if replicas != 4:
        return [lax.all_gather(weight_slice, "rep", axis=1, tiled=True)]
    far = swap(weight_slice, "rep", 2)
    near = swap(weight_slice, "rep", 1)
    return [weight_slice, near, far, swap(far, "rep", 1)]


def sum_gradient(parts):
    if len(parts) != 4:
        return [lax.psum_scatter(parts[0], "rep", scatter_dimension=1, tiled=True)]
    far = swap(parts[3], "rep", 1)
    near = swap(parts[1], "rep", 1)
    return [parts[0], near, swap(add_parts(parts[2], far), "rep", 2)]


def per_device(master_weight, m_code, m_scale, v_code, v_scale, placement, route, x_rows, y_cot):
    local_count = master_weight.shape[0]
    row_count = x_rows.shape[0]
    expert_count = placement.shape[0]
    groups = lax.axis_size("grp")
    replicas = lax.axis_size("rep")
    grad_factor = float(row_count * groups * replicas // expert_count) ** (-0.5)
    capacity = max(2, (3 * row_count + 2 * expert_count - 1) // (2 * expert_count))
    places = expert_count * capacity
    sent, target = dispatch(route, placement, x_rows, y_cot, capacity, groups)
    local = exchange(sent, groups)
    early_master, target = lax.optimization_barrier((master_weight, target))
    weight = gather_weight(cast_weight(early_master), replicas)
    results = products(local, weight, capacity)
    local, results = lax.optimization_barrier((local, results))
    home = exchange(results, groups)

    parts = replicas if replicas == 4 else 1
    hidden = x_rows.shape[1]
    grads = sum_gradient(gradient(local, hidden, capacity, local_count, parts, grad_factor))
    updated = adam(master_weight, grads, m_code, m_scale, v_code, v_scale)
    y_rows, x_grad = collect(home_places(target, places), home, hidden)
    return (y_rows, x_grad) + tuple(updated)


def solution(mesh):
    return jax.shard_map(
        per_device,
        mesh=mesh,
        in_specs=(
            P("grp", "rep", None),
            P("grp", "rep", None),
            P("grp", "rep", None),
            P("grp", "rep", None),
            P("grp", "rep", None),
            P(),
            P(("rep", "grp")),
            P(("rep", "grp"), None),
            P(("rep", "grp"), None),
        ),
        out_specs=(
            P(("rep", "grp"), None),
            P(("rep", "grp"), None),
            P("grp", "rep", None),
            P("grp", "rep", None),
            P("grp", "rep", None),
            P("grp", "rep", None),
            P("grp", "rep", None),
        ),
        check_vma=False,
    )
```

```python
import functools

import jax
import jax.numpy as jnp
from jax import lax
from jax.experimental import pallas as pl
from jax.experimental.pallas import tpu as pltpu
from jax.sharding import PartitionSpec as P

BLOCK = 128
ADAM_STEP = 100

beta_one = 0.9
beta_two = 0.95
learn_rate = 0.01

VMEM_LIMIT = 40 * 1024 * 1024
LARGE_LIMIT = 56 * 1024 * 1024
F32 = jnp.float32
BF16 = jnp.bfloat16


def cost(flops, nbytes):
    return pl.CostEstimate(flops=int(flops), bytes_accessed=int(nbytes), transcendentals=0)


def params(*semantics):
    if semantics:
        return pltpu.CompilerParams(vmem_limit_bytes=VMEM_LIMIT, dimension_semantics=semantics)
    return pltpu.CompilerParams(vmem_limit_bytes=VMEM_LIMIT)


def order_of(device, groups):
    if groups % 2:
        return device
    half = groups // 2
    return device % half * 2 + device // half


def row_targets(route_row, placement_row, capacity, groups):
    expert_count = placement_row.shape[1]
    row_count = route_row.shape[1]
    diagonal = lax.broadcasted_iota(jnp.int32, (expert_count, expert_count), 0) == (
        lax.broadcasted_iota(jnp.int32, (expert_count, expert_count), 1)
    )
    placement_col = jnp.sum(
        jnp.where(diagonal, placement_row, 0).astype(F32), axis=1, keepdims=True
    )
    hot = (placement_col == route_row.astype(F32)).astype(F32)
    earlier = lax.broadcasted_iota(jnp.int32, (row_count, row_count), 0)
    later = lax.broadcasted_iota(jnp.int32, (row_count, row_count), 1)
    before = (earlier < later).astype(F32).astype(BF16)
    position = jnp.dot(hot.astype(BF16), before, preferred_element_type=F32)
    slot = lax.broadcasted_iota(jnp.int32, (expert_count, row_count), 0)
    local_count = expert_count // groups
    order = order_of(slot // local_count, groups)
    start = ((order * local_count + slot % local_count) * capacity).astype(F32)
    return jnp.sum(hot * (start + position), axis=0, keepdims=True).astype(jnp.int32)


def place_matrix(target, places):
    slots = lax.broadcasted_iota(jnp.int32, (places, target.shape[1]), 0)
    return (slots == target).astype(F32).astype(BF16)


def dispatch_kernel(
    capacity, groups, route_hbm, placement_hbm, x_hbm, g_hbm, sent_hbm, target_hbm,
    route_ref, placement_ref, target_ref, x_ref, g_ref, sent_ref, key_sems, in_sems, out_sems,
):
    tiles, _, tile = g_ref.shape
    hidden = x_ref.shape[1]
    keys = [
        pltpu.make_async_copy(route_hbm, route_ref, key_sems.at[0]),
        pltpu.make_async_copy(placement_hbm, placement_ref, key_sems.at[1]),
    ]
    loads = [
        pltpu.make_async_copy(
            g_hbm.at[:, pl.ds(j * tile, tile)], g_ref.at[j], in_sems.at[j]
        )
        for j in range(tiles)
    ]
    loads.append(pltpu.make_async_copy(x_hbm, x_ref, in_sems.at[tiles]))
    for load in keys + loads:
        load.start()
    for load in keys:
        load.wait()
    target = row_targets(route_ref[...], placement_ref[...], capacity, groups)
    target_ref[...] = target
    stores = [pltpu.make_async_copy(target_ref, target_hbm, key_sems.at[2])]
    stores[0].start()
    places = place_matrix(target, sent_ref.shape[0])
    for j in range(tiles + 1):
        loads[j].wait()
        columns = pl.ds(j * tile, tile if j < tiles else hidden)
        rows = g_ref[j] if j < tiles else x_ref[...]
        sent_ref[:, columns] = jnp.dot(places, rows, preferred_element_type=F32).astype(BF16)
        store = pltpu.make_async_copy(
            sent_ref.at[:, columns], sent_hbm.at[:, columns], out_sems.at[j]
        )
        store.start()
        stores.append(store)
    for store in stores:
        store.wait()


def dispatch(route, placement, x_rows, y_cot, capacity, groups):
    row_count, hidden = x_rows.shape
    width = y_cot.shape[1]
    expert_count = placement.shape[0]
    tile = min(width, 512)
    tiles = width // tile
    places = expert_count * capacity
    hbm = pl.BlockSpec(memory_space=pl.ANY)
    return pl.pallas_call(
        functools.partial(dispatch_kernel, capacity, groups),
        in_specs=[hbm, hbm, hbm, hbm],
        out_specs=(hbm, hbm),
        out_shape=(
            jax.ShapeDtypeStruct((places, width + hidden), BF16),
            jax.ShapeDtypeStruct((1, row_count), jnp.int32),
        ),
        scratch_shapes=[
            pltpu.VMEM((1, row_count), jnp.int32),
            pltpu.VMEM((1, expert_count), jnp.int32),
            pltpu.VMEM((1, row_count), jnp.int32),
            pltpu.VMEM((row_count, hidden), BF16),
            pltpu.VMEM((tiles, row_count, tile), BF16),
            pltpu.VMEM((places, width + hidden), BF16),
            pltpu.SemaphoreType.DMA((3,)),
            pltpu.SemaphoreType.DMA((tiles + 1,)),
            pltpu.SemaphoreType.DMA((tiles + 1,)),
        ],
        compiler_params=pltpu.CompilerParams(vmem_limit_bytes=LARGE_LIMIT),
        cost_estimate=cost(
            2 * places * row_count * (hidden + width), 2 * (places + row_count) * (hidden + width)
        ),
        name="dispatch",
    )(route.reshape(1, row_count), placement.reshape(1, -1), x_rows, y_cot)


def hidden_specs(rows, hidden, width):
    return [
        pl.BlockSpec((rows, BLOCK), functools.partial(lambda k, j: (0, k), width // BLOCK + i))
        for i in range(hidden // BLOCK)
    ]


def read_columns(refs):
    return jnp.concatenate([ref[...] for ref in refs], axis=1)


def collect_kernel(
    target_hbm, home_ref, y_hbm, dx_hbm, target_ref, y_ref, dx_ref, target_sem, out_sems
):
    hidden = dx_ref.shape[1]
    width = y_ref.shape[1]
    tiles = out_sems.shape[0] - 1
    tile = width // tiles
    spans = [pl.ds(j * tile, tile) for j in range(tiles)] + [pl.ds(width, hidden)]
    target_load = pltpu.make_async_copy(target_hbm, target_ref, target_sem)
    target_load.start()
    target_load.wait()
    target = target_ref[...]
    slots = lax.broadcasted_iota(jnp.int32, (home_ref.shape[0], target.shape[1]), 0)
    places = (slots == target).astype(F32).T.astype(BF16)
    stores = []
    for j, span in enumerate(spans):
        rows = jnp.dot(places, home_ref[:, span], preferred_element_type=F32).astype(BF16)
        if j < tiles:
            y_ref[:, span] = rows
            store = pltpu.make_async_copy(y_ref.at[:, span], y_hbm.at[:, span], out_sems.at[j])
        else:
            dx_ref[...] = rows
            store = pltpu.make_async_copy(dx_ref, dx_hbm, out_sems.at[j])
        store.start()
        stores.append(store)
    for store in stores:
        store.wait()


def collect(target, home, hidden):
    total, width = home.shape
    width -= hidden
    row_count = target.shape[1]
    tiles = width // min(width, 512)
    hbm = pl.BlockSpec(memory_space=pl.ANY)
    return pl.pallas_call(
        collect_kernel,
        in_specs=[hbm, pl.BlockSpec(memory_space=pltpu.VMEM)],
        out_specs=(hbm, hbm),
        out_shape=(
            jax.ShapeDtypeStruct((row_count, width), BF16),
            jax.ShapeDtypeStruct((row_count, hidden), BF16),
        ),
        scratch_shapes=[
            pltpu.VMEM(target.shape, jnp.int32),
            pltpu.VMEM((row_count, width), BF16),
            pltpu.VMEM((row_count, hidden), BF16),
            pltpu.SemaphoreType.DMA,
            pltpu.SemaphoreType.DMA((tiles + 1,)),
        ],
        compiler_params=params(),
        cost_estimate=cost(
            2 * total * row_count * (hidden + width), 2 * (total + row_count) * (hidden + width)
        ),
        name="collect",
    )(target, home)


def member_rows(rows, capacity, local_count):
    index = lax.broadcasted_iota(jnp.int32, (rows, 1), 0)
    return lax.rem(index, capacity * local_count) // capacity


def spread(x, capacity, local_count):
    member = member_rows(x.shape[0], capacity, local_count)
    zero = jnp.zeros_like(x)
    return jnp.concatenate([jnp.where(member == e, x, zero) for e in range(local_count)], axis=1)


def products_kernel(capacity, pieces, local_hbm, *refs):
    w_hbm, out_hbm = refs[:pieces], refs[pieces]
    x_ref, g_ref, w_ref, wide_ref, total_ref, out_ref, g_sems, w_sems, out_sems = refs[pieces + 1 :]
    step = pl.program_id(0)
    steps, local_count, _, _, tile = w_ref.shape
    hidden = wide_ref.shape[1] // local_count
    columns = pl.ds(pl.multiple_of(step * tile, tile), tile)
    here = lax.axis_index("rep") if pieces > 1 else 0

    def weight_loads(j, span):
        return [
            pltpu.make_async_copy(
                piece.at[e, :, span],
                w_ref.at[j, e, jnp.bitwise_xor(here, i) if pieces > 1 else 0],
                w_sems.at[j, i, e],
            )
            for i, piece in enumerate(w_hbm)
            for e in range(local_count)
        ]

    def row_load(j, span):
        return pltpu.make_async_copy(local_hbm.at[:, span], g_ref.at[j], g_sems.at[j])

    @pl.when(step == 0)
    def _():
        x_load = pltpu.make_async_copy(
            local_hbm.at[:, pl.ds(steps * tile, hidden)], x_ref, g_sems.at[steps]
        )
        x_load.start()
        for j in range(steps):
            span = pl.ds(j * tile, tile)
            for load in weight_loads(j, span) + [row_load(j, span)]:
                load.start()
        x_load.wait()
        wide_ref[...] = spread(x_ref[...], capacity, local_count)
        total_ref[...] = jnp.zeros_like(total_ref)

    for load in weight_loads(step, columns):
        load.wait()
    weight = w_ref[step].reshape(local_count * hidden, tile)
    out_ref[:, columns] = jnp.dot(
        wide_ref[...], weight, preferred_element_type=F32
    ).astype(BF16)
    pltpu.make_async_copy(
        out_ref.at[:, columns], out_hbm.at[:, columns], out_sems.at[step]
    ).start()
    row_load(step, columns).wait()
    total_ref[...] += lax.dot_general(
        g_ref[step], weight, (((1,), (1,)), ((), ())), preferred_element_type=F32
    )

    @pl.when(step == steps - 1)
    def _():
        member = member_rows(total_ref.shape[0], capacity, local_count)
        picked = total_ref[:, :hidden]
        for e in range(1, local_count):
            picked = jnp.where(member == e, total_ref[:, e * hidden : (e + 1) * hidden], picked)
        last = pl.ds(steps * tile, hidden)
        out_ref[:, last] = picked.astype(BF16)
        final = pltpu.make_async_copy(out_ref.at[:, last], out_hbm.at[:, last], out_sems.at[steps])
        final.start()
        for j in range(steps):
            span = pl.ds(j * tile, tile)
            pltpu.make_async_copy(out_ref.at[:, span], out_hbm.at[:, span], out_sems.at[j]).wait()
        final.wait()


def products(local, weight, capacity):
    local_count, slice_rows, width = weight[0].shape
    pieces = len(weight)
    hidden = slice_rows * pieces
    total = local.shape[0]
    tile = min(width, 512)
    tiles = width // tile
    hbm = pl.BlockSpec(memory_space=pl.ANY)
    return pl.pallas_call(
        functools.partial(products_kernel, capacity, pieces),
        grid=(tiles,),
        in_specs=[hbm] * (1 + pieces),
        out_specs=hbm,
        out_shape=jax.ShapeDtypeStruct(local.shape, BF16),
        scratch_shapes=[
            pltpu.VMEM((total, hidden), BF16),
            pltpu.VMEM((tiles, total, tile), BF16),
            pltpu.VMEM((tiles, local_count, pieces, slice_rows, tile), BF16),
            pltpu.VMEM((total, local_count * hidden), BF16),
            pltpu.VMEM((total, local_count * hidden), F32),
            pltpu.VMEM(local.shape, BF16),
            pltpu.SemaphoreType.DMA((tiles + 1,)),
            pltpu.SemaphoreType.DMA((tiles, pieces, local_count)),
            pltpu.SemaphoreType.DMA((tiles + 1,)),
        ],
        compiler_params=pltpu.CompilerParams(
            vmem_limit_bytes=LARGE_LIMIT, dimension_semantics=("arbitrary",)
        ),
        cost_estimate=cost(
            4 * total * local_count * hidden * width,
            2 * (local_count * hidden + 2 * total) * width,
        ),
        name="products",
    )(local, *weight)


def gradient_kernel(capacity, local_count, parts, factor, g_ref, *refs):
    blocks = len(refs) - 2 - (parts if parts > 1 else 0)
    x_refs, wide_ref = refs[:blocks], refs[-1]
    out_refs = refs[blocks:-2] if parts > 1 else refs[blocks:-1]

    @pl.when(pl.program_id(0) == 0)
    def _():
        wide_ref[...] = spread(read_columns(x_refs), capacity, local_count)

    outer = lax.dot_general(
        wide_ref[...], g_ref[...], (((0,), (0,)), ((), ())), preferred_element_type=F32
    )
    low = (outer * factor).astype(BF16)
    if parts == 1:
        out_refs[0][...] = low.reshape(out_refs[0].shape)
        return
    split_ref = refs[-2]
    split_ref[...] = low.reshape(split_ref.shape)
    here = lax.axis_index("rep")
    for i, out_ref in enumerate(out_refs):
        owner = jnp.bitwise_xor(here, i)
        for e in range(local_count):
            out_ref[e] = split_ref[e, owner]


def gradient(local, hidden, capacity, local_count, parts, factor):
    total, width = local.shape
    width -= hidden
    tile = min(width, 512)
    slice_rows = hidden // parts
    specs = hidden_specs(total, hidden, width)
    split = [pltpu.VMEM((local_count, parts, slice_rows, tile), BF16)] if parts > 1 else []
    return list(pl.pallas_call(
        functools.partial(gradient_kernel, capacity, local_count, parts, factor),
        grid=(width // tile,),
        in_specs=[pl.BlockSpec((total, tile), lambda j: (0, j))] + specs,
        out_specs=(pl.BlockSpec((local_count, slice_rows, tile), lambda j: (0, 0, j)),) * parts,
        out_shape=(jax.ShapeDtypeStruct((local_count, slice_rows, width), BF16),) * parts,
        scratch_shapes=split + [pltpu.VMEM((total, local_count * hidden), BF16)],
        compiler_params=pltpu.CompilerParams(
            vmem_limit_bytes=LARGE_LIMIT, dimension_semantics=("arbitrary",)
        ),
        cost_estimate=cost(
            2 * total * local_count * hidden * width,
            2 * (local_count * hidden + total) * width,
        ),
        name="gradient",
    )(*([local] * (1 + len(specs)))))


def cast_kernel(w_ref, out_ref):
    out_ref[...] = w_ref[...].astype(BF16)


def cast_weight(weight):
    members, rows, width = weight.shape
    tile = min(width, 512)
    spec = pl.BlockSpec((members, rows, tile), lambda j: (0, 0, j))
    return pl.pallas_call(
        cast_kernel,
        grid=(width // tile,),
        in_specs=[spec],
        out_specs=spec,
        out_shape=jax.ShapeDtypeStruct(weight.shape, BF16),
        compiler_params=params("arbitrary"),
        cost_estimate=cost(weight.size, 6 * weight.size),
        name="cast_weight",
    )(weight)


def add_kernel(a_ref, b_ref, out_ref):
    out_ref[...] = (a_ref[...].astype(F32) + b_ref[...].astype(F32)).astype(BF16)


def add_parts(a, b):
    members, rows, width = a.shape
    tile = min(width, 1024)
    spec = pl.BlockSpec((members, rows, tile), lambda j: (0, 0, j))
    return pl.pallas_call(
        add_kernel,
        grid=(width // tile,),
        in_specs=[spec, spec],
        out_specs=spec,
        out_shape=jax.ShapeDtypeStruct(a.shape, BF16),
        compiler_params=params("arbitrary"),
        cost_estimate=cost(a.size, 6 * a.size),
        name="add_parts",
    )(a, b)


def adam_kernel(
    parts, master_ref, mc_ref, ms_ref, vc_ref, vs_ref, *refs
):
    grad_refs = refs[:parts]
    master_out, mc_out, ms_out, vc_out, vs_out = refs[parts:]
    blocks = ms_ref.shape[1]
    rows = ms_ref.shape[2]
    corr_one = 1.0 - beta_one**ADAM_STEP
    corr_two = 1.0 - beta_two**ADAM_STEP
    m_scales = (ms_ref[0] * beta_one).T
    v_scales = (vs_ref[0] * beta_two).T
    lane = lax.broadcasted_iota(jnp.int32, (rows, blocks), 1)
    m_tops = jnp.zeros((rows, blocks), F32)
    v_tops = jnp.zeros((rows, blocks), F32)
    for b in range(blocks):
        cols = slice(b * BLOCK, (b + 1) * BLOCK)
        grad = grad_refs[0][0, :, cols].astype(F32)
        for ref in grad_refs[1:]:
            grad = grad + ref[0, :, cols].astype(F32)
        m_next = mc_ref[0, :, cols].astype(F32) * m_scales[:, b : b + 1] + (1.0 - beta_one) * grad
        v_next = vc_ref[0, :, cols].astype(F32) * v_scales[:, b : b + 1] + (
            1.0 - beta_two
        ) * (grad * grad)
        v_hat = v_next * (1.0 / corr_two)
        root = v_hat * lax.rsqrt(v_hat) + 1e-08
        master_out[0, :, cols] = master_ref[0, :, cols] - (learn_rate / corr_one) * m_next / root
        m_top = jnp.max(jnp.abs(m_next), axis=-1, keepdims=True) + 1e-06
        v_top = jnp.max(v_next, axis=-1, keepdims=True) + 1e-06
        mc_out[0, :, cols] = (m_next * (1.0 / m_top)).astype(BF16)
        vc_out[0, :, cols] = (v_next * (1.0 / v_top)).astype(BF16)
        m_tops = jnp.where(lane == b, m_top, m_tops)
        v_tops = jnp.where(lane == b, v_top, v_tops)
    ms_out[0] = m_tops.T
    vs_out[0] = v_tops.T


def adam(master_weight, grads, m_code, m_scale, v_code, v_scale):
    members, rows, width = master_weight.shape
    blocks = m_scale.shape[-1]
    count = 8 if blocks % 8 == 0 else blocks
    big = pl.BlockSpec((1, rows, count * BLOCK), lambda e, j: (e, 0, j))
    small = pl.BlockSpec((1, count, rows), lambda e, j: (e, j, 0))
    scales = jax.ShapeDtypeStruct((members, blocks, rows), F32)
    master_next, m_code_next, m_scale_next, v_code_next, v_scale_next = pl.pallas_call(
        functools.partial(adam_kernel, len(grads)),
        grid=(members, blocks // count),
        in_specs=[big, big, small, big, small] + [big] * len(grads),
        out_specs=(big, big, small, big, small),
        out_shape=(
            jax.ShapeDtypeStruct(master_weight.shape, F32),
            jax.ShapeDtypeStruct(master_weight.shape, BF16),
            scales,
            jax.ShapeDtypeStruct(master_weight.shape, BF16),
            scales,
        ),
        compiler_params=params("arbitrary", "arbitrary"),
        cost_estimate=cost(40 * master_weight.size, 18 * master_weight.size),
        name="adam",
    )(master_weight, m_code, jnp.swapaxes(m_scale, 1, 2), v_code, jnp.swapaxes(v_scale, 1, 2), *grads)
    return (
        master_next,
        m_code_next,
        jnp.swapaxes(m_scale_next, 1, 2),
        v_code_next,
        jnp.swapaxes(v_scale_next, 1, 2),
    )


def swap(array, axis, offset):
    size = lax.axis_size(axis)
    return lax.ppermute(array, axis, [(i, i ^ offset) for i in range(size)])


def exchange(buffer, groups):
    places, width = buffer.shape
    parts = buffer.reshape(groups, places // groups, width)
    members = sorted(range(groups), key=lambda device: order_of(device, groups))
    moved = lax.all_to_all(
        parts, "grp", split_axis=0, concat_axis=0, tiled=True, axis_index_groups=[members]
    )
    return moved.reshape(places, width)


def gather_weight(weight_slice, replicas):
    if replicas != 4:
        return [lax.all_gather(weight_slice, "rep", axis=1, tiled=True)]
    far = swap(weight_slice, "rep", 2)
    near = swap(weight_slice, "rep", 1)
    return [weight_slice, near, far, swap(far, "rep", 1)]


def sum_gradient(parts):
    if len(parts) != 4:
        return [lax.psum_scatter(parts[0], "rep", scatter_dimension=1, tiled=True)]
    far = swap(parts[3], "rep", 1)
    near = swap(parts[1], "rep", 1)
    return [parts[0], near, swap(add_parts(parts[2], far), "rep", 2)]


def per_device(master_weight, m_code, m_scale, v_code, v_scale, placement, route, x_rows, y_cot):
    local_count = master_weight.shape[0]
    row_count = x_rows.shape[0]
    expert_count = placement.shape[0]
    groups = lax.axis_size("grp")
    replicas = lax.axis_size("rep")
    grad_factor = float(row_count * groups * replicas // expert_count) ** (-0.5)
    capacity = max(2, (3 * row_count + 2 * expert_count - 1) // (2 * expert_count))
    places = expert_count * capacity
    sent, target = dispatch(route, placement, x_rows, y_cot, capacity, groups)
    local = exchange(sent, groups)
    early_master, target = lax.optimization_barrier((master_weight, target))
    weight = gather_weight(cast_weight(early_master), replicas)
    results = products(local, weight, capacity)
    local, results = lax.optimization_barrier((local, results))
    home = exchange(results, groups)

    parts = replicas if replicas == 4 else 1
    hidden = x_rows.shape[1]
    grads = sum_gradient(gradient(local, hidden, capacity, local_count, parts, grad_factor))
    updated = adam(master_weight, grads, m_code, m_scale, v_code, v_scale)
    y_rows, x_grad = collect(target, home, hidden)
    return (y_rows, x_grad) + tuple(updated)


def solution(mesh):
    return jax.shard_map(
        per_device,
        mesh=mesh,
        in_specs=(
            P("grp", "rep", None),
            P("grp", "rep", None),
            P("grp", "rep", None),
            P("grp", "rep", None),
            P("grp", "rep", None),
            P(),
            P(("rep", "grp")),
            P(("rep", "grp"), None),
            P(("rep", "grp"), None),
        ),
        out_specs=(
            P(("rep", "grp"), None),
            P(("rep", "grp"), None),
            P("grp", "rep", None),
            P("grp", "rep", None),
            P("grp", "rep", None),
            P("grp", "rep", None),
            P("grp", "rep", None),
        ),
        check_vma=False,
    )
```

```python
import functools

import jax
import jax.numpy as jnp
from jax import lax
from jax.experimental import pallas as pl
from jax.experimental.pallas import tpu as pltpu
from jax.sharding import PartitionSpec as P

BLOCK = 128
ADAM_STEP = 100

beta_one = 0.9
beta_two = 0.95
learn_rate = 0.01

VMEM_LIMIT = 40 * 1024 * 1024
LARGE_LIMIT = 56 * 1024 * 1024
F32 = jnp.float32
BF16 = jnp.bfloat16


def cost(flops, nbytes):
    return pl.CostEstimate(flops=int(flops), bytes_accessed=int(nbytes), transcendentals=0)


def params(*semantics):
    if semantics:
        return pltpu.CompilerParams(vmem_limit_bytes=VMEM_LIMIT, dimension_semantics=semantics)
    return pltpu.CompilerParams(vmem_limit_bytes=VMEM_LIMIT)


def order_of(device, groups):
    if groups % 2:
        return device
    half = groups // 2
    return device % half * 2 + device // half


def row_targets(route_row, placement_row, capacity, groups):
    expert_count = placement_row.shape[1]
    row_count = route_row.shape[1]
    diagonal = lax.broadcasted_iota(jnp.int32, (expert_count, expert_count), 0) == (
        lax.broadcasted_iota(jnp.int32, (expert_count, expert_count), 1)
    )
    placement_col = jnp.sum(
        jnp.where(diagonal, placement_row, 0).astype(F32), axis=1, keepdims=True
    )
    hot = (placement_col == route_row.astype(F32)).astype(F32)
    earlier = lax.broadcasted_iota(jnp.int32, (row_count, row_count), 0)
    later = lax.broadcasted_iota(jnp.int32, (row_count, row_count), 1)
    before = (earlier < later).astype(F32).astype(BF16)
    position = jnp.dot(hot.astype(BF16), before, preferred_element_type=F32)
    slot = lax.broadcasted_iota(jnp.int32, (expert_count, row_count), 0)
    local_count = expert_count // groups
    order = order_of(slot // local_count, groups)
    start = ((order * local_count + slot % local_count) * capacity).astype(F32)
    return jnp.sum(hot * (start + position), axis=0, keepdims=True).astype(jnp.int32)


def place_matrix(target, places):
    slots = lax.broadcasted_iota(jnp.int32, (places, target.shape[1]), 0)
    return (slots == target).astype(F32).astype(BF16)


def dispatch_kernel(
    capacity, groups, route_hbm, placement_hbm, x_hbm, g_hbm, sent_hbm, target_hbm,
    route_ref, placement_ref, target_ref, x_ref, g_ref, sent_ref, key_sems, in_sems, out_sems,
):
    row_count, hidden = x_ref.shape
    width = g_ref.shape[1]
    tiles = out_sems.shape[0] - 1
    tile = width // tiles
    parts = in_sems.shape[0] - 1
    keys = [
        pltpu.make_async_copy(route_hbm, route_ref, key_sems.at[0]),
        pltpu.make_async_copy(placement_hbm, placement_ref, key_sems.at[1]),
    ]
    bands = [pl.ds(i * (row_count // parts), row_count // parts) for i in range(parts)]
    loads = [pltpu.make_async_copy(x_hbm, x_ref, in_sems.at[parts])] + [
        pltpu.make_async_copy(g_hbm.at[band], g_ref.at[band], in_sems.at[i])
        for i, band in enumerate(bands)
    ]
    for load in keys + loads:
        load.start()
    for load in keys:
        load.wait()
    target = row_targets(route_ref[...], placement_ref[...], capacity, groups)
    target_ref[...] = target
    stores = [pltpu.make_async_copy(target_ref, target_hbm, key_sems.at[2])]
    stores[0].start()
    places = place_matrix(target, sent_ref.shape[0])
    for j in range(tiles + 1):
        for load in loads[:1] if j == 0 else loads[1:] if j == 1 else []:
            load.wait()
        columns = pl.ds((j - 1) * tile, tile) if j else pl.ds(width, hidden)
        rows = g_ref[:, columns] if j else x_ref[...]
        sent_ref[:, columns] = jnp.dot(places, rows, preferred_element_type=F32).astype(BF16)
        store = pltpu.make_async_copy(
            sent_ref.at[:, columns], sent_hbm.at[:, columns], out_sems.at[j]
        )
        store.start()
        stores.append(store)
    for store in stores:
        store.wait()


def dispatch(route, placement, x_rows, y_cot, capacity, groups):
    row_count, hidden = x_rows.shape
    width = y_cot.shape[1]
    expert_count = placement.shape[0]
    tile = min(width, 512)
    tiles = width // tile
    parts = 4 if row_count % 64 == 0 else 1
    places = expert_count * capacity
    hbm = pl.BlockSpec(memory_space=pl.ANY)
    return pl.pallas_call(
        functools.partial(dispatch_kernel, capacity, groups),
        in_specs=[hbm, hbm, hbm, hbm],
        out_specs=(hbm, hbm),
        out_shape=(
            jax.ShapeDtypeStruct((places, width + hidden), BF16),
            jax.ShapeDtypeStruct((1, row_count), jnp.int32),
        ),
        scratch_shapes=[
            pltpu.VMEM((1, row_count), jnp.int32),
            pltpu.VMEM((1, expert_count), jnp.int32),
            pltpu.VMEM((1, row_count), jnp.int32),
            pltpu.VMEM((row_count, hidden), BF16),
            pltpu.VMEM((row_count, width), BF16),
            pltpu.VMEM((places, width + hidden), BF16),
            pltpu.SemaphoreType.DMA((3,)),
            pltpu.SemaphoreType.DMA((parts + 1,)),
            pltpu.SemaphoreType.DMA((tiles + 1,)),
        ],
        compiler_params=pltpu.CompilerParams(vmem_limit_bytes=LARGE_LIMIT),
        cost_estimate=cost(
            2 * places * row_count * (hidden + width), 2 * (places + row_count) * (hidden + width)
        ),
        name="dispatch",
    )(route.reshape(1, row_count), placement.reshape(1, -1), x_rows, y_cot)


def hidden_specs(rows, hidden, width):
    return [
        pl.BlockSpec((rows, BLOCK), functools.partial(lambda k, j: (0, k), width // BLOCK + i))
        for i in range(hidden // BLOCK)
    ]


def read_columns(refs):
    return jnp.concatenate([ref[...] for ref in refs], axis=1)


def collect_kernel(
    target_hbm, home_ref, y_hbm, dx_hbm, target_ref, y_ref, dx_ref, target_sem, out_sems
):
    hidden = dx_ref.shape[1]
    width = y_ref.shape[1]
    tiles = out_sems.shape[0] - 1
    tile = width // tiles
    spans = [pl.ds(j * tile, tile) for j in range(tiles)] + [pl.ds(width, hidden)]
    target_load = pltpu.make_async_copy(target_hbm, target_ref, target_sem)
    target_load.start()
    target_load.wait()
    target = target_ref[...]
    slots = lax.broadcasted_iota(jnp.int32, (home_ref.shape[0], target.shape[1]), 0)
    places = (slots == target).astype(F32).T.astype(BF16)
    stores = []
    for j, span in enumerate(spans):
        rows = jnp.dot(places, home_ref[:, span], preferred_element_type=F32).astype(BF16)
        if j < tiles:
            y_ref[:, span] = rows
            store = pltpu.make_async_copy(y_ref.at[:, span], y_hbm.at[:, span], out_sems.at[j])
        else:
            dx_ref[...] = rows
            store = pltpu.make_async_copy(dx_ref, dx_hbm, out_sems.at[j])
        store.start()
        stores.append(store)
    for store in stores:
        store.wait()


def collect(target, home, hidden):
    total, width = home.shape
    width -= hidden
    row_count = target.shape[1]
    tiles = width // min(width, 512)
    hbm = pl.BlockSpec(memory_space=pl.ANY)
    return pl.pallas_call(
        collect_kernel,
        in_specs=[hbm, pl.BlockSpec(memory_space=pltpu.VMEM)],
        out_specs=(hbm, hbm),
        out_shape=(
            jax.ShapeDtypeStruct((row_count, width), BF16),
            jax.ShapeDtypeStruct((row_count, hidden), BF16),
        ),
        scratch_shapes=[
            pltpu.VMEM(target.shape, jnp.int32),
            pltpu.VMEM((row_count, width), BF16),
            pltpu.VMEM((row_count, hidden), BF16),
            pltpu.SemaphoreType.DMA,
            pltpu.SemaphoreType.DMA((tiles + 1,)),
        ],
        compiler_params=params(),
        cost_estimate=cost(
            2 * total * row_count * (hidden + width), 2 * (total + row_count) * (hidden + width)
        ),
        name="collect",
    )(target, home)


def member_rows(rows, capacity, local_count):
    index = lax.broadcasted_iota(jnp.int32, (rows, 1), 0)
    return lax.rem(index, capacity * local_count) // capacity


def spread(x, capacity, local_count):
    member = member_rows(x.shape[0], capacity, local_count)
    zero = jnp.zeros_like(x)
    return jnp.concatenate([jnp.where(member == e, x, zero) for e in range(local_count)], axis=1)


def join_kernel(*refs):
    piece_refs, out_ref = refs[:-1], refs[-1]
    pieces = len(piece_refs)
    here = lax.axis_index("rep") if pieces > 1 else 0
    for i, ref in enumerate(piece_refs):
        owner = jnp.bitwise_xor(here, i) if pieces > 1 else 0
        for e in range(out_ref.shape[1]):
            out_ref[0, e, owner] = ref[e]


def join_weight(weight):
    local_count, rows, width = weight[0].shape
    pieces = len(weight)
    tile = min(width, 512)
    tiles = width // tile
    joined = pl.pallas_call(
        join_kernel,
        grid=(tiles,),
        in_specs=[pl.BlockSpec((local_count, rows, tile), lambda j: (0, 0, j))] * pieces,
        out_specs=pl.BlockSpec((1, local_count, pieces, rows, tile), lambda j: (j, 0, 0, 0, 0)),
        out_shape=jax.ShapeDtypeStruct((tiles, local_count, pieces, rows, tile), BF16),
        compiler_params=pltpu.CompilerParams(
            vmem_limit_bytes=LARGE_LIMIT, dimension_semantics=("arbitrary",)
        ),
        cost_estimate=cost(0, 4 * local_count * pieces * rows * width),
        name="join_weight",
    )(*weight)
    return joined.reshape(tiles, local_count * pieces * rows, tile)


def products_kernel(
    capacity, local_count, local_hbm, w_hbm, out_hbm,
    local_ref, w_ref, wide_ref, total_ref, out_ref, local_sem, w_sems, out_sems,
):
    step = pl.program_id(0)
    steps, _, tile = w_ref.shape
    hidden = wide_ref.shape[1] // local_count
    columns = pl.ds(pl.multiple_of(step * tile, tile), tile)

    def weight_load(j):
        return pltpu.make_async_copy(w_hbm.at[j], w_ref.at[j], w_sems.at[j])

    @pl.when(step == 0)
    def _():
        local_load = pltpu.make_async_copy(local_hbm, local_ref, local_sem)
        local_load.start()
        weight_load(0).start()
        total_ref[...] = jnp.zeros_like(total_ref)
        local_load.wait()
        for j in range(1, steps):
            weight_load(j).start()
        wide_ref[...] = spread(local_ref[:, steps * tile :], capacity, local_count)

    weight_load(step).wait()
    weight = w_ref[step]
    out_ref[:, columns] = jnp.dot(
        wide_ref[...], weight, preferred_element_type=F32
    ).astype(BF16)
    pltpu.make_async_copy(
        out_ref.at[:, columns], out_hbm.at[:, columns], out_sems.at[step]
    ).start()
    total_ref[...] += lax.dot_general(
        local_ref[:, columns], weight, (((1,), (1,)), ((), ())), preferred_element_type=F32
    )

    @pl.when(step == steps - 1)
    def _():
        member = member_rows(total_ref.shape[0], capacity, local_count)
        picked = total_ref[:, :hidden]
        for e in range(1, local_count):
            picked = jnp.where(member == e, total_ref[:, e * hidden : (e + 1) * hidden], picked)
        last = pl.ds(steps * tile, hidden)
        out_ref[:, last] = picked.astype(BF16)
        final = pltpu.make_async_copy(out_ref.at[:, last], out_hbm.at[:, last], out_sems.at[steps])
        final.start()
        for j in range(steps):
            span = pl.ds(j * tile, tile)
            pltpu.make_async_copy(out_ref.at[:, span], out_hbm.at[:, span], out_sems.at[j]).wait()
        final.wait()


def products(local, weight, capacity, local_count):
    tiles, wide, tile = weight.shape
    width = tiles * tile
    total = local.shape[0]
    hbm = pl.BlockSpec(memory_space=pl.ANY)
    return pl.pallas_call(
        functools.partial(products_kernel, capacity, local_count),
        grid=(tiles,),
        in_specs=[hbm, hbm],
        out_specs=hbm,
        out_shape=jax.ShapeDtypeStruct(local.shape, BF16),
        scratch_shapes=[
            pltpu.VMEM(local.shape, BF16),
            pltpu.VMEM(weight.shape, BF16),
            pltpu.VMEM((total, wide), BF16),
            pltpu.VMEM((total, wide), F32),
            pltpu.VMEM(local.shape, BF16),
            pltpu.SemaphoreType.DMA,
            pltpu.SemaphoreType.DMA((tiles,)),
            pltpu.SemaphoreType.DMA((tiles + 1,)),
        ],
        compiler_params=pltpu.CompilerParams(
            vmem_limit_bytes=LARGE_LIMIT, dimension_semantics=("arbitrary",)
        ),
        cost_estimate=cost(4 * total * wide * width, 2 * (wide + 2 * total) * width),
        name="products",
    )(local, weight)


def gradient_kernel(capacity, local_count, parts, factor, g_ref, *refs):
    blocks = len(refs) - 2 - (parts if parts > 1 else 0)
    x_refs, wide_ref = refs[:blocks], refs[-1]
    out_refs = refs[blocks:-2] if parts > 1 else refs[blocks:-1]

    @pl.when(pl.program_id(0) == 0)
    def _():
        wide_ref[...] = spread(read_columns(x_refs), capacity, local_count)

    outer = lax.dot_general(
        wide_ref[...], g_ref[...], (((0,), (0,)), ((), ())), preferred_element_type=F32
    )
    low = (outer * factor).astype(BF16)
    if parts == 1:
        out_refs[0][...] = low.reshape(out_refs[0].shape)
        return
    split_ref = refs[-2]
    split_ref[...] = low.reshape(split_ref.shape)
    here = lax.axis_index("rep")
    for i, out_ref in enumerate(out_refs):
        owner = jnp.bitwise_xor(here, i)
        for e in range(local_count):
            out_ref[e] = split_ref[e, owner]


def gradient(local, hidden, capacity, local_count, parts, factor):
    total, width = local.shape
    width -= hidden
    tile = min(width, 512)
    slice_rows = hidden // parts
    specs = hidden_specs(total, hidden, width)
    split = [pltpu.VMEM((local_count, parts, slice_rows, tile), BF16)] if parts > 1 else []
    return list(pl.pallas_call(
        functools.partial(gradient_kernel, capacity, local_count, parts, factor),
        grid=(width // tile,),
        in_specs=[pl.BlockSpec((total, tile), lambda j: (0, j))] + specs,
        out_specs=(pl.BlockSpec((local_count, slice_rows, tile), lambda j: (0, 0, j)),) * parts,
        out_shape=(jax.ShapeDtypeStruct((local_count, slice_rows, width), BF16),) * parts,
        scratch_shapes=split + [pltpu.VMEM((total, local_count * hidden), BF16)],
        compiler_params=pltpu.CompilerParams(
            vmem_limit_bytes=LARGE_LIMIT, dimension_semantics=("arbitrary",)
        ),
        cost_estimate=cost(
            2 * total * local_count * hidden * width,
            2 * (local_count * hidden + total) * width,
        ),
        name="gradient",
    )(*([local] * (1 + len(specs)))))


def cast_kernel(w_ref, out_ref):
    out_ref[...] = w_ref[...].astype(BF16)


def cast_weight(weight):
    members, rows, width = weight.shape
    tile = min(width, 512)
    spec = pl.BlockSpec((members, rows, tile), lambda j: (0, 0, j))
    return pl.pallas_call(
        cast_kernel,
        grid=(width // tile,),
        in_specs=[spec],
        out_specs=spec,
        out_shape=jax.ShapeDtypeStruct(weight.shape, BF16),
        compiler_params=params("arbitrary"),
        cost_estimate=cost(weight.size, 6 * weight.size),
        name="cast_weight",
    )(weight)


def add_kernel(a_ref, b_ref, out_ref):
    out_ref[...] = (a_ref[...].astype(F32) + b_ref[...].astype(F32)).astype(BF16)


def add_parts(a, b):
    members, rows, width = a.shape
    tile = min(width, 1024)
    spec = pl.BlockSpec((members, rows, tile), lambda j: (0, 0, j))
    return pl.pallas_call(
        add_kernel,
        grid=(width // tile,),
        in_specs=[spec, spec],
        out_specs=spec,
        out_shape=jax.ShapeDtypeStruct(a.shape, BF16),
        compiler_params=params("arbitrary"),
        cost_estimate=cost(a.size, 6 * a.size),
        name="add_parts",
    )(a, b)


def adam_kernel(
    parts, master_ref, mc_ref, ms_ref, vc_ref, vs_ref, *refs
):
    grad_refs = refs[:parts]
    master_out, mc_out, ms_out, vc_out, vs_out = refs[parts:]
    blocks = ms_ref.shape[1]
    rows = ms_ref.shape[2]
    corr_one = 1.0 - beta_one**ADAM_STEP
    corr_two = 1.0 - beta_two**ADAM_STEP
    m_scales = (ms_ref[0] * beta_one).T
    v_scales = (vs_ref[0] * beta_two).T
    lane = lax.broadcasted_iota(jnp.int32, (rows, blocks), 1)
    m_tops = jnp.zeros((rows, blocks), F32)
    v_tops = jnp.zeros((rows, blocks), F32)
    for b in range(blocks):
        cols = slice(b * BLOCK, (b + 1) * BLOCK)
        grad = grad_refs[0][0, :, cols].astype(F32)
        for ref in grad_refs[1:]:
            grad = grad + ref[0, :, cols].astype(F32)
        m_next = mc_ref[0, :, cols].astype(F32) * m_scales[:, b : b + 1] + (1.0 - beta_one) * grad
        v_next = vc_ref[0, :, cols].astype(F32) * v_scales[:, b : b + 1] + (
            1.0 - beta_two
        ) * (grad * grad)
        v_hat = v_next * (1.0 / corr_two)
        root = v_hat * lax.rsqrt(v_hat) + 1e-08
        master_out[0, :, cols] = master_ref[0, :, cols] - (learn_rate / corr_one) * m_next / root
        m_top = jnp.max(jnp.abs(m_next), axis=-1, keepdims=True) + 1e-06
        v_top = jnp.max(v_next, axis=-1, keepdims=True) + 1e-06
        mc_out[0, :, cols] = (m_next * (1.0 / m_top)).astype(BF16)
        vc_out[0, :, cols] = (v_next * (1.0 / v_top)).astype(BF16)
        m_tops = jnp.where(lane == b, m_top, m_tops)
        v_tops = jnp.where(lane == b, v_top, v_tops)
    ms_out[0] = m_tops.T
    vs_out[0] = v_tops.T


def adam(master_weight, grads, m_code, m_scale, v_code, v_scale):
    members, rows, width = master_weight.shape
    blocks = m_scale.shape[-1]
    count = 8 if blocks % 8 == 0 else blocks
    big = pl.BlockSpec((1, rows, count * BLOCK), lambda e, j: (e, 0, j))
    small = pl.BlockSpec((1, count, rows), lambda e, j: (e, j, 0))
    scales = jax.ShapeDtypeStruct((members, blocks, rows), F32)
    master_next, m_code_next, m_scale_next, v_code_next, v_scale_next = pl.pallas_call(
        functools.partial(adam_kernel, len(grads)),
        grid=(members, blocks // count),
        in_specs=[big, big, small, big, small] + [big] * len(grads),
        out_specs=(big, big, small, big, small),
        out_shape=(
            jax.ShapeDtypeStruct(master_weight.shape, F32),
            jax.ShapeDtypeStruct(master_weight.shape, BF16),
            scales,
            jax.ShapeDtypeStruct(master_weight.shape, BF16),
            scales,
        ),
        compiler_params=params("arbitrary", "arbitrary"),
        cost_estimate=cost(40 * master_weight.size, 18 * master_weight.size),
        name="adam",
    )(master_weight, m_code, jnp.swapaxes(m_scale, 1, 2), v_code, jnp.swapaxes(v_scale, 1, 2), *grads)
    return (
        master_next,
        m_code_next,
        jnp.swapaxes(m_scale_next, 1, 2),
        v_code_next,
        jnp.swapaxes(v_scale_next, 1, 2),
    )


def swap(array, axis, offset):
    size = lax.axis_size(axis)
    return lax.ppermute(array, axis, [(i, i ^ offset) for i in range(size)])


def exchange(buffer, groups):
    places, width = buffer.shape
    parts = buffer.reshape(groups, places // groups, width)
    members = sorted(range(groups), key=lambda device: order_of(device, groups))
    moved = lax.all_to_all(
        parts, "grp", split_axis=0, concat_axis=0, tiled=True, axis_index_groups=[members]
    )
    return moved.reshape(places, width)


def gather_weight(weight_slice, replicas):
    if replicas != 4:
        return [lax.all_gather(weight_slice, "rep", axis=1, tiled=True)]
    far = swap(weight_slice, "rep", 2)
    near = swap(weight_slice, "rep", 1)
    return [weight_slice, near, far, swap(far, "rep", 1)]


def sum_gradient(parts):
    if len(parts) != 4:
        return [lax.psum_scatter(parts[0], "rep", scatter_dimension=1, tiled=True)]
    far = swap(parts[3], "rep", 1)
    near = swap(parts[1], "rep", 1)
    return [parts[0], near, swap(add_parts(parts[2], far), "rep", 2)]


def per_device(master_weight, m_code, m_scale, v_code, v_scale, placement, route, x_rows, y_cot):
    local_count = master_weight.shape[0]
    row_count = x_rows.shape[0]
    expert_count = placement.shape[0]
    groups = lax.axis_size("grp")
    replicas = lax.axis_size("rep")
    grad_factor = float(row_count * groups * replicas // expert_count) ** (-0.5)
    capacity = max(2, (3 * row_count + 2 * expert_count - 1) // (2 * expert_count))
    places = expert_count * capacity
    sent, target = dispatch(route, placement, x_rows, y_cot, capacity, groups)
    local = exchange(sent, groups)
    early_master, target = lax.optimization_barrier((master_weight, target))
    weight = join_weight(gather_weight(cast_weight(early_master), replicas))
    results = products(local, weight, capacity, local_count)
    local, results = lax.optimization_barrier((local, results))
    home = exchange(results, groups)

    parts = replicas if replicas == 4 else 1
    hidden = x_rows.shape[1]
    grads = sum_gradient(gradient(local, hidden, capacity, local_count, parts, grad_factor))
    updated = adam(master_weight, grads, m_code, m_scale, v_code, v_scale)
    y_rows, x_grad = collect(target, home, hidden)
    return (y_rows, x_grad) + tuple(updated)


def solution(mesh):
    return jax.shard_map(
        per_device,
        mesh=mesh,
        in_specs=(
            P("grp", "rep", None),
            P("grp", "rep", None),
            P("grp", "rep", None),
            P("grp", "rep", None),
            P("grp", "rep", None),
            P(),
            P(("rep", "grp")),
            P(("rep", "grp"), None),
            P(("rep", "grp"), None),
        ),
        out_specs=(
            P(("rep", "grp"), None),
            P(("rep", "grp"), None),
            P("grp", "rep", None),
            P("grp", "rep", None),
            P("grp", "rep", None),
            P("grp", "rep", None),
            P("grp", "rep", None),
        ),
        check_vma=False,
    )
```

```python
import functools

import jax
import jax.numpy as jnp
from jax import lax
from jax.experimental import pallas as pl
from jax.experimental.pallas import tpu as pltpu
from jax.sharding import PartitionSpec as P

BLOCK = 128
ADAM_STEP = 100

beta_one = 0.9
beta_two = 0.95
learn_rate = 0.01

VMEM_LIMIT = 40 * 1024 * 1024
LARGE_LIMIT = 60 * 1024 * 1024 + 512 * 1024
F32 = jnp.float32
BF16 = jnp.bfloat16


def cost(flops, nbytes):
    return pl.CostEstimate(flops=int(flops), bytes_accessed=int(nbytes), transcendentals=0)


def params(*semantics):
    if semantics:
        return pltpu.CompilerParams(vmem_limit_bytes=VMEM_LIMIT, dimension_semantics=semantics)
    return pltpu.CompilerParams(vmem_limit_bytes=VMEM_LIMIT)


def order_of(device, groups):
    if groups % 2:
        return device
    half = groups // 2
    return device % half * 2 + device // half


def row_targets(route_row, placement_row, capacity, groups):
    expert_count = placement_row.shape[1]
    row_count = route_row.shape[1]
    diagonal = lax.broadcasted_iota(jnp.int32, (expert_count, expert_count), 0) == (
        lax.broadcasted_iota(jnp.int32, (expert_count, expert_count), 1)
    )
    placement_col = jnp.sum(
        jnp.where(diagonal, placement_row, 0).astype(F32), axis=1, keepdims=True
    )
    hot = (placement_col == route_row.astype(F32)).astype(F32)
    earlier = lax.broadcasted_iota(jnp.int32, (row_count, row_count), 0)
    later = lax.broadcasted_iota(jnp.int32, (row_count, row_count), 1)
    before = (earlier < later).astype(F32).astype(BF16)
    position = jnp.dot(hot.astype(BF16), before, preferred_element_type=F32)
    slot = lax.broadcasted_iota(jnp.int32, (expert_count, row_count), 0)
    local_count = expert_count // groups
    order = order_of(slot // local_count, groups)
    start = ((order * local_count + slot % local_count) * capacity).astype(F32)
    return jnp.sum(hot * (start + position), axis=0, keepdims=True).astype(jnp.int32)


def place_matrix(target, places):
    slots = lax.broadcasted_iota(jnp.int32, (places, target.shape[1]), 0)
    return (slots == target).astype(F32).astype(BF16)


def dispatch_kernel(
    capacity, groups, route_hbm, placement_hbm, x_hbm, g_hbm, sent_hbm, target_hbm,
    route_ref, placement_ref, target_ref, x_ref, g_ref, sent_ref, key_sems, in_sems, out_sems,
):
    row_count, hidden = x_ref.shape
    width = g_ref.shape[1]
    tiles = out_sems.shape[0] - 1
    tile = width // tiles
    parts = in_sems.shape[0] - 1
    keys = [
        pltpu.make_async_copy(route_hbm, route_ref, key_sems.at[0]),
        pltpu.make_async_copy(placement_hbm, placement_ref, key_sems.at[1]),
    ]
    bands = [pl.ds(i * (row_count // parts), row_count // parts) for i in range(parts)]
    loads = [pltpu.make_async_copy(x_hbm, x_ref, in_sems.at[parts])] + [
        pltpu.make_async_copy(g_hbm.at[band], g_ref.at[band], in_sems.at[i])
        for i, band in enumerate(bands)
    ]
    for load in keys + loads:
        load.start()
    for load in keys:
        load.wait()
    target = row_targets(route_ref[...], placement_ref[...], capacity, groups)
    target_ref[...] = target
    stores = [pltpu.make_async_copy(target_ref, target_hbm, key_sems.at[2])]
    stores[0].start()
    places = place_matrix(target, sent_ref.shape[0])
    for j in range(tiles + 1):
        for load in loads[:1] if j == 0 else loads[1:] if j == 1 else []:
            load.wait()
        columns = pl.ds((j - 1) * tile, tile) if j else pl.ds(width, hidden)
        rows = g_ref[:, columns] if j else x_ref[...]
        sent_ref[:, columns] = jnp.dot(places, rows, preferred_element_type=F32).astype(BF16)
        store = pltpu.make_async_copy(
            sent_ref.at[:, columns], sent_hbm.at[:, columns], out_sems.at[j]
        )
        store.start()
        stores.append(store)
    for store in stores:
        store.wait()


def dispatch(route, placement, x_rows, y_cot, capacity, groups):
    row_count, hidden = x_rows.shape
    width = y_cot.shape[1]
    expert_count = placement.shape[0]
    tile = min(width, 512)
    tiles = width // tile
    parts = 4 if row_count % 64 == 0 else 1
    places = expert_count * capacity
    hbm = pl.BlockSpec(memory_space=pl.ANY)
    return pl.pallas_call(
        functools.partial(dispatch_kernel, capacity, groups),
        in_specs=[hbm, hbm, hbm, hbm],
        out_specs=(hbm, hbm),
        out_shape=(
            jax.ShapeDtypeStruct((places, width + hidden), BF16),
            jax.ShapeDtypeStruct((1, row_count), jnp.int32),
        ),
        scratch_shapes=[
            pltpu.VMEM((1, row_count), jnp.int32),
            pltpu.VMEM((1, expert_count), jnp.int32),
            pltpu.VMEM((1, row_count), jnp.int32),
            pltpu.VMEM((row_count, hidden), BF16),
            pltpu.VMEM((row_count, width), BF16),
            pltpu.VMEM((places, width + hidden), BF16),
            pltpu.SemaphoreType.DMA((3,)),
            pltpu.SemaphoreType.DMA((parts + 1,)),
            pltpu.SemaphoreType.DMA((tiles + 1,)),
        ],
        compiler_params=pltpu.CompilerParams(vmem_limit_bytes=LARGE_LIMIT),
        cost_estimate=cost(
            2 * places * row_count * (hidden + width), 2 * (places + row_count) * (hidden + width)
        ),
        name="dispatch",
    )(route.reshape(1, row_count), placement.reshape(1, -1), x_rows, y_cot)


def hidden_specs(rows, hidden, width):
    return [
        pl.BlockSpec((rows, BLOCK), functools.partial(lambda k, j: (0, k), width // BLOCK + i))
        for i in range(hidden // BLOCK)
    ]


def read_columns(refs):
    return jnp.concatenate([ref[...] for ref in refs], axis=1)


def collect_kernel(
    target_hbm, home_ref, y_hbm, dx_hbm, target_ref, y_ref, dx_ref, target_sem, out_sems
):
    hidden = dx_ref.shape[1]
    width = y_ref.shape[1]
    tiles = out_sems.shape[0] - 1
    tile = width // tiles
    spans = [pl.ds(j * tile, tile) for j in range(tiles)] + [pl.ds(width, hidden)]
    target_load = pltpu.make_async_copy(target_hbm, target_ref, target_sem)
    target_load.start()
    target_load.wait()
    target = target_ref[...]
    slots = lax.broadcasted_iota(jnp.int32, (home_ref.shape[0], target.shape[1]), 0)
    places = (slots == target).astype(F32).T.astype(BF16)
    stores = []
    for j, span in enumerate(spans):
        rows = jnp.dot(places, home_ref[:, span], preferred_element_type=F32).astype(BF16)
        if j < tiles:
            y_ref[:, span] = rows
            store = pltpu.make_async_copy(y_ref.at[:, span], y_hbm.at[:, span], out_sems.at[j])
        else:
            dx_ref[...] = rows
            store = pltpu.make_async_copy(dx_ref, dx_hbm, out_sems.at[j])
        store.start()
        stores.append(store)
    for store in stores:
        store.wait()


def collect(target, home, hidden):
    total, width = home.shape
    width -= hidden
    row_count = target.shape[1]
    tiles = width // min(width, 512)
    hbm = pl.BlockSpec(memory_space=pl.ANY)
    return pl.pallas_call(
        collect_kernel,
        in_specs=[hbm, pl.BlockSpec(memory_space=pltpu.VMEM)],
        out_specs=(hbm, hbm),
        out_shape=(
            jax.ShapeDtypeStruct((row_count, width), BF16),
            jax.ShapeDtypeStruct((row_count, hidden), BF16),
        ),
        scratch_shapes=[
            pltpu.VMEM(target.shape, jnp.int32),
            pltpu.VMEM((row_count, width), BF16),
            pltpu.VMEM((row_count, hidden), BF16),
            pltpu.SemaphoreType.DMA,
            pltpu.SemaphoreType.DMA((tiles + 1,)),
        ],
        compiler_params=params(),
        cost_estimate=cost(
            2 * total * row_count * (hidden + width), 2 * (total + row_count) * (hidden + width)
        ),
        name="collect",
    )(target, home)


def member_rows(rows, capacity, local_count):
    index = lax.broadcasted_iota(jnp.int32, (rows, 1), 0)
    return lax.rem(index, capacity * local_count) // capacity


def spread(x, capacity, local_count):
    member = member_rows(x.shape[0], capacity, local_count)
    zero = jnp.zeros_like(x)
    return jnp.concatenate([jnp.where(member == e, x, zero) for e in range(local_count)], axis=1)


def join_kernel(*refs):
    piece_refs, out_ref = refs[:-1], refs[-1]
    pieces = len(piece_refs)
    here = lax.axis_index("rep") if pieces > 1 else 0
    for i, ref in enumerate(piece_refs):
        owner = jnp.bitwise_xor(here, i) if pieces > 1 else 0
        for e in range(out_ref.shape[1]):
            out_ref[0, e, owner] = ref[e]


def join_weight(weight):
    local_count, rows, width = weight[0].shape
    pieces = len(weight)
    tile = min(width, 512)
    tiles = width // tile
    joined = pl.pallas_call(
        join_kernel,
        grid=(tiles,),
        in_specs=[pl.BlockSpec((local_count, rows, tile), lambda j: (0, 0, j))] * pieces,
        out_specs=pl.BlockSpec((1, local_count, pieces, rows, tile), lambda j: (j, 0, 0, 0, 0)),
        out_shape=jax.ShapeDtypeStruct((tiles, local_count, pieces, rows, tile), BF16),
        compiler_params=pltpu.CompilerParams(
            vmem_limit_bytes=LARGE_LIMIT, dimension_semantics=("arbitrary",)
        ),
        cost_estimate=cost(0, 4 * local_count * pieces * rows * width),
        name="join_weight",
    )(*weight)
    return joined.reshape(tiles, local_count * pieces * rows, tile)


def member_parts(value, capacity, local_count):
    rows, width = value.shape
    groups = rows // (capacity * local_count)
    parts = value.astype(F32).reshape(groups, local_count, capacity, width)
    return [
        parts[:, e].reshape(groups * capacity, width).astype(BF16) for e in range(local_count)
    ]


def join_members(parts, capacity):
    groups = parts[0].shape[0] // capacity
    width = parts[0].shape[1]
    stacked = [part.reshape(groups, 1, capacity, width) for part in parts]
    joined = jnp.concatenate(stacked, axis=1)
    return joined.reshape(groups * len(parts) * capacity, width)


def pick_members(totals, capacity):
    member = member_rows(totals[0].shape[0], capacity, len(totals))
    picked = totals[0]
    for e in range(1, len(totals)):
        picked = jnp.where(member == e, totals[e], picked)
    return picked


def products_kernel(
    capacity, apart, local_hbm, w_hbm, out_hbm,
    local_ref, w_ref, x_ref, total_ref, out_ref, local_sem, w_sems, out_sems,
):
    step = pl.program_id(0)
    steps, _, tile = w_ref.shape
    local_count, _, hidden = total_ref.shape
    columns = pl.ds(pl.multiple_of(step * tile, tile), tile)

    def weight_load(j):
        return pltpu.make_async_copy(w_hbm.at[j], w_ref.at[j], w_sems.at[j])

    @pl.when(step == 0)
    def _():
        local_load = pltpu.make_async_copy(local_hbm, local_ref, local_sem)
        local_load.start()
        weight_load(0).start()
        total_ref[...] = jnp.zeros_like(total_ref)
        local_load.wait()
        for j in range(1, steps):
            weight_load(j).start()
        x = local_ref[:, steps * tile :]
        for e, part in enumerate(member_parts(x, capacity, local_count) if apart else [x]):
            x_ref[e] = part

    weight_load(step).wait()
    weights = [w_ref[step, e * hidden : (e + 1) * hidden] for e in range(local_count)]
    xs = [x_ref[e if apart else 0] for e in range(local_count)]
    ys = [jnp.dot(x, w, preferred_element_type=F32) for x, w in zip(xs, weights)]
    y = join_members(ys, capacity) if apart else pick_members(ys, capacity)
    out_ref[:, columns] = y.astype(BF16)
    pltpu.make_async_copy(
        out_ref.at[:, columns], out_hbm.at[:, columns], out_sems.at[step]
    ).start()
    g = local_ref[:, columns]
    gs = member_parts(g, capacity, local_count) if apart else [g] * local_count
    for e in range(local_count):
        total_ref[e] += lax.dot_general(
            gs[e], weights[e], (((1,), (1,)), ((), ())), preferred_element_type=F32
        )

    @pl.when(step == steps - 1)
    def _():
        totals = [total_ref[e] for e in range(local_count)]
        dx = join_members(totals, capacity) if apart else pick_members(totals, capacity)
        last = pl.ds(steps * tile, hidden)
        out_ref[:, last] = dx.astype(BF16)
        final = pltpu.make_async_copy(out_ref.at[:, last], out_hbm.at[:, last], out_sems.at[steps])
        final.start()
        for j in range(steps):
            span = pl.ds(j * tile, tile)
            pltpu.make_async_copy(out_ref.at[:, span], out_hbm.at[:, span], out_sems.at[j]).wait()
        final.wait()


def products(local, weight, capacity, local_count):
    tiles, wide, tile = weight.shape
    width = tiles * tile
    total = local.shape[0]
    hidden = wide // local_count
    apart = capacity % 8 == 0
    rows = total // local_count if apart else total
    hbm = pl.BlockSpec(memory_space=pl.ANY)
    return pl.pallas_call(
        functools.partial(products_kernel, capacity, apart),
        grid=(tiles,),
        in_specs=[hbm, hbm],
        out_specs=hbm,
        out_shape=jax.ShapeDtypeStruct(local.shape, BF16),
        scratch_shapes=[
            pltpu.VMEM(local.shape, BF16),
            pltpu.VMEM(weight.shape, BF16),
            pltpu.VMEM((local_count if apart else 1, rows, hidden), BF16),
            pltpu.VMEM((local_count, rows, hidden), F32),
            pltpu.VMEM(local.shape, BF16),
            pltpu.SemaphoreType.DMA,
            pltpu.SemaphoreType.DMA((tiles,)),
            pltpu.SemaphoreType.DMA((tiles + 1,)),
        ],
        compiler_params=pltpu.CompilerParams(
            vmem_limit_bytes=LARGE_LIMIT, dimension_semantics=("arbitrary",)
        ),
        cost_estimate=cost(4 * rows * wide * width, 2 * (wide + 2 * total) * width),
        name="products",
    )(local, weight)


def gradient_kernel(capacity, local_count, parts, factor, g_ref, *refs):
    blocks = len(refs) - 2 - (parts if parts > 1 else 0)
    x_refs, wide_ref = refs[:blocks], refs[-1]
    out_refs = refs[blocks:-2] if parts > 1 else refs[blocks:-1]

    @pl.when(pl.program_id(0) == 0)
    def _():
        wide_ref[...] = spread(read_columns(x_refs), capacity, local_count)

    outer = lax.dot_general(
        wide_ref[...], g_ref[...], (((0,), (0,)), ((), ())), preferred_element_type=F32
    )
    low = (outer * factor).astype(BF16)
    if parts == 1:
        out_refs[0][...] = low.reshape(out_refs[0].shape)
        return
    split_ref = refs[-2]
    split_ref[...] = low.reshape(split_ref.shape)
    here = lax.axis_index("rep")
    for i, out_ref in enumerate(out_refs):
        owner = jnp.bitwise_xor(here, i)
        for e in range(local_count):
            out_ref[e] = split_ref[e, owner]


def gradient(local, hidden, capacity, local_count, parts, factor):
    total, width = local.shape
    width -= hidden
    tile = min(width, 512)
    slice_rows = hidden // parts
    specs = hidden_specs(total, hidden, width)
    split = [pltpu.VMEM((local_count, parts, slice_rows, tile), BF16)] if parts > 1 else []
    return list(pl.pallas_call(
        functools.partial(gradient_kernel, capacity, local_count, parts, factor),
        grid=(width // tile,),
        in_specs=[pl.BlockSpec((total, tile), lambda j: (0, j))] + specs,
        out_specs=(pl.BlockSpec((local_count, slice_rows, tile), lambda j: (0, 0, j)),) * parts,
        out_shape=(jax.ShapeDtypeStruct((local_count, slice_rows, width), BF16),) * parts,
        scratch_shapes=split + [pltpu.VMEM((total, local_count * hidden), BF16)],
        compiler_params=pltpu.CompilerParams(
            vmem_limit_bytes=LARGE_LIMIT, dimension_semantics=("arbitrary",)
        ),
        cost_estimate=cost(
            2 * total * local_count * hidden * width,
            2 * (local_count * hidden + total) * width,
        ),
        name="gradient",
    )(*([local] * (1 + len(specs)))))


def cast_kernel(w_ref, out_ref):
    out_ref[...] = w_ref[...].astype(BF16)


def cast_weight(weight):
    members, rows, width = weight.shape
    tile = min(width, 512)
    spec = pl.BlockSpec((members, rows, tile), lambda j: (0, 0, j))
    return pl.pallas_call(
        cast_kernel,
        grid=(width // tile,),
        in_specs=[spec],
        out_specs=spec,
        out_shape=jax.ShapeDtypeStruct(weight.shape, BF16),
        compiler_params=params("arbitrary"),
        cost_estimate=cost(weight.size, 6 * weight.size),
        name="cast_weight",
    )(weight)


def add_kernel(a_ref, b_ref, out_ref):
    out_ref[...] = (a_ref[...].astype(F32) + b_ref[...].astype(F32)).astype(BF16)


def add_parts(a, b):
    members, rows, width = a.shape
    tile = min(width, 1024)
    spec = pl.BlockSpec((members, rows, tile), lambda j: (0, 0, j))
    return pl.pallas_call(
        add_kernel,
        grid=(width // tile,),
        in_specs=[spec, spec],
        out_specs=spec,
        out_shape=jax.ShapeDtypeStruct(a.shape, BF16),
        compiler_params=params("arbitrary"),
        cost_estimate=cost(a.size, 6 * a.size),
        name="add_parts",
    )(a, b)


def adam_kernel(
    parts, master_ref, mc_ref, ms_ref, vc_ref, vs_ref, *refs
):
    grad_refs = refs[:parts]
    master_out, mc_out, ms_out, vc_out, vs_out = refs[parts:]
    blocks = ms_ref.shape[1]
    rows = ms_ref.shape[2]
    corr_one = 1.0 - beta_one**ADAM_STEP
    corr_two = 1.0 - beta_two**ADAM_STEP
    m_scales = (ms_ref[0] * beta_one).T
    v_scales = (vs_ref[0] * beta_two).T
    lane = lax.broadcasted_iota(jnp.int32, (rows, blocks), 1)
    m_tops = jnp.zeros((rows, blocks), F32)
    v_tops = jnp.zeros((rows, blocks), F32)
    for b in range(blocks):
        cols = slice(b * BLOCK, (b + 1) * BLOCK)
        grad = grad_refs[0][0, :, cols].astype(F32)
        for ref in grad_refs[1:]:
            grad = grad + ref[0, :, cols].astype(F32)
        m_next = mc_ref[0, :, cols].astype(F32) * m_scales[:, b : b + 1] + (1.0 - beta_one) * grad
        v_next = vc_ref[0, :, cols].astype(F32) * v_scales[:, b : b + 1] + (
            1.0 - beta_two
        ) * (grad * grad)
        v_hat = v_next * (1.0 / corr_two)
        root = v_hat * lax.rsqrt(v_hat) + 1e-08
        master_out[0, :, cols] = master_ref[0, :, cols] - (learn_rate / corr_one) * m_next / root
        m_top = jnp.max(jnp.abs(m_next), axis=-1, keepdims=True) + 1e-06
        v_top = jnp.max(v_next, axis=-1, keepdims=True) + 1e-06
        mc_out[0, :, cols] = (m_next * (1.0 / m_top)).astype(BF16)
        vc_out[0, :, cols] = (v_next * (1.0 / v_top)).astype(BF16)
        m_tops = jnp.where(lane == b, m_top, m_tops)
        v_tops = jnp.where(lane == b, v_top, v_tops)
    ms_out[0] = m_tops.T
    vs_out[0] = v_tops.T


def adam(master_weight, grads, m_code, m_scale, v_code, v_scale):
    members, rows, width = master_weight.shape
    blocks = m_scale.shape[-1]
    count = 8 if blocks % 8 == 0 else blocks
    big = pl.BlockSpec((1, rows, count * BLOCK), lambda e, j: (e, 0, j))
    small = pl.BlockSpec((1, count, rows), lambda e, j: (e, j, 0))
    scales = jax.ShapeDtypeStruct((members, blocks, rows), F32)
    master_next, m_code_next, m_scale_next, v_code_next, v_scale_next = pl.pallas_call(
        functools.partial(adam_kernel, len(grads)),
        grid=(members, blocks // count),
        in_specs=[big, big, small, big, small] + [big] * len(grads),
        out_specs=(big, big, small, big, small),
        out_shape=(
            jax.ShapeDtypeStruct(master_weight.shape, F32),
            jax.ShapeDtypeStruct(master_weight.shape, BF16),
            scales,
            jax.ShapeDtypeStruct(master_weight.shape, BF16),
            scales,
        ),
        compiler_params=params("arbitrary", "arbitrary"),
        cost_estimate=cost(40 * master_weight.size, 18 * master_weight.size),
        name="adam",
    )(master_weight, m_code, jnp.swapaxes(m_scale, 1, 2), v_code, jnp.swapaxes(v_scale, 1, 2), *grads)
    return (
        master_next,
        m_code_next,
        jnp.swapaxes(m_scale_next, 1, 2),
        v_code_next,
        jnp.swapaxes(v_scale_next, 1, 2),
    )


def swap(array, axis, offset):
    size = lax.axis_size(axis)
    return lax.ppermute(array, axis, [(i, i ^ offset) for i in range(size)])


def exchange(buffer, groups):
    places, width = buffer.shape
    parts = buffer.reshape(groups, places // groups, width)
    members = sorted(range(groups), key=lambda device: order_of(device, groups))
    moved = lax.all_to_all(
        parts, "grp", split_axis=0, concat_axis=0, tiled=True, axis_index_groups=[members]
    )
    return moved.reshape(places, width)


def gather_weight(weight_slice, replicas):
    if replicas != 4:
        return [lax.all_gather(weight_slice, "rep", axis=1, tiled=True)]
    far = swap(weight_slice, "rep", 2)
    near = swap(weight_slice, "rep", 1)
    return [weight_slice, near, far, swap(far, "rep", 1)]


def sum_gradient(parts):
    if len(parts) != 4:
        return [lax.psum_scatter(parts[0], "rep", scatter_dimension=1, tiled=True)]
    far = swap(parts[3], "rep", 1)
    near = swap(parts[1], "rep", 1)
    return [parts[0], near, swap(add_parts(parts[2], far), "rep", 2)]


def per_device(master_weight, m_code, m_scale, v_code, v_scale, placement, route, x_rows, y_cot):
    local_count = master_weight.shape[0]
    row_count = x_rows.shape[0]
    expert_count = placement.shape[0]
    groups = lax.axis_size("grp")
    replicas = lax.axis_size("rep")
    grad_factor = float(row_count * groups * replicas // expert_count) ** (-0.5)
    capacity = max(2, (3 * row_count + 2 * expert_count - 1) // (2 * expert_count))
    places = expert_count * capacity
    sent, target = dispatch(route, placement, x_rows, y_cot, capacity, groups)
    local = exchange(sent, groups)
    early_master, target = lax.optimization_barrier((master_weight, target))
    weight = join_weight(gather_weight(cast_weight(early_master), replicas))
    results = products(local, weight, capacity, local_count)
    local, results = lax.optimization_barrier((local, results))
    home = exchange(results, groups)

    parts = replicas if replicas == 4 else 1
    hidden = x_rows.shape[1]
    grads = sum_gradient(gradient(local, hidden, capacity, local_count, parts, grad_factor))
    updated = adam(master_weight, grads, m_code, m_scale, v_code, v_scale)
    y_rows, x_grad = collect(target, home, hidden)
    return (y_rows, x_grad) + tuple(updated)


def solution(mesh):
    return jax.shard_map(
        per_device,
        mesh=mesh,
        in_specs=(
            P("grp", "rep", None),
            P("grp", "rep", None),
            P("grp", "rep", None),
            P("grp", "rep", None),
            P("grp", "rep", None),
            P(),
            P(("rep", "grp")),
            P(("rep", "grp"), None),
            P(("rep", "grp"), None),
        ),
        out_specs=(
            P(("rep", "grp"), None),
            P(("rep", "grp"), None),
            P("grp", "rep", None),
            P("grp", "rep", None),
            P("grp", "rep", None),
            P("grp", "rep", None),
            P("grp", "rep", None),
        ),
        check_vma=False,
    )
```

```python
import functools

import jax
import jax.numpy as jnp
from jax import lax
from jax.experimental import pallas as pl
from jax.experimental.pallas import tpu as pltpu
from jax.sharding import PartitionSpec as P

BLOCK = 128
ADAM_STEP = 100

beta_one = 0.9
beta_two = 0.95
learn_rate = 0.01

VMEM_LIMIT = 40 * 1024 * 1024
LARGE_LIMIT = 60 * 1024 * 1024 + 512 * 1024
F32 = jnp.float32
BF16 = jnp.bfloat16


def cost(flops, nbytes):
    return pl.CostEstimate(flops=int(flops), bytes_accessed=int(nbytes), transcendentals=0)


def params(*semantics):
    if semantics:
        return pltpu.CompilerParams(vmem_limit_bytes=VMEM_LIMIT, dimension_semantics=semantics)
    return pltpu.CompilerParams(vmem_limit_bytes=VMEM_LIMIT)


def order_of(device, groups):
    if groups % 4:
        return device
    count = groups // 2
    outer, inner = device // 2, device % 2
    upper = outer // (count // 2)
    near = outer + upper * (count - 1 - 2 * outer)
    return (inner * (count // 2) + near) * 2 + upper


def row_targets(route_row, placement_row, capacity, groups):
    expert_count = placement_row.shape[1]
    row_count = route_row.shape[1]
    diagonal = lax.broadcasted_iota(jnp.int32, (expert_count, expert_count), 0) == (
        lax.broadcasted_iota(jnp.int32, (expert_count, expert_count), 1)
    )
    placement_col = jnp.sum(
        jnp.where(diagonal, placement_row, 0).astype(F32), axis=1, keepdims=True
    )
    hot = (placement_col == route_row.astype(F32)).astype(F32)
    earlier = lax.broadcasted_iota(jnp.int32, (row_count, row_count), 0)
    later = lax.broadcasted_iota(jnp.int32, (row_count, row_count), 1)
    before = (earlier < later).astype(F32).astype(BF16)
    position = jnp.dot(hot.astype(BF16), before, preferred_element_type=F32)
    slot = lax.broadcasted_iota(jnp.int32, (expert_count, row_count), 0)
    local_count = expert_count // groups
    order = order_of(slot // local_count, groups)
    start = ((order * local_count + slot % local_count) * capacity).astype(F32)
    return jnp.sum(hot * (start + position), axis=0, keepdims=True).astype(jnp.int32)


def place_matrix(target, places):
    slots = lax.broadcasted_iota(jnp.int32, (places, target.shape[1]), 0)
    return (slots == target).astype(F32).astype(BF16)


def dispatch_kernel(
    capacity, groups, route_hbm, placement_hbm, x_hbm, g_hbm, sent_hbm, target_hbm,
    route_ref, placement_ref, target_ref, x_ref, g_ref, sent_ref, key_sems, in_sems, out_sems,
):
    row_count, hidden = x_ref.shape
    width = g_ref.shape[1]
    tiles = out_sems.shape[0] - 1
    tile = width // tiles
    parts = in_sems.shape[0] - 1
    keys = [
        pltpu.make_async_copy(route_hbm, route_ref, key_sems.at[0]),
        pltpu.make_async_copy(placement_hbm, placement_ref, key_sems.at[1]),
    ]
    bands = [pl.ds(i * (row_count // parts), row_count // parts) for i in range(parts)]
    loads = [pltpu.make_async_copy(x_hbm, x_ref, in_sems.at[parts])] + [
        pltpu.make_async_copy(g_hbm.at[band], g_ref.at[band], in_sems.at[i])
        for i, band in enumerate(bands)
    ]
    for load in keys + loads:
        load.start()
    for load in keys:
        load.wait()
    target = row_targets(route_ref[...], placement_ref[...], capacity, groups)
    target_ref[...] = target
    stores = [pltpu.make_async_copy(target_ref, target_hbm, key_sems.at[2])]
    stores[0].start()
    places = place_matrix(target, sent_ref.shape[0])
    for j in range(tiles + 1):
        for load in loads[:1] if j == 0 else loads[1:] if j == 1 else []:
            load.wait()
        columns = pl.ds((j - 1) * tile, tile) if j else pl.ds(width, hidden)
        rows = g_ref[:, columns] if j else x_ref[...]
        sent_ref[:, columns] = jnp.dot(places, rows, preferred_element_type=F32).astype(BF16)
        store = pltpu.make_async_copy(
            sent_ref.at[:, columns], sent_hbm.at[:, columns], out_sems.at[j]
        )
        store.start()
        stores.append(store)
    for store in stores:
        store.wait()


def dispatch(route, placement, x_rows, y_cot, capacity, groups):
    row_count, hidden = x_rows.shape
    width = y_cot.shape[1]
    expert_count = placement.shape[0]
    tile = min(width, 512)
    tiles = width // tile
    parts = 4 if row_count % 64 == 0 else 1
    places = expert_count * capacity
    hbm = pl.BlockSpec(memory_space=pl.ANY)
    return pl.pallas_call(
        functools.partial(dispatch_kernel, capacity, groups),
        in_specs=[hbm, hbm, hbm, hbm],
        out_specs=(hbm, hbm),
        out_shape=(
            jax.ShapeDtypeStruct((places, width + hidden), BF16),
            jax.ShapeDtypeStruct((1, row_count), jnp.int32),
        ),
        scratch_shapes=[
            pltpu.VMEM((1, row_count), jnp.int32),
            pltpu.VMEM((1, expert_count), jnp.int32),
            pltpu.VMEM((1, row_count), jnp.int32),
            pltpu.VMEM((row_count, hidden), BF16),
            pltpu.VMEM((row_count, width), BF16),
            pltpu.VMEM((places, width + hidden), BF16),
            pltpu.SemaphoreType.DMA((3,)),
            pltpu.SemaphoreType.DMA((parts + 1,)),
            pltpu.SemaphoreType.DMA((tiles + 1,)),
        ],
        compiler_params=pltpu.CompilerParams(vmem_limit_bytes=LARGE_LIMIT),
        cost_estimate=cost(
            2 * places * row_count * (hidden + width), 2 * (places + row_count) * (hidden + width)
        ),
        name="dispatch",
    )(route.reshape(1, row_count), placement.reshape(1, -1), x_rows, y_cot)


def hidden_specs(rows, hidden, width):
    return [
        pl.BlockSpec((rows, BLOCK), functools.partial(lambda k, j: (0, k), width // BLOCK + i))
        for i in range(hidden // BLOCK)
    ]


def read_columns(refs):
    return jnp.concatenate([ref[...] for ref in refs], axis=1)


def collect_kernel(
    target_hbm, home_ref, y_hbm, dx_hbm, target_ref, y_ref, dx_ref, target_sem, out_sems
):
    hidden = dx_ref.shape[1]
    width = y_ref.shape[1]
    tiles = out_sems.shape[0] - 1
    tile = width // tiles
    spans = [pl.ds(j * tile, tile) for j in range(tiles)] + [pl.ds(width, hidden)]
    target_load = pltpu.make_async_copy(target_hbm, target_ref, target_sem)
    target_load.start()
    target_load.wait()
    target = target_ref[...]
    slots = lax.broadcasted_iota(jnp.int32, (home_ref.shape[0], target.shape[1]), 0)
    places = (slots == target).astype(F32).T.astype(BF16)
    stores = []
    for j, span in enumerate(spans):
        rows = jnp.dot(places, home_ref[:, span], preferred_element_type=F32).astype(BF16)
        if j < tiles:
            y_ref[:, span] = rows
            store = pltpu.make_async_copy(y_ref.at[:, span], y_hbm.at[:, span], out_sems.at[j])
        else:
            dx_ref[...] = rows
            store = pltpu.make_async_copy(dx_ref, dx_hbm, out_sems.at[j])
        store.start()
        stores.append(store)
    for store in stores:
        store.wait()


def collect(target, home, hidden):
    total, width = home.shape
    width -= hidden
    row_count = target.shape[1]
    tiles = width // min(width, 512)
    hbm = pl.BlockSpec(memory_space=pl.ANY)
    return pl.pallas_call(
        collect_kernel,
        in_specs=[hbm, pl.BlockSpec(memory_space=pltpu.VMEM)],
        out_specs=(hbm, hbm),
        out_shape=(
            jax.ShapeDtypeStruct((row_count, width), BF16),
            jax.ShapeDtypeStruct((row_count, hidden), BF16),
        ),
        scratch_shapes=[
            pltpu.VMEM(target.shape, jnp.int32),
            pltpu.VMEM((row_count, width), BF16),
            pltpu.VMEM((row_count, hidden), BF16),
            pltpu.SemaphoreType.DMA,
            pltpu.SemaphoreType.DMA((tiles + 1,)),
        ],
        compiler_params=params(),
        cost_estimate=cost(
            2 * total * row_count * (hidden + width), 2 * (total + row_count) * (hidden + width)
        ),
        name="collect",
    )(target, home)


def member_rows(rows, capacity, local_count):
    index = lax.broadcasted_iota(jnp.int32, (rows, 1), 0)
    return lax.rem(index, capacity * local_count) // capacity


def spread(x, capacity, local_count):
    member = member_rows(x.shape[0], capacity, local_count)
    zero = jnp.zeros_like(x)
    return jnp.concatenate([jnp.where(member == e, x, zero) for e in range(local_count)], axis=1)


def join_kernel(*refs):
    piece_refs, out_ref = refs[:-1], refs[-1]
    pieces = len(piece_refs)
    here = lax.axis_index("rep") if pieces > 1 else 0
    for i, ref in enumerate(piece_refs):
        owner = jnp.bitwise_xor(here, i) if pieces > 1 else 0
        for e in range(out_ref.shape[1]):
            out_ref[0, e, owner] = ref[e]


def join_weight(weight):
    local_count, rows, width = weight[0].shape
    pieces = len(weight)
    tile = min(width, 512)
    tiles = width // tile
    joined = pl.pallas_call(
        join_kernel,
        grid=(tiles,),
        in_specs=[pl.BlockSpec((local_count, rows, tile), lambda j: (0, 0, j))] * pieces,
        out_specs=pl.BlockSpec((1, local_count, pieces, rows, tile), lambda j: (j, 0, 0, 0, 0)),
        out_shape=jax.ShapeDtypeStruct((tiles, local_count, pieces, rows, tile), BF16),
        compiler_params=pltpu.CompilerParams(
            vmem_limit_bytes=LARGE_LIMIT, dimension_semantics=("arbitrary",)
        ),
        cost_estimate=cost(0, 4 * local_count * pieces * rows * width),
        name="join_weight",
    )(*weight)
    return joined.reshape(tiles, local_count * pieces * rows, tile)


def member_parts(value, capacity, local_count):
    rows, width = value.shape
    groups = rows // (capacity * local_count)
    parts = value.astype(F32).reshape(groups, local_count, capacity, width)
    return [
        parts[:, e].reshape(groups * capacity, width).astype(BF16) for e in range(local_count)
    ]


def join_members(parts, capacity):
    groups = parts[0].shape[0] // capacity
    width = parts[0].shape[1]
    stacked = [part.reshape(groups, 1, capacity, width) for part in parts]
    joined = jnp.concatenate(stacked, axis=1)
    return joined.reshape(groups * len(parts) * capacity, width)


def pick_members(totals, capacity):
    member = member_rows(totals[0].shape[0], capacity, len(totals))
    picked = totals[0]
    for e in range(1, len(totals)):
        picked = jnp.where(member == e, totals[e], picked)
    return picked


def products_kernel(
    capacity, apart, local_hbm, w_hbm, out_hbm,
    local_ref, w_ref, x_ref, total_ref, out_ref, local_sem, w_sems, out_sems,
):
    step = pl.program_id(0)
    steps, _, tile = w_ref.shape
    local_count, _, hidden = total_ref.shape
    columns = pl.ds(pl.multiple_of(step * tile, tile), tile)

    def weight_load(j):
        return pltpu.make_async_copy(w_hbm.at[j], w_ref.at[j], w_sems.at[j])

    @pl.when(step == 0)
    def _():
        local_load = pltpu.make_async_copy(local_hbm, local_ref, local_sem)
        local_load.start()
        weight_load(0).start()
        total_ref[...] = jnp.zeros_like(total_ref)
        local_load.wait()
        for j in range(1, steps):
            weight_load(j).start()
        x = local_ref[:, steps * tile :]
        for e, part in enumerate(member_parts(x, capacity, local_count) if apart else [x]):
            x_ref[e] = part

    weight_load(step).wait()
    weights = [w_ref[step, e * hidden : (e + 1) * hidden] for e in range(local_count)]
    xs = [x_ref[e if apart else 0] for e in range(local_count)]
    ys = [jnp.dot(x, w, preferred_element_type=F32) for x, w in zip(xs, weights)]
    y = join_members(ys, capacity) if apart else pick_members(ys, capacity)
    out_ref[:, columns] = y.astype(BF16)
    pltpu.make_async_copy(
        out_ref.at[:, columns], out_hbm.at[:, columns], out_sems.at[step]
    ).start()
    g = local_ref[:, columns]
    gs = member_parts(g, capacity, local_count) if apart else [g] * local_count
    for e in range(local_count):
        total_ref[e] += lax.dot_general(
            gs[e], weights[e], (((1,), (1,)), ((), ())), preferred_element_type=F32
        )

    @pl.when(step == steps - 1)
    def _():
        totals = [total_ref[e] for e in range(local_count)]
        dx = join_members(totals, capacity) if apart else pick_members(totals, capacity)
        last = pl.ds(steps * tile, hidden)
        out_ref[:, last] = dx.astype(BF16)
        final = pltpu.make_async_copy(out_ref.at[:, last], out_hbm.at[:, last], out_sems.at[steps])
        final.start()
        for j in range(steps):
            span = pl.ds(j * tile, tile)
            pltpu.make_async_copy(out_ref.at[:, span], out_hbm.at[:, span], out_sems.at[j]).wait()
        final.wait()


def products(local, weight, capacity, local_count):
    tiles, wide, tile = weight.shape
    width = tiles * tile
    total = local.shape[0]
    hidden = wide // local_count
    apart = capacity % 8 == 0
    rows = total // local_count if apart else total
    hbm = pl.BlockSpec(memory_space=pl.ANY)
    return pl.pallas_call(
        functools.partial(products_kernel, capacity, apart),
        grid=(tiles,),
        in_specs=[hbm, hbm],
        out_specs=hbm,
        out_shape=jax.ShapeDtypeStruct(local.shape, BF16),
        scratch_shapes=[
            pltpu.VMEM(local.shape, BF16),
            pltpu.VMEM(weight.shape, BF16),
            pltpu.VMEM((local_count if apart else 1, rows, hidden), BF16),
            pltpu.VMEM((local_count, rows, hidden), F32),
            pltpu.VMEM(local.shape, BF16),
            pltpu.SemaphoreType.DMA,
            pltpu.SemaphoreType.DMA((tiles,)),
            pltpu.SemaphoreType.DMA((tiles + 1,)),
        ],
        compiler_params=pltpu.CompilerParams(
            vmem_limit_bytes=LARGE_LIMIT, dimension_semantics=("arbitrary",)
        ),
        cost_estimate=cost(4 * rows * wide * width, 2 * (wide + 2 * total) * width),
        name="products",
    )(local, weight)


def gradient_kernel(capacity, local_count, parts, factor, g_ref, *refs):
    blocks = len(refs) - 2 - (parts if parts > 1 else 0)
    x_refs, wide_ref = refs[:blocks], refs[-1]
    out_refs = refs[blocks:-2] if parts > 1 else refs[blocks:-1]

    @pl.when(pl.program_id(0) == 0)
    def _():
        wide_ref[...] = spread(read_columns(x_refs), capacity, local_count)

    outer = lax.dot_general(
        wide_ref[...], g_ref[...], (((0,), (0,)), ((), ())), preferred_element_type=F32
    )
    low = (outer * factor).astype(BF16)
    if parts == 1:
        out_refs[0][...] = low.reshape(out_refs[0].shape)
        return
    split_ref = refs[-2]
    split_ref[...] = low.reshape(split_ref.shape)
    here = lax.axis_index("rep")
    for i, out_ref in enumerate(out_refs):
        owner = jnp.bitwise_xor(here, i)
        for e in range(local_count):
            out_ref[e] = split_ref[e, owner]


def gradient(local, hidden, capacity, local_count, parts, factor):
    total, width = local.shape
    width -= hidden
    tile = min(width, 512)
    slice_rows = hidden // parts
    specs = hidden_specs(total, hidden, width)
    split = [pltpu.VMEM((local_count, parts, slice_rows, tile), BF16)] if parts > 1 else []
    return list(pl.pallas_call(
        functools.partial(gradient_kernel, capacity, local_count, parts, factor),
        grid=(width // tile,),
        in_specs=[pl.BlockSpec((total, tile), lambda j: (0, j))] + specs,
        out_specs=(pl.BlockSpec((local_count, slice_rows, tile), lambda j: (0, 0, j)),) * parts,
        out_shape=(jax.ShapeDtypeStruct((local_count, slice_rows, width), BF16),) * parts,
        scratch_shapes=split + [pltpu.VMEM((total, local_count * hidden), BF16)],
        compiler_params=pltpu.CompilerParams(
            vmem_limit_bytes=LARGE_LIMIT, dimension_semantics=("arbitrary",)
        ),
        cost_estimate=cost(
            2 * total * local_count * hidden * width,
            2 * (local_count * hidden + total) * width,
        ),
        name="gradient",
    )(*([local] * (1 + len(specs)))))


def cast_kernel(w_ref, out_ref):
    out_ref[...] = w_ref[...].astype(BF16)


def cast_weight(weight):
    members, rows, width = weight.shape
    tile = min(width, 512)
    spec = pl.BlockSpec((members, rows, tile), lambda j: (0, 0, j))
    return pl.pallas_call(
        cast_kernel,
        grid=(width // tile,),
        in_specs=[spec],
        out_specs=spec,
        out_shape=jax.ShapeDtypeStruct(weight.shape, BF16),
        compiler_params=params("arbitrary"),
        cost_estimate=cost(weight.size, 6 * weight.size),
        name="cast_weight",
    )(weight)


def add_kernel(a_ref, b_ref, out_ref):
    out_ref[...] = (a_ref[...].astype(F32) + b_ref[...].astype(F32)).astype(BF16)


def add_parts(a, b):
    members, rows, width = a.shape
    tile = min(width, 1024)
    spec = pl.BlockSpec((members, rows, tile), lambda j: (0, 0, j))
    return pl.pallas_call(
        add_kernel,
        grid=(width // tile,),
        in_specs=[spec, spec],
        out_specs=spec,
        out_shape=jax.ShapeDtypeStruct(a.shape, BF16),
        compiler_params=params("arbitrary"),
        cost_estimate=cost(a.size, 6 * a.size),
        name="add_parts",
    )(a, b)


def adam_kernel(
    parts, master_ref, mc_ref, ms_ref, vc_ref, vs_ref, *refs
):
    grad_refs = refs[:parts]
    master_out, mc_out, ms_out, vc_out, vs_out = refs[parts:]
    blocks = ms_ref.shape[1]
    rows = ms_ref.shape[2]
    corr_one = 1.0 - beta_one**ADAM_STEP
    corr_two = 1.0 - beta_two**ADAM_STEP
    m_scales = (ms_ref[0] * beta_one).T
    v_scales = (vs_ref[0] * beta_two).T
    lane = lax.broadcasted_iota(jnp.int32, (rows, blocks), 1)
    m_tops = jnp.zeros((rows, blocks), F32)
    v_tops = jnp.zeros((rows, blocks), F32)
    for b in range(blocks):
        cols = slice(b * BLOCK, (b + 1) * BLOCK)
        grad = grad_refs[0][0, :, cols].astype(F32)
        for ref in grad_refs[1:]:
            grad = grad + ref[0, :, cols].astype(F32)
        m_next = mc_ref[0, :, cols].astype(F32) * m_scales[:, b : b + 1] + (1.0 - beta_one) * grad
        v_next = vc_ref[0, :, cols].astype(F32) * v_scales[:, b : b + 1] + (
            1.0 - beta_two
        ) * (grad * grad)
        v_hat = v_next * (1.0 / corr_two)
        root = v_hat * lax.rsqrt(v_hat) + 1e-08
        master_out[0, :, cols] = master_ref[0, :, cols] - (learn_rate / corr_one) * m_next / root
        m_top = jnp.max(jnp.abs(m_next), axis=-1, keepdims=True) + 1e-06
        v_top = jnp.max(v_next, axis=-1, keepdims=True) + 1e-06
        mc_out[0, :, cols] = (m_next * (1.0 / m_top)).astype(BF16)
        vc_out[0, :, cols] = (v_next * (1.0 / v_top)).astype(BF16)
        m_tops = jnp.where(lane == b, m_top, m_tops)
        v_tops = jnp.where(lane == b, v_top, v_tops)
    ms_out[0] = m_tops.T
    vs_out[0] = v_tops.T


def adam(master_weight, grads, m_code, m_scale, v_code, v_scale):
    members, rows, width = master_weight.shape
    blocks = m_scale.shape[-1]
    count = 8 if blocks % 8 == 0 else blocks
    big = pl.BlockSpec((1, rows, count * BLOCK), lambda e, j: (e, 0, j))
    small = pl.BlockSpec((1, count, rows), lambda e, j: (e, j, 0))
    scales = jax.ShapeDtypeStruct((members, blocks, rows), F32)
    master_next, m_code_next, m_scale_next, v_code_next, v_scale_next = pl.pallas_call(
        functools.partial(adam_kernel, len(grads)),
        grid=(members, blocks // count),
        in_specs=[big, big, small, big, small] + [big] * len(grads),
        out_specs=(big, big, small, big, small),
        out_shape=(
            jax.ShapeDtypeStruct(master_weight.shape, F32),
            jax.ShapeDtypeStruct(master_weight.shape, BF16),
            scales,
            jax.ShapeDtypeStruct(master_weight.shape, BF16),
            scales,
        ),
        compiler_params=params("arbitrary", "arbitrary"),
        cost_estimate=cost(40 * master_weight.size, 18 * master_weight.size),
        name="adam",
    )(master_weight, m_code, jnp.swapaxes(m_scale, 1, 2), v_code, jnp.swapaxes(v_scale, 1, 2), *grads)
    return (
        master_next,
        m_code_next,
        jnp.swapaxes(m_scale_next, 1, 2),
        v_code_next,
        jnp.swapaxes(v_scale_next, 1, 2),
    )


def swap(array, axis, offset):
    size = lax.axis_size(axis)
    return lax.ppermute(array, axis, [(i, i ^ offset) for i in range(size)])


def exchange(buffer, groups):
    places, width = buffer.shape
    parts = buffer.reshape(groups, places // groups, width)
    members = sorted(range(groups), key=lambda device: order_of(device, groups))
    moved = lax.all_to_all(
        parts, "grp", split_axis=0, concat_axis=0, tiled=True, axis_index_groups=[members]
    )
    return moved.reshape(places, width)


def gather_weight(weight_slice, replicas):
    if replicas != 4:
        return [lax.all_gather(weight_slice, "rep", axis=1, tiled=True)]
    far = swap(weight_slice, "rep", 2)
    near = swap(weight_slice, "rep", 1)
    return [weight_slice, near, far, swap(far, "rep", 1)]


def sum_gradient(parts):
    if len(parts) != 4:
        return [lax.psum_scatter(parts[0], "rep", scatter_dimension=1, tiled=True)]
    far = swap(parts[3], "rep", 1)
    near = swap(parts[1], "rep", 1)
    return [parts[0], near, swap(add_parts(parts[2], far), "rep", 2)]


def per_device(master_weight, m_code, m_scale, v_code, v_scale, placement, route, x_rows, y_cot):
    local_count = master_weight.shape[0]
    row_count = x_rows.shape[0]
    expert_count = placement.shape[0]
    groups = lax.axis_size("grp")
    replicas = lax.axis_size("rep")
    grad_factor = float(row_count * groups * replicas // expert_count) ** (-0.5)
    capacity = max(2, (3 * row_count + 2 * expert_count - 1) // (2 * expert_count))
    places = expert_count * capacity
    sent, target = dispatch(route, placement, x_rows, y_cot, capacity, groups)
    local = exchange(sent, groups)
    early_master, target = lax.optimization_barrier((master_weight, target))
    weight = join_weight(gather_weight(cast_weight(early_master), replicas))
    results = products(local, weight, capacity, local_count)
    local, results = lax.optimization_barrier((local, results))
    home = exchange(results, groups)

    parts = replicas if replicas == 4 else 1
    hidden = x_rows.shape[1]
    grads = sum_gradient(gradient(local, hidden, capacity, local_count, parts, grad_factor))
    updated = adam(master_weight, grads, m_code, m_scale, v_code, v_scale)
    y_rows, x_grad = collect(target, home, hidden)
    return (y_rows, x_grad) + tuple(updated)


def solution(mesh):
    return jax.shard_map(
        per_device,
        mesh=mesh,
        in_specs=(
            P("grp", "rep", None),
            P("grp", "rep", None),
            P("grp", "rep", None),
            P("grp", "rep", None),
            P("grp", "rep", None),
            P(),
            P(("rep", "grp")),
            P(("rep", "grp"), None),
            P(("rep", "grp"), None),
        ),
        out_specs=(
            P(("rep", "grp"), None),
            P(("rep", "grp"), None),
            P("grp", "rep", None),
            P("grp", "rep", None),
            P("grp", "rep", None),
            P("grp", "rep", None),
            P("grp", "rep", None),
        ),
        check_vma=False,
    )
```

```python
import functools

import jax
import jax.numpy as jnp
from jax import lax
from jax.experimental import pallas as pl
from jax.experimental.pallas import tpu as pltpu
from jax.sharding import PartitionSpec as P

BLOCK = 128
ADAM_STEP = 100

beta_one = 0.9
beta_two = 0.95
learn_rate = 0.01

VMEM_LIMIT = 40 * 1024 * 1024
LARGE_LIMIT = 60 * 1024 * 1024 + 512 * 1024
F32 = jnp.float32
BF16 = jnp.bfloat16


def cost(flops, nbytes):
    return pl.CostEstimate(flops=int(flops), bytes_accessed=int(nbytes), transcendentals=0)


def params(*semantics):
    if semantics:
        return pltpu.CompilerParams(vmem_limit_bytes=VMEM_LIMIT, dimension_semantics=semantics)
    return pltpu.CompilerParams(vmem_limit_bytes=VMEM_LIMIT)


def order_of(device, groups):
    if groups % 2:
        return device
    half = groups // 2
    upper = device // half
    near = device + upper * (groups - 1 - 2 * device)
    return near + (upper + near) % 2 * half


def row_targets(route_row, placement_row, capacity, groups):
    expert_count = placement_row.shape[1]
    row_count = route_row.shape[1]
    diagonal = lax.broadcasted_iota(jnp.int32, (expert_count, expert_count), 0) == (
        lax.broadcasted_iota(jnp.int32, (expert_count, expert_count), 1)
    )
    placement_col = jnp.sum(
        jnp.where(diagonal, placement_row, 0).astype(F32), axis=1, keepdims=True
    )
    hot = (placement_col == route_row.astype(F32)).astype(F32)
    earlier = lax.broadcasted_iota(jnp.int32, (row_count, row_count), 0)
    later = lax.broadcasted_iota(jnp.int32, (row_count, row_count), 1)
    before = (earlier < later).astype(F32).astype(BF16)
    position = jnp.dot(hot.astype(BF16), before, preferred_element_type=F32)
    slot = lax.broadcasted_iota(jnp.int32, (expert_count, row_count), 0)
    local_count = expert_count // groups
    order = order_of(slot // local_count, groups)
    start = ((order * local_count + slot % local_count) * capacity).astype(F32)
    return jnp.sum(hot * (start + position), axis=0, keepdims=True).astype(jnp.int32)


def place_matrix(target, places):
    slots = lax.broadcasted_iota(jnp.int32, (places, target.shape[1]), 0)
    return (slots == target).astype(F32).astype(BF16)


def dispatch_kernel(
    capacity, groups, route_hbm, placement_hbm, x_hbm, g_hbm, sent_hbm, target_hbm,
    route_ref, placement_ref, target_ref, x_ref, g_ref, sent_ref, key_sems, in_sems, out_sems,
):
    row_count, hidden = x_ref.shape
    width = g_ref.shape[1]
    tiles = out_sems.shape[0] - 1
    tile = width // tiles
    parts = in_sems.shape[0] - 1
    keys = [
        pltpu.make_async_copy(route_hbm, route_ref, key_sems.at[0]),
        pltpu.make_async_copy(placement_hbm, placement_ref, key_sems.at[1]),
    ]
    bands = [pl.ds(i * (row_count // parts), row_count // parts) for i in range(parts)]
    loads = [pltpu.make_async_copy(x_hbm, x_ref, in_sems.at[parts])] + [
        pltpu.make_async_copy(g_hbm.at[band], g_ref.at[band], in_sems.at[i])
        for i, band in enumerate(bands)
    ]
    for load in keys + loads:
        load.start()
    for load in keys:
        load.wait()
    target = row_targets(route_ref[...], placement_ref[...], capacity, groups)
    target_ref[...] = target
    stores = [pltpu.make_async_copy(target_ref, target_hbm, key_sems.at[2])]
    stores[0].start()
    places = place_matrix(target, sent_ref.shape[0])
    for j in range(tiles + 1):
        for load in loads[:1] if j == 0 else loads[1:] if j == 1 else []:
            load.wait()
        columns = pl.ds((j - 1) * tile, tile) if j else pl.ds(width, hidden)
        rows = g_ref[:, columns] if j else x_ref[...]
        sent_ref[:, columns] = jnp.dot(places, rows, preferred_element_type=F32).astype(BF16)
        store = pltpu.make_async_copy(
            sent_ref.at[:, columns], sent_hbm.at[:, columns], out_sems.at[j]
        )
        store.start()
        stores.append(store)
    for store in stores:
        store.wait()


def dispatch(route, placement, x_rows, y_cot, capacity, groups):
    row_count, hidden = x_rows.shape
    width = y_cot.shape[1]
    expert_count = placement.shape[0]
    tile = min(width, 512)
    tiles = width // tile
    parts = 4 if row_count % 64 == 0 else 1
    places = expert_count * capacity
    hbm = pl.BlockSpec(memory_space=pl.ANY)
    return pl.pallas_call(
        functools.partial(dispatch_kernel, capacity, groups),
        in_specs=[hbm, hbm, hbm, hbm],
        out_specs=(hbm, hbm),
        out_shape=(
            jax.ShapeDtypeStruct((places, width + hidden), BF16),
            jax.ShapeDtypeStruct((1, row_count), jnp.int32),
        ),
        scratch_shapes=[
            pltpu.VMEM((1, row_count), jnp.int32),
            pltpu.VMEM((1, expert_count), jnp.int32),
            pltpu.VMEM((1, row_count), jnp.int32),
            pltpu.VMEM((row_count, hidden), BF16),
            pltpu.VMEM((row_count, width), BF16),
            pltpu.VMEM((places, width + hidden), BF16),
            pltpu.SemaphoreType.DMA((3,)),
            pltpu.SemaphoreType.DMA((parts + 1,)),
            pltpu.SemaphoreType.DMA((tiles + 1,)),
        ],
        compiler_params=pltpu.CompilerParams(vmem_limit_bytes=LARGE_LIMIT),
        cost_estimate=cost(
            2 * places * row_count * (hidden + width), 2 * (places + row_count) * (hidden + width)
        ),
        name="dispatch",
    )(route.reshape(1, row_count), placement.reshape(1, -1), x_rows, y_cot)


def hidden_specs(rows, hidden, width):
    return [
        pl.BlockSpec((rows, BLOCK), functools.partial(lambda k, j: (0, k), width // BLOCK + i))
        for i in range(hidden // BLOCK)
    ]


def read_columns(refs):
    return jnp.concatenate([ref[...] for ref in refs], axis=1)


def collect_kernel(
    target_hbm, home_ref, y_hbm, dx_hbm, target_ref, y_ref, dx_ref, target_sem, out_sems
):
    hidden = dx_ref.shape[1]
    width = y_ref.shape[1]
    tiles = out_sems.shape[0] - 1
    tile = width // tiles
    spans = [pl.ds(j * tile, tile) for j in range(tiles)] + [pl.ds(width, hidden)]
    target_load = pltpu.make_async_copy(target_hbm, target_ref, target_sem)
    target_load.start()
    target_load.wait()
    target = target_ref[...]
    slots = lax.broadcasted_iota(jnp.int32, (home_ref.shape[0], target.shape[1]), 0)
    places = (slots == target).astype(F32).T.astype(BF16)
    stores = []
    for j, span in enumerate(spans):
        rows = jnp.dot(places, home_ref[:, span], preferred_element_type=F32).astype(BF16)
        if j < tiles:
            y_ref[:, span] = rows
            store = pltpu.make_async_copy(y_ref.at[:, span], y_hbm.at[:, span], out_sems.at[j])
        else:
            dx_ref[...] = rows
            store = pltpu.make_async_copy(dx_ref, dx_hbm, out_sems.at[j])
        store.start()
        stores.append(store)
    for store in stores:
        store.wait()


def collect(target, home, hidden):
    total, width = home.shape
    width -= hidden
    row_count = target.shape[1]
    tiles = width // min(width, 512)
    hbm = pl.BlockSpec(memory_space=pl.ANY)
    return pl.pallas_call(
        collect_kernel,
        in_specs=[hbm, pl.BlockSpec(memory_space=pltpu.VMEM)],
        out_specs=(hbm, hbm),
        out_shape=(
            jax.ShapeDtypeStruct((row_count, width), BF16),
            jax.ShapeDtypeStruct((row_count, hidden), BF16),
        ),
        scratch_shapes=[
            pltpu.VMEM(target.shape, jnp.int32),
            pltpu.VMEM((row_count, width), BF16),
            pltpu.VMEM((row_count, hidden), BF16),
            pltpu.SemaphoreType.DMA,
            pltpu.SemaphoreType.DMA((tiles + 1,)),
        ],
        compiler_params=params(),
        cost_estimate=cost(
            2 * total * row_count * (hidden + width), 2 * (total + row_count) * (hidden + width)
        ),
        name="collect",
    )(target, home)


def member_rows(rows, capacity, local_count):
    index = lax.broadcasted_iota(jnp.int32, (rows, 1), 0)
    return lax.rem(index, capacity * local_count) // capacity


def spread(x, capacity, local_count):
    member = member_rows(x.shape[0], capacity, local_count)
    zero = jnp.zeros_like(x)
    return jnp.concatenate([jnp.where(member == e, x, zero) for e in range(local_count)], axis=1)


def join_kernel(*refs):
    piece_refs, out_ref = refs[:-1], refs[-1]
    pieces = len(piece_refs)
    here = lax.axis_index("rep") if pieces > 1 else 0
    for i, ref in enumerate(piece_refs):
        owner = jnp.bitwise_xor(here, i) if pieces > 1 else 0
        for e in range(out_ref.shape[1]):
            out_ref[0, e, owner] = ref[e]


def join_weight(weight):
    local_count, rows, width = weight[0].shape
    pieces = len(weight)
    tile = min(width, 512)
    tiles = width // tile
    joined = pl.pallas_call(
        join_kernel,
        grid=(tiles,),
        in_specs=[pl.BlockSpec((local_count, rows, tile), lambda j: (0, 0, j))] * pieces,
        out_specs=pl.BlockSpec((1, local_count, pieces, rows, tile), lambda j: (j, 0, 0, 0, 0)),
        out_shape=jax.ShapeDtypeStruct((tiles, local_count, pieces, rows, tile), BF16),
        compiler_params=pltpu.CompilerParams(
            vmem_limit_bytes=LARGE_LIMIT, dimension_semantics=("arbitrary",)
        ),
        cost_estimate=cost(0, 4 * local_count * pieces * rows * width),
        name="join_weight",
    )(*weight)
    return joined.reshape(tiles, local_count * pieces * rows, tile)


def member_parts(value, capacity, local_count):
    rows, width = value.shape
    groups = rows // (capacity * local_count)
    parts = value.astype(F32).reshape(groups, local_count, capacity, width)
    return [
        parts[:, e].reshape(groups * capacity, width).astype(BF16) for e in range(local_count)
    ]


def join_members(parts, capacity):
    groups = parts[0].shape[0] // capacity
    width = parts[0].shape[1]
    stacked = [part.reshape(groups, 1, capacity, width) for part in parts]
    joined = jnp.concatenate(stacked, axis=1)
    return joined.reshape(groups * len(parts) * capacity, width)


def pick_members(totals, capacity):
    member = member_rows(totals[0].shape[0], capacity, len(totals))
    picked = totals[0]
    for e in range(1, len(totals)):
        picked = jnp.where(member == e, totals[e], picked)
    return picked


def products_kernel(
    capacity, apart, local_hbm, w_hbm, out_hbm,
    local_ref, w_ref, x_ref, total_ref, out_ref, local_sem, w_sems, out_sems,
):
    step = pl.program_id(0)
    steps, _, tile = w_ref.shape
    local_count, _, hidden = total_ref.shape
    columns = pl.ds(pl.multiple_of(step * tile, tile), tile)

    def weight_load(j):
        return pltpu.make_async_copy(w_hbm.at[j], w_ref.at[j], w_sems.at[j])

    @pl.when(step == 0)
    def _():
        local_load = pltpu.make_async_copy(local_hbm, local_ref, local_sem)
        local_load.start()
        weight_load(0).start()
        total_ref[...] = jnp.zeros_like(total_ref)
        local_load.wait()
        for j in range(1, steps):
            weight_load(j).start()
        x = local_ref[:, steps * tile :]
        for e, part in enumerate(member_parts(x, capacity, local_count) if apart else [x]):
            x_ref[e] = part

    weight_load(step).wait()
    weights = [w_ref[step, e * hidden : (e + 1) * hidden] for e in range(local_count)]
    xs = [x_ref[e if apart else 0] for e in range(local_count)]
    ys = [jnp.dot(x, w, preferred_element_type=F32) for x, w in zip(xs, weights)]
    y = join_members(ys, capacity) if apart else pick_members(ys, capacity)
    out_ref[:, columns] = y.astype(BF16)
    pltpu.make_async_copy(
        out_ref.at[:, columns], out_hbm.at[:, columns], out_sems.at[step]
    ).start()
    g = local_ref[:, columns]
    gs = member_parts(g, capacity, local_count) if apart else [g] * local_count
    for e in range(local_count):
        total_ref[e] += lax.dot_general(
            gs[e], weights[e], (((1,), (1,)), ((), ())), preferred_element_type=F32
        )

    @pl.when(step == steps - 1)
    def _():
        totals = [total_ref[e] for e in range(local_count)]
        dx = join_members(totals, capacity) if apart else pick_members(totals, capacity)
        last = pl.ds(steps * tile, hidden)
        out_ref[:, last] = dx.astype(BF16)
        final = pltpu.make_async_copy(out_ref.at[:, last], out_hbm.at[:, last], out_sems.at[steps])
        final.start()
        for j in range(steps):
            span = pl.ds(j * tile, tile)
            pltpu.make_async_copy(out_ref.at[:, span], out_hbm.at[:, span], out_sems.at[j]).wait()
        final.wait()


def products(local, weight, capacity, local_count):
    tiles, wide, tile = weight.shape
    width = tiles * tile
    total = local.shape[0]
    hidden = wide // local_count
    apart = capacity % 8 == 0
    rows = total // local_count if apart else total
    hbm = pl.BlockSpec(memory_space=pl.ANY)
    return pl.pallas_call(
        functools.partial(products_kernel, capacity, apart),
        grid=(tiles,),
        in_specs=[hbm, hbm],
        out_specs=hbm,
        out_shape=jax.ShapeDtypeStruct(local.shape, BF16),
        scratch_shapes=[
            pltpu.VMEM(local.shape, BF16),
            pltpu.VMEM(weight.shape, BF16),
            pltpu.VMEM((local_count if apart else 1, rows, hidden), BF16),
            pltpu.VMEM((local_count, rows, hidden), F32),
            pltpu.VMEM(local.shape, BF16),
            pltpu.SemaphoreType.DMA,
            pltpu.SemaphoreType.DMA((tiles,)),
            pltpu.SemaphoreType.DMA((tiles + 1,)),
        ],
        compiler_params=pltpu.CompilerParams(
            vmem_limit_bytes=LARGE_LIMIT, dimension_semantics=("arbitrary",)
        ),
        cost_estimate=cost(4 * rows * wide * width, 2 * (wide + 2 * total) * width),
        name="products",
    )(local, weight)


def gradient_kernel(capacity, local_count, parts, factor, g_ref, *refs):
    blocks = len(refs) - 2 - (parts if parts > 1 else 0)
    x_refs, wide_ref = refs[:blocks], refs[-1]
    out_refs = refs[blocks:-2] if parts > 1 else refs[blocks:-1]

    @pl.when(pl.program_id(0) == 0)
    def _():
        wide_ref[...] = spread(read_columns(x_refs), capacity, local_count)

    outer = lax.dot_general(
        wide_ref[...], g_ref[...], (((0,), (0,)), ((), ())), preferred_element_type=F32
    )
    low = (outer * factor).astype(BF16)
    if parts == 1:
        out_refs[0][...] = low.reshape(out_refs[0].shape)
        return
    split_ref = refs[-2]
    split_ref[...] = low.reshape(split_ref.shape)
    here = lax.axis_index("rep")
    for i, out_ref in enumerate(out_refs):
        owner = jnp.bitwise_xor(here, i)
        for e in range(local_count):
            out_ref[e] = split_ref[e, owner]


def gradient(local, hidden, capacity, local_count, parts, factor):
    total, width = local.shape
    width -= hidden
    tile = min(width, 512)
    slice_rows = hidden // parts
    specs = hidden_specs(total, hidden, width)
    split = [pltpu.VMEM((local_count, parts, slice_rows, tile), BF16)] if parts > 1 else []
    return list(pl.pallas_call(
        functools.partial(gradient_kernel, capacity, local_count, parts, factor),
        grid=(width // tile,),
        in_specs=[pl.BlockSpec((total, tile), lambda j: (0, j))] + specs,
        out_specs=(pl.BlockSpec((local_count, slice_rows, tile), lambda j: (0, 0, j)),) * parts,
        out_shape=(jax.ShapeDtypeStruct((local_count, slice_rows, width), BF16),) * parts,
        scratch_shapes=split + [pltpu.VMEM((total, local_count * hidden), BF16)],
        compiler_params=pltpu.CompilerParams(
            vmem_limit_bytes=LARGE_LIMIT, dimension_semantics=("arbitrary",)
        ),
        cost_estimate=cost(
            2 * total * local_count * hidden * width,
            2 * (local_count * hidden + total) * width,
        ),
        name="gradient",
    )(*([local] * (1 + len(specs)))))


def cast_kernel(w_ref, out_ref):
    out_ref[...] = w_ref[...].astype(BF16)


def cast_weight(weight):
    members, rows, width = weight.shape
    tile = min(width, 512)
    spec = pl.BlockSpec((members, rows, tile), lambda j: (0, 0, j))
    return pl.pallas_call(
        cast_kernel,
        grid=(width // tile,),
        in_specs=[spec],
        out_specs=spec,
        out_shape=jax.ShapeDtypeStruct(weight.shape, BF16),
        compiler_params=params("arbitrary"),
        cost_estimate=cost(weight.size, 6 * weight.size),
        name="cast_weight",
    )(weight)


def add_kernel(a_ref, b_ref, out_ref):
    out_ref[...] = (a_ref[...].astype(F32) + b_ref[...].astype(F32)).astype(BF16)


def add_parts(a, b):
    members, rows, width = a.shape
    tile = min(width, 1024)
    spec = pl.BlockSpec((members, rows, tile), lambda j: (0, 0, j))
    return pl.pallas_call(
        add_kernel,
        grid=(width // tile,),
        in_specs=[spec, spec],
        out_specs=spec,
        out_shape=jax.ShapeDtypeStruct(a.shape, BF16),
        compiler_params=params("arbitrary"),
        cost_estimate=cost(a.size, 6 * a.size),
        name="add_parts",
    )(a, b)


def adam_kernel(
    parts, master_ref, mc_ref, ms_ref, vc_ref, vs_ref, *refs
):
    grad_refs = refs[:parts]
    master_out, mc_out, ms_out, vc_out, vs_out = refs[parts:]
    blocks = ms_ref.shape[1]
    rows = ms_ref.shape[2]
    corr_one = 1.0 - beta_one**ADAM_STEP
    corr_two = 1.0 - beta_two**ADAM_STEP
    m_scales = (ms_ref[0] * beta_one).T
    v_scales = (vs_ref[0] * beta_two).T
    lane = lax.broadcasted_iota(jnp.int32, (rows, blocks), 1)
    m_tops = jnp.zeros((rows, blocks), F32)
    v_tops = jnp.zeros((rows, blocks), F32)
    for b in range(blocks):
        cols = slice(b * BLOCK, (b + 1) * BLOCK)
        grad = grad_refs[0][0, :, cols].astype(F32)
        for ref in grad_refs[1:]:
            grad = grad + ref[0, :, cols].astype(F32)
        m_next = mc_ref[0, :, cols].astype(F32) * m_scales[:, b : b + 1] + (1.0 - beta_one) * grad
        v_next = vc_ref[0, :, cols].astype(F32) * v_scales[:, b : b + 1] + (
            1.0 - beta_two
        ) * (grad * grad)
        v_hat = v_next * (1.0 / corr_two)
        root = v_hat * lax.rsqrt(v_hat) + 1e-08
        master_out[0, :, cols] = master_ref[0, :, cols] - (learn_rate / corr_one) * m_next / root
        m_top = jnp.max(jnp.abs(m_next), axis=-1, keepdims=True) + 1e-06
        v_top = jnp.max(v_next, axis=-1, keepdims=True) + 1e-06
        mc_out[0, :, cols] = (m_next * (1.0 / m_top)).astype(BF16)
        vc_out[0, :, cols] = (v_next * (1.0 / v_top)).astype(BF16)
        m_tops = jnp.where(lane == b, m_top, m_tops)
        v_tops = jnp.where(lane == b, v_top, v_tops)
    ms_out[0] = m_tops.T
    vs_out[0] = v_tops.T


def adam(master_weight, grads, m_code, m_scale, v_code, v_scale):
    members, rows, width = master_weight.shape
    blocks = m_scale.shape[-1]
    count = 8 if blocks % 8 == 0 else blocks
    big = pl.BlockSpec((1, rows, count * BLOCK), lambda e, j: (e, 0, j))
    small = pl.BlockSpec((1, count, rows), lambda e, j: (e, j, 0))
    scales = jax.ShapeDtypeStruct((members, blocks, rows), F32)
    master_next, m_code_next, m_scale_next, v_code_next, v_scale_next = pl.pallas_call(
        functools.partial(adam_kernel, len(grads)),
        grid=(members, blocks // count),
        in_specs=[big, big, small, big, small] + [big] * len(grads),
        out_specs=(big, big, small, big, small),
        out_shape=(
            jax.ShapeDtypeStruct(master_weight.shape, F32),
            jax.ShapeDtypeStruct(master_weight.shape, BF16),
            scales,
            jax.ShapeDtypeStruct(master_weight.shape, BF16),
            scales,
        ),
        compiler_params=params("arbitrary", "arbitrary"),
        cost_estimate=cost(40 * master_weight.size, 18 * master_weight.size),
        name="adam",
    )(master_weight, m_code, jnp.swapaxes(m_scale, 1, 2), v_code, jnp.swapaxes(v_scale, 1, 2), *grads)
    return (
        master_next,
        m_code_next,
        jnp.swapaxes(m_scale_next, 1, 2),
        v_code_next,
        jnp.swapaxes(v_scale_next, 1, 2),
    )


def swap(array, axis, offset):
    size = lax.axis_size(axis)
    return lax.ppermute(array, axis, [(i, i ^ offset) for i in range(size)])


def exchange(buffer, groups):
    places, width = buffer.shape
    parts = buffer.reshape(groups, places // groups, width)
    members = sorted(range(groups), key=lambda device: order_of(device, groups))
    moved = lax.all_to_all(
        parts, "grp", split_axis=0, concat_axis=0, tiled=True, axis_index_groups=[members]
    )
    return moved.reshape(places, width)


def gather_weight(weight_slice, replicas):
    if replicas != 4:
        return [lax.all_gather(weight_slice, "rep", axis=1, tiled=True)]
    far = swap(weight_slice, "rep", 2)
    near = swap(weight_slice, "rep", 1)
    return [weight_slice, near, far, swap(far, "rep", 1)]


def sum_gradient(parts):
    if len(parts) != 4:
        return [lax.psum_scatter(parts[0], "rep", scatter_dimension=1, tiled=True)]
    far = swap(parts[3], "rep", 1)
    near = swap(parts[1], "rep", 1)
    return [parts[0], near, swap(add_parts(parts[2], far), "rep", 2)]


def per_device(master_weight, m_code, m_scale, v_code, v_scale, placement, route, x_rows, y_cot):
    local_count = master_weight.shape[0]
    row_count = x_rows.shape[0]
    expert_count = placement.shape[0]
    groups = lax.axis_size("grp")
    replicas = lax.axis_size("rep")
    grad_factor = float(row_count * groups * replicas // expert_count) ** (-0.5)
    capacity = max(2, (3 * row_count + 2 * expert_count - 1) // (2 * expert_count))
    places = expert_count * capacity
    sent, target = dispatch(route, placement, x_rows, y_cot, capacity, groups)
    local = exchange(sent, groups)
    early_master, target = lax.optimization_barrier((master_weight, target))
    weight = join_weight(gather_weight(cast_weight(early_master), replicas))
    results = products(local, weight, capacity, local_count)
    local, results = lax.optimization_barrier((local, results))
    home = exchange(results, groups)

    parts = replicas if replicas == 4 else 1
    hidden = x_rows.shape[1]
    grads = sum_gradient(gradient(local, hidden, capacity, local_count, parts, grad_factor))
    updated = adam(master_weight, grads, m_code, m_scale, v_code, v_scale)
    y_rows, x_grad = collect(target, home, hidden)
    return (y_rows, x_grad) + tuple(updated)


def solution(mesh):
    return jax.shard_map(
        per_device,
        mesh=mesh,
        in_specs=(
            P("grp", "rep", None),
            P("grp", "rep", None),
            P("grp", "rep", None),
            P("grp", "rep", None),
            P("grp", "rep", None),
            P(),
            P(("rep", "grp")),
            P(("rep", "grp"), None),
            P(("rep", "grp"), None),
        ),
        out_specs=(
            P(("rep", "grp"), None),
            P(("rep", "grp"), None),
            P("grp", "rep", None),
            P("grp", "rep", None),
            P("grp", "rep", None),
            P("grp", "rep", None),
            P("grp", "rep", None),
        ),
        check_vma=False,
    )
```

```python
import functools

import jax
import jax.numpy as jnp
from jax import lax
from jax.experimental import pallas as pl
from jax.experimental.pallas import tpu as pltpu
from jax.sharding import PartitionSpec as P

BLOCK = 128
ADAM_STEP = 100

beta_one = 0.9
beta_two = 0.95
learn_rate = 0.01

VMEM_LIMIT = 40 * 1024 * 1024
LARGE_LIMIT = 60 * 1024 * 1024 + 512 * 1024
F32 = jnp.float32
BF16 = jnp.bfloat16


def cost(flops, nbytes):
    return pl.CostEstimate(flops=int(flops), bytes_accessed=int(nbytes), transcendentals=0)


def params(*semantics):
    if semantics:
        return pltpu.CompilerParams(vmem_limit_bytes=VMEM_LIMIT, dimension_semantics=semantics)
    return pltpu.CompilerParams(vmem_limit_bytes=VMEM_LIMIT)


def order_of(device, groups):
    if groups % 4:
        return device
    half = groups // 2
    upper = device // half
    near = device + upper * (groups - 1 - 2 * device)
    place = near % 2 * (half // 2) + near // 2
    return place + (upper + place) % 2 * half


def row_targets(route_row, placement_row, capacity, groups):
    expert_count = placement_row.shape[1]
    row_count = route_row.shape[1]
    diagonal = lax.broadcasted_iota(jnp.int32, (expert_count, expert_count), 0) == (
        lax.broadcasted_iota(jnp.int32, (expert_count, expert_count), 1)
    )
    placement_col = jnp.sum(
        jnp.where(diagonal, placement_row, 0).astype(F32), axis=1, keepdims=True
    )
    hot = (placement_col == route_row.astype(F32)).astype(F32)
    earlier = lax.broadcasted_iota(jnp.int32, (row_count, row_count), 0)
    later = lax.broadcasted_iota(jnp.int32, (row_count, row_count), 1)
    before = (earlier < later).astype(F32).astype(BF16)
    position = jnp.dot(hot.astype(BF16), before, preferred_element_type=F32)
    slot = lax.broadcasted_iota(jnp.int32, (expert_count, row_count), 0)
    local_count = expert_count // groups
    order = order_of(slot // local_count, groups)
    start = ((order * local_count + slot % local_count) * capacity).astype(F32)
    return jnp.sum(hot * (start + position), axis=0, keepdims=True).astype(jnp.int32)


def place_matrix(target, places):
    slots = lax.broadcasted_iota(jnp.int32, (places, target.shape[1]), 0)
    return (slots == target).astype(F32).astype(BF16)


def dispatch_kernel(
    capacity, groups, route_hbm, placement_hbm, x_hbm, g_hbm, sent_hbm, target_hbm,
    route_ref, placement_ref, target_ref, x_ref, g_ref, sent_ref, key_sems, in_sems, out_sems,
):
    row_count, hidden = x_ref.shape
    width = g_ref.shape[1]
    tiles = out_sems.shape[0] - 1
    tile = width // tiles
    parts = in_sems.shape[0] - 1
    keys = [
        pltpu.make_async_copy(route_hbm, route_ref, key_sems.at[0]),
        pltpu.make_async_copy(placement_hbm, placement_ref, key_sems.at[1]),
    ]
    bands = [pl.ds(i * (row_count // parts), row_count // parts) for i in range(parts)]
    loads = [pltpu.make_async_copy(x_hbm, x_ref, in_sems.at[parts])] + [
        pltpu.make_async_copy(g_hbm.at[band], g_ref.at[band], in_sems.at[i])
        for i, band in enumerate(bands)
    ]
    for load in keys + loads:
        load.start()
    for load in keys:
        load.wait()
    target = row_targets(route_ref[...], placement_ref[...], capacity, groups)
    target_ref[...] = target
    stores = [pltpu.make_async_copy(target_ref, target_hbm, key_sems.at[2])]
    stores[0].start()
    places = place_matrix(target, sent_ref.shape[0])
    for j in range(tiles + 1):
        for load in loads[:1] if j == 0 else loads[1:] if j == 1 else []:
            load.wait()
        columns = pl.ds((j - 1) * tile, tile) if j else pl.ds(width, hidden)
        rows = g_ref[:, columns] if j else x_ref[...]
        sent_ref[:, columns] = jnp.dot(places, rows, preferred_element_type=F32).astype(BF16)
        store = pltpu.make_async_copy(
            sent_ref.at[:, columns], sent_hbm.at[:, columns], out_sems.at[j]
        )
        store.start()
        stores.append(store)
    for store in stores:
        store.wait()


def dispatch(route, placement, x_rows, y_cot, capacity, groups):
    row_count, hidden = x_rows.shape
    width = y_cot.shape[1]
    expert_count = placement.shape[0]
    tile = min(width, 512)
    tiles = width // tile
    parts = 4 if row_count % 64 == 0 else 1
    places = expert_count * capacity
    hbm = pl.BlockSpec(memory_space=pl.ANY)
    return pl.pallas_call(
        functools.partial(dispatch_kernel, capacity, groups),
        in_specs=[hbm, hbm, hbm, hbm],
        out_specs=(hbm, hbm),
        out_shape=(
            jax.ShapeDtypeStruct((places, width + hidden), BF16),
            jax.ShapeDtypeStruct((1, row_count), jnp.int32),
        ),
        scratch_shapes=[
            pltpu.VMEM((1, row_count), jnp.int32),
            pltpu.VMEM((1, expert_count), jnp.int32),
            pltpu.VMEM((1, row_count), jnp.int32),
            pltpu.VMEM((row_count, hidden), BF16),
            pltpu.VMEM((row_count, width), BF16),
            pltpu.VMEM((places, width + hidden), BF16),
            pltpu.SemaphoreType.DMA((3,)),
            pltpu.SemaphoreType.DMA((parts + 1,)),
            pltpu.SemaphoreType.DMA((tiles + 1,)),
        ],
        compiler_params=pltpu.CompilerParams(vmem_limit_bytes=LARGE_LIMIT),
        cost_estimate=cost(
            2 * places * row_count * (hidden + width), 2 * (places + row_count) * (hidden + width)
        ),
        name="dispatch",
    )(route.reshape(1, row_count), placement.reshape(1, -1), x_rows, y_cot)


def hidden_specs(rows, hidden, width):
    return [
        pl.BlockSpec((rows, BLOCK), functools.partial(lambda k, j: (0, k), width // BLOCK + i))
        for i in range(hidden // BLOCK)
    ]


def read_columns(refs):
    return jnp.concatenate([ref[...] for ref in refs], axis=1)


def collect_kernel(
    target_hbm, home_ref, y_hbm, dx_hbm, target_ref, y_ref, dx_ref, target_sem, out_sems
):
    hidden = dx_ref.shape[1]
    width = y_ref.shape[1]
    tiles = out_sems.shape[0] - 1
    tile = width // tiles
    spans = [pl.ds(j * tile, tile) for j in range(tiles)] + [pl.ds(width, hidden)]
    target_load = pltpu.make_async_copy(target_hbm, target_ref, target_sem)
    target_load.start()
    target_load.wait()
    target = target_ref[...]
    slots = lax.broadcasted_iota(jnp.int32, (home_ref.shape[0], target.shape[1]), 0)
    places = (slots == target).astype(F32).T.astype(BF16)
    stores = []
    for j, span in enumerate(spans):
        rows = jnp.dot(places, home_ref[:, span], preferred_element_type=F32).astype(BF16)
        if j < tiles:
            y_ref[:, span] = rows
            store = pltpu.make_async_copy(y_ref.at[:, span], y_hbm.at[:, span], out_sems.at[j])
        else:
            dx_ref[...] = rows
            store = pltpu.make_async_copy(dx_ref, dx_hbm, out_sems.at[j])
        store.start()
        stores.append(store)
    for store in stores:
        store.wait()


def collect(target, home, hidden):
    total, width = home.shape
    width -= hidden
    row_count = target.shape[1]
    tiles = width // min(width, 512)
    hbm = pl.BlockSpec(memory_space=pl.ANY)
    return pl.pallas_call(
        collect_kernel,
        in_specs=[hbm, pl.BlockSpec(memory_space=pltpu.VMEM)],
        out_specs=(hbm, hbm),
        out_shape=(
            jax.ShapeDtypeStruct((row_count, width), BF16),
            jax.ShapeDtypeStruct((row_count, hidden), BF16),
        ),
        scratch_shapes=[
            pltpu.VMEM(target.shape, jnp.int32),
            pltpu.VMEM((row_count, width), BF16),
            pltpu.VMEM((row_count, hidden), BF16),
            pltpu.SemaphoreType.DMA,
            pltpu.SemaphoreType.DMA((tiles + 1,)),
        ],
        compiler_params=params(),
        cost_estimate=cost(
            2 * total * row_count * (hidden + width), 2 * (total + row_count) * (hidden + width)
        ),
        name="collect",
    )(target, home)


def member_rows(rows, capacity, local_count):
    index = lax.broadcasted_iota(jnp.int32, (rows, 1), 0)
    return lax.rem(index, capacity * local_count) // capacity


def spread(x, capacity, local_count):
    member = member_rows(x.shape[0], capacity, local_count)
    zero = jnp.zeros_like(x)
    return jnp.concatenate([jnp.where(member == e, x, zero) for e in range(local_count)], axis=1)


def join_kernel(*refs):
    piece_refs, out_ref = refs[:-1], refs[-1]
    pieces = len(piece_refs)
    here = lax.axis_index("rep") if pieces > 1 else 0
    for i, ref in enumerate(piece_refs):
        owner = jnp.bitwise_xor(here, i) if pieces > 1 else 0
        for e in range(out_ref.shape[1]):
            out_ref[0, e, owner] = ref[e]


def join_weight(weight):
    local_count, rows, width = weight[0].shape
    pieces = len(weight)
    tile = min(width, 512)
    tiles = width // tile
    joined = pl.pallas_call(
        join_kernel,
        grid=(tiles,),
        in_specs=[pl.BlockSpec((local_count, rows, tile), lambda j: (0, 0, j))] * pieces,
        out_specs=pl.BlockSpec((1, local_count, pieces, rows, tile), lambda j: (j, 0, 0, 0, 0)),
        out_shape=jax.ShapeDtypeStruct((tiles, local_count, pieces, rows, tile), BF16),
        compiler_params=pltpu.CompilerParams(
            vmem_limit_bytes=LARGE_LIMIT, dimension_semantics=("arbitrary",)
        ),
        cost_estimate=cost(0, 4 * local_count * pieces * rows * width),
        name="join_weight",
    )(*weight)
    return joined.reshape(tiles, local_count * pieces * rows, tile)


def member_parts(value, capacity, local_count):
    rows, width = value.shape
    groups = rows // (capacity * local_count)
    parts = value.astype(F32).reshape(groups, local_count, capacity, width)
    return [
        parts[:, e].reshape(groups * capacity, width).astype(BF16) for e in range(local_count)
    ]


def join_members(parts, capacity):
    groups = parts[0].shape[0] // capacity
    width = parts[0].shape[1]
    stacked = [part.reshape(groups, 1, capacity, width) for part in parts]
    joined = jnp.concatenate(stacked, axis=1)
    return joined.reshape(groups * len(parts) * capacity, width)


def pick_members(totals, capacity):
    member = member_rows(totals[0].shape[0], capacity, len(totals))
    picked = totals[0]
    for e in range(1, len(totals)):
        picked = jnp.where(member == e, totals[e], picked)
    return picked


def products_kernel(
    capacity, apart, local_hbm, w_hbm, out_hbm,
    local_ref, w_ref, x_ref, total_ref, out_ref, local_sem, w_sems, out_sems,
):
    step = pl.program_id(0)
    steps, _, tile = w_ref.shape
    local_count, _, hidden = total_ref.shape
    columns = pl.ds(pl.multiple_of(step * tile, tile), tile)

    def weight_load(j):
        return pltpu.make_async_copy(w_hbm.at[j], w_ref.at[j], w_sems.at[j])

    @pl.when(step == 0)
    def _():
        local_load = pltpu.make_async_copy(local_hbm, local_ref, local_sem)
        local_load.start()
        weight_load(0).start()
        total_ref[...] = jnp.zeros_like(total_ref)
        local_load.wait()
        for j in range(1, steps):
            weight_load(j).start()
        x = local_ref[:, steps * tile :]
        for e, part in enumerate(member_parts(x, capacity, local_count) if apart else [x]):
            x_ref[e] = part

    weight_load(step).wait()
    weights = [w_ref[step, e * hidden : (e + 1) * hidden] for e in range(local_count)]
    xs = [x_ref[e if apart else 0] for e in range(local_count)]
    ys = [jnp.dot(x, w, preferred_element_type=F32) for x, w in zip(xs, weights)]
    y = join_members(ys, capacity) if apart else pick_members(ys, capacity)
    out_ref[:, columns] = y.astype(BF16)
    pltpu.make_async_copy(
        out_ref.at[:, columns], out_hbm.at[:, columns], out_sems.at[step]
    ).start()
    g = local_ref[:, columns]
    gs = member_parts(g, capacity, local_count) if apart else [g] * local_count
    for e in range(local_count):
        total_ref[e] += lax.dot_general(
            gs[e], weights[e], (((1,), (1,)), ((), ())), preferred_element_type=F32
        )

    @pl.when(step == steps - 1)
    def _():
        totals = [total_ref[e] for e in range(local_count)]
        dx = join_members(totals, capacity) if apart else pick_members(totals, capacity)
        last = pl.ds(steps * tile, hidden)
        out_ref[:, last] = dx.astype(BF16)
        final = pltpu.make_async_copy(out_ref.at[:, last], out_hbm.at[:, last], out_sems.at[steps])
        final.start()
        for j in range(steps):
            span = pl.ds(j * tile, tile)
            pltpu.make_async_copy(out_ref.at[:, span], out_hbm.at[:, span], out_sems.at[j]).wait()
        final.wait()


def products(local, weight, capacity, local_count):
    tiles, wide, tile = weight.shape
    width = tiles * tile
    total = local.shape[0]
    hidden = wide // local_count
    apart = capacity % 8 == 0
    rows = total // local_count if apart else total
    hbm = pl.BlockSpec(memory_space=pl.ANY)
    return pl.pallas_call(
        functools.partial(products_kernel, capacity, apart),
        grid=(tiles,),
        in_specs=[hbm, hbm],
        out_specs=hbm,
        out_shape=jax.ShapeDtypeStruct(local.shape, BF16),
        scratch_shapes=[
            pltpu.VMEM(local.shape, BF16),
            pltpu.VMEM(weight.shape, BF16),
            pltpu.VMEM((local_count if apart else 1, rows, hidden), BF16),
            pltpu.VMEM((local_count, rows, hidden), F32),
            pltpu.VMEM(local.shape, BF16),
            pltpu.SemaphoreType.DMA,
            pltpu.SemaphoreType.DMA((tiles,)),
            pltpu.SemaphoreType.DMA((tiles + 1,)),
        ],
        compiler_params=pltpu.CompilerParams(
            vmem_limit_bytes=LARGE_LIMIT, dimension_semantics=("arbitrary",)
        ),
        cost_estimate=cost(4 * rows * wide * width, 2 * (wide + 2 * total) * width),
        name="products",
    )(local, weight)


def gradient_kernel(capacity, local_count, parts, factor, g_ref, *refs):
    blocks = len(refs) - 2 - (parts if parts > 1 else 0)
    x_refs, wide_ref = refs[:blocks], refs[-1]
    out_refs = refs[blocks:-2] if parts > 1 else refs[blocks:-1]

    @pl.when(pl.program_id(0) == 0)
    def _():
        wide_ref[...] = spread(read_columns(x_refs), capacity, local_count)

    outer = lax.dot_general(
        wide_ref[...], g_ref[...], (((0,), (0,)), ((), ())), preferred_element_type=F32
    )
    low = (outer * factor).astype(BF16)
    if parts == 1:
        out_refs[0][...] = low.reshape(out_refs[0].shape)
        return
    split_ref = refs[-2]
    split_ref[...] = low.reshape(split_ref.shape)
    here = lax.axis_index("rep")
    for i, out_ref in enumerate(out_refs):
        owner = jnp.bitwise_xor(here, i)
        for e in range(local_count):
            out_ref[e] = split_ref[e, owner]


def gradient(local, hidden, capacity, local_count, parts, factor):
    total, width = local.shape
    width -= hidden
    tile = min(width, 512)
    slice_rows = hidden // parts
    specs = hidden_specs(total, hidden, width)
    split = [pltpu.VMEM((local_count, parts, slice_rows, tile), BF16)] if parts > 1 else []
    return list(pl.pallas_call(
        functools.partial(gradient_kernel, capacity, local_count, parts, factor),
        grid=(width // tile,),
        in_specs=[pl.BlockSpec((total, tile), lambda j: (0, j))] + specs,
        out_specs=(pl.BlockSpec((local_count, slice_rows, tile), lambda j: (0, 0, j)),) * parts,
        out_shape=(jax.ShapeDtypeStruct((local_count, slice_rows, width), BF16),) * parts,
        scratch_shapes=split + [pltpu.VMEM((total, local_count * hidden), BF16)],
        compiler_params=pltpu.CompilerParams(
            vmem_limit_bytes=LARGE_LIMIT, dimension_semantics=("arbitrary",)
        ),
        cost_estimate=cost(
            2 * total * local_count * hidden * width,
            2 * (local_count * hidden + total) * width,
        ),
        name="gradient",
    )(*([local] * (1 + len(specs)))))


def cast_kernel(w_ref, out_ref):
    out_ref[...] = w_ref[...].astype(BF16)


def cast_weight(weight):
    members, rows, width = weight.shape
    tile = min(width, 512)
    spec = pl.BlockSpec((members, rows, tile), lambda j: (0, 0, j))
    return pl.pallas_call(
        cast_kernel,
        grid=(width // tile,),
        in_specs=[spec],
        out_specs=spec,
        out_shape=jax.ShapeDtypeStruct(weight.shape, BF16),
        compiler_params=params("arbitrary"),
        cost_estimate=cost(weight.size, 6 * weight.size),
        name="cast_weight",
    )(weight)


def add_kernel(a_ref, b_ref, out_ref):
    out_ref[...] = (a_ref[...].astype(F32) + b_ref[...].astype(F32)).astype(BF16)


def add_parts(a, b):
    members, rows, width = a.shape
    tile = min(width, 1024)
    spec = pl.BlockSpec((members, rows, tile), lambda j: (0, 0, j))
    return pl.pallas_call(
        add_kernel,
        grid=(width // tile,),
        in_specs=[spec, spec],
        out_specs=spec,
        out_shape=jax.ShapeDtypeStruct(a.shape, BF16),
        compiler_params=params("arbitrary"),
        cost_estimate=cost(a.size, 6 * a.size),
        name="add_parts",
    )(a, b)


def adam_kernel(
    parts, master_ref, mc_ref, ms_ref, vc_ref, vs_ref, *refs
):
    grad_refs = refs[:parts]
    master_out, mc_out, ms_out, vc_out, vs_out = refs[parts:]
    blocks = ms_ref.shape[1]
    rows = ms_ref.shape[2]
    corr_one = 1.0 - beta_one**ADAM_STEP
    corr_two = 1.0 - beta_two**ADAM_STEP
    m_scales = (ms_ref[0] * beta_one).T
    v_scales = (vs_ref[0] * beta_two).T
    lane = lax.broadcasted_iota(jnp.int32, (rows, blocks), 1)
    m_tops = jnp.zeros((rows, blocks), F32)
    v_tops = jnp.zeros((rows, blocks), F32)
    for b in range(blocks):
        cols = slice(b * BLOCK, (b + 1) * BLOCK)
        grad = grad_refs[0][0, :, cols].astype(F32)
        for ref in grad_refs[1:]:
            grad = grad + ref[0, :, cols].astype(F32)
        m_next = mc_ref[0, :, cols].astype(F32) * m_scales[:, b : b + 1] + (1.0 - beta_one) * grad
        v_next = vc_ref[0, :, cols].astype(F32) * v_scales[:, b : b + 1] + (
            1.0 - beta_two
        ) * (grad * grad)
        v_hat = v_next * (1.0 / corr_two)
        root = v_hat * lax.rsqrt(v_hat) + 1e-08
        master_out[0, :, cols] = master_ref[0, :, cols] - (learn_rate / corr_one) * m_next / root
        m_top = jnp.max(jnp.abs(m_next), axis=-1, keepdims=True) + 1e-06
        v_top = jnp.max(v_next, axis=-1, keepdims=True) + 1e-06
        mc_out[0, :, cols] = (m_next * (1.0 / m_top)).astype(BF16)
        vc_out[0, :, cols] = (v_next * (1.0 / v_top)).astype(BF16)
        m_tops = jnp.where(lane == b, m_top, m_tops)
        v_tops = jnp.where(lane == b, v_top, v_tops)
    ms_out[0] = m_tops.T
    vs_out[0] = v_tops.T


def adam(master_weight, grads, m_code, m_scale, v_code, v_scale):
    members, rows, width = master_weight.shape
    blocks = m_scale.shape[-1]
    count = 8 if blocks % 8 == 0 else blocks
    big = pl.BlockSpec((1, rows, count * BLOCK), lambda e, j: (e, 0, j))
    small = pl.BlockSpec((1, count, rows), lambda e, j: (e, j, 0))
    scales = jax.ShapeDtypeStruct((members, blocks, rows), F32)
    master_next, m_code_next, m_scale_next, v_code_next, v_scale_next = pl.pallas_call(
        functools.partial(adam_kernel, len(grads)),
        grid=(members, blocks // count),
        in_specs=[big, big, small, big, small] + [big] * len(grads),
        out_specs=(big, big, small, big, small),
        out_shape=(
            jax.ShapeDtypeStruct(master_weight.shape, F32),
            jax.ShapeDtypeStruct(master_weight.shape, BF16),
            scales,
            jax.ShapeDtypeStruct(master_weight.shape, BF16),
            scales,
        ),
        compiler_params=params("arbitrary", "arbitrary"),
        cost_estimate=cost(40 * master_weight.size, 18 * master_weight.size),
        name="adam",
    )(master_weight, m_code, jnp.swapaxes(m_scale, 1, 2), v_code, jnp.swapaxes(v_scale, 1, 2), *grads)
    return (
        master_next,
        m_code_next,
        jnp.swapaxes(m_scale_next, 1, 2),
        v_code_next,
        jnp.swapaxes(v_scale_next, 1, 2),
    )


def swap(array, axis, offset):
    size = lax.axis_size(axis)
    return lax.ppermute(array, axis, [(i, i ^ offset) for i in range(size)])


def exchange(buffer, groups):
    places, width = buffer.shape
    parts = buffer.reshape(groups, places // groups, width)
    members = sorted(range(groups), key=lambda device: order_of(device, groups))
    moved = lax.all_to_all(
        parts, "grp", split_axis=0, concat_axis=0, tiled=True, axis_index_groups=[members]
    )
    return moved.reshape(places, width)


def gather_weight(weight_slice, replicas):
    if replicas != 4:
        return [lax.all_gather(weight_slice, "rep", axis=1, tiled=True)]
    far = swap(weight_slice, "rep", 2)
    near = swap(weight_slice, "rep", 1)
    return [weight_slice, near, far, swap(far, "rep", 1)]


def sum_gradient(parts):
    if len(parts) != 4:
        return [lax.psum_scatter(parts[0], "rep", scatter_dimension=1, tiled=True)]
    far = swap(parts[3], "rep", 1)
    near = swap(parts[1], "rep", 1)
    return [parts[0], near, swap(add_parts(parts[2], far), "rep", 2)]


def per_device(master_weight, m_code, m_scale, v_code, v_scale, placement, route, x_rows, y_cot):
    local_count = master_weight.shape[0]
    row_count = x_rows.shape[0]
    expert_count = placement.shape[0]
    groups = lax.axis_size("grp")
    replicas = lax.axis_size("rep")
    grad_factor = float(row_count * groups * replicas // expert_count) ** (-0.5)
    capacity = max(2, (3 * row_count + 2 * expert_count - 1) // (2 * expert_count))
    places = expert_count * capacity
    sent, target = dispatch(route, placement, x_rows, y_cot, capacity, groups)
    local = exchange(sent, groups)
    early_master, target = lax.optimization_barrier((master_weight, target))
    weight = join_weight(gather_weight(cast_weight(early_master), replicas))
    results = products(local, weight, capacity, local_count)
    local, results = lax.optimization_barrier((local, results))
    home = exchange(results, groups)

    parts = replicas if replicas == 4 else 1
    hidden = x_rows.shape[1]
    grads = sum_gradient(gradient(local, hidden, capacity, local_count, parts, grad_factor))
    updated = adam(master_weight, grads, m_code, m_scale, v_code, v_scale)
    y_rows, x_grad = collect(target, home, hidden)
    return (y_rows, x_grad) + tuple(updated)


def solution(mesh):
    return jax.shard_map(
        per_device,
        mesh=mesh,
        in_specs=(
            P("grp", "rep", None),
            P("grp", "rep", None),
            P("grp", "rep", None),
            P("grp", "rep", None),
            P("grp", "rep", None),
            P(),
            P(("rep", "grp")),
            P(("rep", "grp"), None),
            P(("rep", "grp"), None),
        ),
        out_specs=(
            P(("rep", "grp"), None),
            P(("rep", "grp"), None),
            P("grp", "rep", None),
            P("grp", "rep", None),
            P("grp", "rep", None),
            P("grp", "rep", None),
            P("grp", "rep", None),
        ),
        check_vma=False,
    )
```

```python
import functools

import jax
import jax.numpy as jnp
from jax import lax
from jax.experimental import pallas as pl
from jax.experimental.pallas import tpu as pltpu
from jax.sharding import PartitionSpec as P

BLOCK = 128
ADAM_STEP = 100

beta_one = 0.9
beta_two = 0.95
learn_rate = 0.01

VMEM_LIMIT = 40 * 1024 * 1024
LARGE_LIMIT = 60 * 1024 * 1024 + 512 * 1024
F32 = jnp.float32
BF16 = jnp.bfloat16


def cost(flops, nbytes):
    return pl.CostEstimate(flops=int(flops), bytes_accessed=int(nbytes), transcendentals=0)


def params(*semantics):
    if semantics:
        return pltpu.CompilerParams(vmem_limit_bytes=VMEM_LIMIT, dimension_semantics=semantics)
    return pltpu.CompilerParams(vmem_limit_bytes=VMEM_LIMIT)


def order_of(device, groups):
    if groups % 2:
        return device
    half = groups // 2
    upper = device // half
    near = device + upper * (groups - 1 - 2 * device)
    return near + (upper + near) % 2 * half


def row_targets(route_row, placement_row, capacity, groups):
    expert_count = placement_row.shape[1]
    row_count = route_row.shape[1]
    diagonal = lax.broadcasted_iota(jnp.int32, (expert_count, expert_count), 0) == (
        lax.broadcasted_iota(jnp.int32, (expert_count, expert_count), 1)
    )
    placement_col = jnp.sum(
        jnp.where(diagonal, placement_row, 0).astype(F32), axis=1, keepdims=True
    )
    hot = (placement_col == route_row.astype(F32)).astype(F32)
    earlier = lax.broadcasted_iota(jnp.int32, (row_count, row_count), 0)
    later = lax.broadcasted_iota(jnp.int32, (row_count, row_count), 1)
    before = (earlier < later).astype(F32).astype(BF16)
    position = jnp.dot(hot.astype(BF16), before, preferred_element_type=F32)
    slot = lax.broadcasted_iota(jnp.int32, (expert_count, row_count), 0)
    local_count = expert_count // groups
    order = order_of(slot // local_count, groups)
    start = ((order * local_count + slot % local_count) * capacity).astype(F32)
    return jnp.sum(hot * (start + position), axis=0, keepdims=True).astype(jnp.int32)


def place_matrix(target, places):
    slots = lax.broadcasted_iota(jnp.int32, (places, target.shape[1]), 0)
    return (slots == target).astype(F32).astype(BF16)


def dispatch_kernel(
    capacity, groups, route_hbm, placement_hbm, x_hbm, g_hbm, sent_hbm, target_hbm,
    route_ref, placement_ref, target_ref, x_ref, g_ref, sent_ref, key_sems, in_sems, out_sems,
):
    row_count, hidden = x_ref.shape
    width = g_ref.shape[1]
    tiles = out_sems.shape[0] - 1
    tile = width // tiles
    parts = in_sems.shape[0] - 1
    keys = [
        pltpu.make_async_copy(route_hbm, route_ref, key_sems.at[0]),
        pltpu.make_async_copy(placement_hbm, placement_ref, key_sems.at[1]),
    ]
    bands = [pl.ds(i * (row_count // parts), row_count // parts) for i in range(parts)]
    loads = [pltpu.make_async_copy(x_hbm, x_ref, in_sems.at[parts])] + [
        pltpu.make_async_copy(g_hbm.at[band], g_ref.at[band], in_sems.at[i])
        for i, band in enumerate(bands)
    ]
    for load in keys + loads:
        load.start()
    for load in keys:
        load.wait()
    target = row_targets(route_ref[...], placement_ref[...], capacity, groups)
    target_ref[...] = target
    stores = [pltpu.make_async_copy(target_ref, target_hbm, key_sems.at[2])]
    stores[0].start()
    places = place_matrix(target, sent_ref.shape[0])
    for j in range(tiles + 1):
        for load in loads[:1] if j == 0 else loads[1:] if j == 1 else []:
            load.wait()
        columns = pl.ds((j - 1) * tile, tile) if j else pl.ds(width, hidden)
        rows = g_ref[:, columns] if j else x_ref[...]
        sent_ref[:, columns] = jnp.dot(places, rows, preferred_element_type=F32).astype(BF16)
        store = pltpu.make_async_copy(
            sent_ref.at[:, columns], sent_hbm.at[:, columns], out_sems.at[j]
        )
        store.start()
        stores.append(store)
    for store in stores:
        store.wait()


def dispatch(route, placement, x_rows, y_cot, capacity, groups):
    row_count, hidden = x_rows.shape
    width = y_cot.shape[1]
    expert_count = placement.shape[0]
    tile = min(width, 512)
    tiles = width // tile
    parts = 4 if row_count % 64 == 0 else 1
    places = expert_count * capacity
    hbm = pl.BlockSpec(memory_space=pl.ANY)
    return pl.pallas_call(
        functools.partial(dispatch_kernel, capacity, groups),
        in_specs=[hbm, hbm, hbm, hbm],
        out_specs=(hbm, hbm),
        out_shape=(
            jax.ShapeDtypeStruct((places, width + hidden), BF16),
            jax.ShapeDtypeStruct((1, row_count), jnp.int32),
        ),
        scratch_shapes=[
            pltpu.VMEM((1, row_count), jnp.int32),
            pltpu.VMEM((1, expert_count), jnp.int32),
            pltpu.VMEM((1, row_count), jnp.int32),
            pltpu.VMEM((row_count, hidden), BF16),
            pltpu.VMEM((row_count, width), BF16),
            pltpu.VMEM((places, width + hidden), BF16),
            pltpu.SemaphoreType.DMA((3,)),
            pltpu.SemaphoreType.DMA((parts + 1,)),
            pltpu.SemaphoreType.DMA((tiles + 1,)),
        ],
        compiler_params=pltpu.CompilerParams(vmem_limit_bytes=LARGE_LIMIT),
        cost_estimate=cost(
            2 * places * row_count * (hidden + width), 2 * (places + row_count) * (hidden + width)
        ),
        name="dispatch",
    )(route.reshape(1, row_count), placement.reshape(1, -1), x_rows, y_cot)


def hidden_specs(rows, hidden, width):
    return [
        pl.BlockSpec((rows, BLOCK), functools.partial(lambda k, j: (0, k), width // BLOCK + i))
        for i in range(hidden // BLOCK)
    ]


def read_columns(refs):
    return jnp.concatenate([ref[...] for ref in refs], axis=1)


def collect_kernel(
    target_hbm, home_ref, y_hbm, dx_hbm, target_ref, y_ref, dx_ref, target_sem, out_sems
):
    hidden = dx_ref.shape[1]
    width = y_ref.shape[1]
    tiles = out_sems.shape[0] - 1
    tile = width // tiles
    spans = [pl.ds(j * tile, tile) for j in range(tiles)] + [pl.ds(width, hidden)]
    target_load = pltpu.make_async_copy(target_hbm, target_ref, target_sem)
    target_load.start()
    target_load.wait()
    target = target_ref[...]
    slots = lax.broadcasted_iota(jnp.int32, (home_ref.shape[0], target.shape[1]), 0)
    places = (slots == target).astype(F32).T.astype(BF16)
    stores = []
    for j, span in enumerate(spans):
        rows = jnp.dot(places, home_ref[:, span], preferred_element_type=F32).astype(BF16)
        if j < tiles:
            y_ref[:, span] = rows
            store = pltpu.make_async_copy(y_ref.at[:, span], y_hbm.at[:, span], out_sems.at[j])
        else:
            dx_ref[...] = rows
            store = pltpu.make_async_copy(dx_ref, dx_hbm, out_sems.at[j])
        store.start()
        stores.append(store)
    for store in stores:
        store.wait()


def collect(target, home, hidden):
    total, width = home.shape
    width -= hidden
    row_count = target.shape[1]
    tiles = width // min(width, 512)
    hbm = pl.BlockSpec(memory_space=pl.ANY)
    return pl.pallas_call(
        collect_kernel,
        in_specs=[hbm, pl.BlockSpec(memory_space=pltpu.VMEM)],
        out_specs=(hbm, hbm),
        out_shape=(
            jax.ShapeDtypeStruct((row_count, width), BF16),
            jax.ShapeDtypeStruct((row_count, hidden), BF16),
        ),
        scratch_shapes=[
            pltpu.VMEM(target.shape, jnp.int32),
            pltpu.VMEM((row_count, width), BF16),
            pltpu.VMEM((row_count, hidden), BF16),
            pltpu.SemaphoreType.DMA,
            pltpu.SemaphoreType.DMA((tiles + 1,)),
        ],
        compiler_params=params(),
        cost_estimate=cost(
            2 * total * row_count * (hidden + width), 2 * (total + row_count) * (hidden + width)
        ),
        name="collect",
    )(target, home)


def member_rows(rows, capacity, local_count):
    index = lax.broadcasted_iota(jnp.int32, (rows, 1), 0)
    return lax.rem(index, capacity * local_count) // capacity


def spread(x, capacity, local_count):
    member = member_rows(x.shape[0], capacity, local_count)
    zero = jnp.zeros_like(x)
    return jnp.concatenate([jnp.where(member == e, x, zero) for e in range(local_count)], axis=1)


def join_kernel(*refs):
    piece_refs, out_ref = refs[:-1], refs[-1]
    pieces = len(piece_refs)
    here = lax.axis_index("rep") if pieces > 1 else 0
    for i, ref in enumerate(piece_refs):
        owner = jnp.bitwise_xor(here, i) if pieces > 1 else 0
        for e in range(out_ref.shape[1]):
            out_ref[0, e, owner] = ref[e]


def join_weight(weight):
    local_count, rows, width = weight[0].shape
    pieces = len(weight)
    tile = min(width, 512)
    tiles = width // tile
    joined = pl.pallas_call(
        join_kernel,
        grid=(tiles,),
        in_specs=[pl.BlockSpec((local_count, rows, tile), lambda j: (0, 0, j))] * pieces,
        out_specs=pl.BlockSpec((1, local_count, pieces, rows, tile), lambda j: (j, 0, 0, 0, 0)),
        out_shape=jax.ShapeDtypeStruct((tiles, local_count, pieces, rows, tile), BF16),
        compiler_params=pltpu.CompilerParams(
            vmem_limit_bytes=LARGE_LIMIT, dimension_semantics=("arbitrary",)
        ),
        cost_estimate=cost(0, 4 * local_count * pieces * rows * width),
        name="join_weight",
    )(*weight)
    return joined.reshape(tiles, local_count * pieces * rows, tile)


def member_parts(value, capacity, local_count):
    rows, width = value.shape
    groups = rows // (capacity * local_count)
    parts = value.astype(F32).reshape(groups, local_count, capacity, width)
    return [
        parts[:, e].reshape(groups * capacity, width).astype(BF16) for e in range(local_count)
    ]


def join_members(parts, capacity):
    groups = parts[0].shape[0] // capacity
    width = parts[0].shape[1]
    stacked = [part.reshape(groups, 1, capacity, width) for part in parts]
    joined = jnp.concatenate(stacked, axis=1)
    return joined.reshape(groups * len(parts) * capacity, width)


def pick_members(totals, capacity):
    member = member_rows(totals[0].shape[0], capacity, len(totals))
    picked = totals[0]
    for e in range(1, len(totals)):
        picked = jnp.where(member == e, totals[e], picked)
    return picked


def products_kernel(
    capacity, apart, local_hbm, w_hbm, out_hbm,
    local_ref, w_ref, x_ref, total_ref, out_ref, local_sems, w_sems, out_sems,
):
    step = pl.program_id(0)
    steps, _, tile = w_ref.shape
    local_count, _, hidden = total_ref.shape
    columns = pl.ds(pl.multiple_of(step * tile, tile), tile)

    def weight_load(j):
        return pltpu.make_async_copy(w_hbm.at[j], w_ref.at[j], w_sems.at[j])

    @pl.when(step == 0)
    def _():
        bands = local_sems.shape[0]
        rows = local_ref.shape[0] // bands
        local_loads = [
            pltpu.make_async_copy(
                local_hbm.at[pl.ds(i * rows, rows)],
                local_ref.at[pl.ds(i * rows, rows)],
                local_sems.at[i],
            )
            for i in range(bands)
        ]
        for load in local_loads:
            load.start()
        weight_load(0).start()
        total_ref[...] = jnp.zeros_like(total_ref)
        for load in local_loads:
            load.wait()
        for j in range(1, steps):
            weight_load(j).start()
        x = local_ref[:, steps * tile :]
        for e, part in enumerate(member_parts(x, capacity, local_count) if apart else [x]):
            x_ref[e] = part

    weight_load(step).wait()
    weights = [w_ref[step, e * hidden : (e + 1) * hidden] for e in range(local_count)]
    xs = [x_ref[e if apart else 0] for e in range(local_count)]
    ys = [jnp.dot(x, w, preferred_element_type=F32) for x, w in zip(xs, weights)]
    y = join_members(ys, capacity) if apart else pick_members(ys, capacity)
    out_ref[:, columns] = y.astype(BF16)
    pltpu.make_async_copy(
        out_ref.at[:, columns], out_hbm.at[:, columns], out_sems.at[step]
    ).start()
    g = local_ref[:, columns]
    gs = member_parts(g, capacity, local_count) if apart else [g] * local_count
    for e in range(local_count):
        total_ref[e] += lax.dot_general(
            gs[e], weights[e], (((1,), (1,)), ((), ())), preferred_element_type=F32
        )

    @pl.when(step == steps - 1)
    def _():
        totals = [total_ref[e] for e in range(local_count)]
        dx = join_members(totals, capacity) if apart else pick_members(totals, capacity)
        last = pl.ds(steps * tile, hidden)
        out_ref[:, last] = dx.astype(BF16)
        final = pltpu.make_async_copy(out_ref.at[:, last], out_hbm.at[:, last], out_sems.at[steps])
        final.start()
        for j in range(steps):
            span = pl.ds(j * tile, tile)
            pltpu.make_async_copy(out_ref.at[:, span], out_hbm.at[:, span], out_sems.at[j]).wait()
        final.wait()


def products(local, weight, capacity, local_count):
    tiles, wide, tile = weight.shape
    width = tiles * tile
    total = local.shape[0]
    hidden = wide // local_count
    apart = capacity % 8 == 0
    rows = total // local_count if apart else total
    hbm = pl.BlockSpec(memory_space=pl.ANY)
    return pl.pallas_call(
        functools.partial(products_kernel, capacity, apart),
        grid=(tiles,),
        in_specs=[hbm, hbm],
        out_specs=hbm,
        out_shape=jax.ShapeDtypeStruct(local.shape, BF16),
        scratch_shapes=[
            pltpu.VMEM(local.shape, BF16),
            pltpu.VMEM(weight.shape, BF16),
            pltpu.VMEM((local_count if apart else 1, rows, hidden), BF16),
            pltpu.VMEM((local_count, rows, hidden), F32),
            pltpu.VMEM(local.shape, BF16),
            pltpu.SemaphoreType.DMA((4 if total % 64 == 0 else 1,)),
            pltpu.SemaphoreType.DMA((tiles,)),
            pltpu.SemaphoreType.DMA((tiles + 1,)),
        ],
        compiler_params=pltpu.CompilerParams(
            vmem_limit_bytes=LARGE_LIMIT, dimension_semantics=("arbitrary",)
        ),
        cost_estimate=cost(4 * rows * wide * width, 2 * (wide + 2 * total) * width),
        name="products",
    )(local, weight)


def gradient_kernel(capacity, local_count, parts, factor, g_ref, *refs):
    blocks = len(refs) - 2 - (parts if parts > 1 else 0)
    x_refs, wide_ref = refs[:blocks], refs[-1]
    out_refs = refs[blocks:-2] if parts > 1 else refs[blocks:-1]

    @pl.when(pl.program_id(0) == 0)
    def _():
        wide_ref[...] = spread(read_columns(x_refs), capacity, local_count)

    outer = lax.dot_general(
        wide_ref[...], g_ref[...], (((0,), (0,)), ((), ())), preferred_element_type=F32
    )
    low = (outer * factor).astype(BF16)
    if parts == 1:
        out_refs[0][...] = low.reshape(out_refs[0].shape)
        return
    split_ref = refs[-2]
    split_ref[...] = low.reshape(split_ref.shape)
    here = lax.axis_index("rep")
    for i, out_ref in enumerate(out_refs):
        owner = jnp.bitwise_xor(here, i)
        for e in range(local_count):
            out_ref[e] = split_ref[e, owner]


def gradient(local, hidden, capacity, local_count, parts, factor):
    total, width = local.shape
    width -= hidden
    tile = min(width, 512)
    slice_rows = hidden // parts
    specs = hidden_specs(total, hidden, width)
    split = [pltpu.VMEM((local_count, parts, slice_rows, tile), BF16)] if parts > 1 else []
    return list(pl.pallas_call(
        functools.partial(gradient_kernel, capacity, local_count, parts, factor),
        grid=(width // tile,),
        in_specs=[pl.BlockSpec((total, tile), lambda j: (0, j))] + specs,
        out_specs=(pl.BlockSpec((local_count, slice_rows, tile), lambda j: (0, 0, j)),) * parts,
        out_shape=(jax.ShapeDtypeStruct((local_count, slice_rows, width), BF16),) * parts,
        scratch_shapes=split + [pltpu.VMEM((total, local_count * hidden), BF16)],
        compiler_params=pltpu.CompilerParams(
            vmem_limit_bytes=LARGE_LIMIT, dimension_semantics=("arbitrary",)
        ),
        cost_estimate=cost(
            2 * total * local_count * hidden * width,
            2 * (local_count * hidden + total) * width,
        ),
        name="gradient",
    )(*([local] * (1 + len(specs)))))


def cast_kernel(w_ref, out_ref):
    out_ref[...] = w_ref[...].astype(BF16)


def cast_weight(weight):
    members, rows, width = weight.shape
    tile = min(width, 512)
    spec = pl.BlockSpec((members, rows, tile), lambda j: (0, 0, j))
    return pl.pallas_call(
        cast_kernel,
        grid=(width // tile,),
        in_specs=[spec],
        out_specs=spec,
        out_shape=jax.ShapeDtypeStruct(weight.shape, BF16),
        compiler_params=params("arbitrary"),
        cost_estimate=cost(weight.size, 6 * weight.size),
        name="cast_weight",
    )(weight)


def add_kernel(a_ref, b_ref, out_ref):
    out_ref[...] = (a_ref[...].astype(F32) + b_ref[...].astype(F32)).astype(BF16)


def add_parts(a, b):
    members, rows, width = a.shape
    tile = min(width, 1024)
    spec = pl.BlockSpec((members, rows, tile), lambda j: (0, 0, j))
    return pl.pallas_call(
        add_kernel,
        grid=(width // tile,),
        in_specs=[spec, spec],
        out_specs=spec,
        out_shape=jax.ShapeDtypeStruct(a.shape, BF16),
        compiler_params=params("arbitrary"),
        cost_estimate=cost(a.size, 6 * a.size),
        name="add_parts",
    )(a, b)


def adam_kernel(
    parts, master_ref, mc_ref, ms_ref, vc_ref, vs_ref, *refs
):
    grad_refs = refs[:parts]
    master_out, mc_out, ms_out, vc_out, vs_out = refs[parts:]
    blocks = ms_ref.shape[1]
    rows = ms_ref.shape[2]
    corr_one = 1.0 - beta_one**ADAM_STEP
    corr_two = 1.0 - beta_two**ADAM_STEP
    m_scales = (ms_ref[0] * beta_one).T
    v_scales = (vs_ref[0] * beta_two).T
    lane = lax.broadcasted_iota(jnp.int32, (rows, blocks), 1)
    m_tops = jnp.zeros((rows, blocks), F32)
    v_tops = jnp.zeros((rows, blocks), F32)
    for b in range(blocks):
        cols = slice(b * BLOCK, (b + 1) * BLOCK)
        grad = grad_refs[0][0, :, cols].astype(F32)
        for ref in grad_refs[1:]:
            grad = grad + ref[0, :, cols].astype(F32)
        m_next = mc_ref[0, :, cols].astype(F32) * m_scales[:, b : b + 1] + (1.0 - beta_one) * grad
        v_next = vc_ref[0, :, cols].astype(F32) * v_scales[:, b : b + 1] + (
            1.0 - beta_two
        ) * (grad * grad)
        v_hat = v_next * (1.0 / corr_two)
        root = v_hat * lax.rsqrt(v_hat) + 1e-08
        master_out[0, :, cols] = master_ref[0, :, cols] - (learn_rate / corr_one) * m_next / root
        m_top = jnp.max(jnp.abs(m_next), axis=-1, keepdims=True) + 1e-06
        v_top = jnp.max(v_next, axis=-1, keepdims=True) + 1e-06
        mc_out[0, :, cols] = (m_next * (1.0 / m_top)).astype(BF16)
        vc_out[0, :, cols] = (v_next * (1.0 / v_top)).astype(BF16)
        m_tops = jnp.where(lane == b, m_top, m_tops)
        v_tops = jnp.where(lane == b, v_top, v_tops)
    ms_out[0] = m_tops.T
    vs_out[0] = v_tops.T


def adam(master_weight, grads, m_code, m_scale, v_code, v_scale):
    members, rows, width = master_weight.shape
    blocks = m_scale.shape[-1]
    count = 8 if blocks % 8 == 0 else blocks
    big = pl.BlockSpec((1, rows, count * BLOCK), lambda e, j: (e, 0, j))
    small = pl.BlockSpec((1, count, rows), lambda e, j: (e, j, 0))
    scales = jax.ShapeDtypeStruct((members, blocks, rows), F32)
    master_next, m_code_next, m_scale_next, v_code_next, v_scale_next = pl.pallas_call(
        functools.partial(adam_kernel, len(grads)),
        grid=(members, blocks // count),
        in_specs=[big, big, small, big, small] + [big] * len(grads),
        out_specs=(big, big, small, big, small),
        out_shape=(
            jax.ShapeDtypeStruct(master_weight.shape, F32),
            jax.ShapeDtypeStruct(master_weight.shape, BF16),
            scales,
            jax.ShapeDtypeStruct(master_weight.shape, BF16),
            scales,
        ),
        compiler_params=params("arbitrary", "arbitrary"),
        cost_estimate=cost(40 * master_weight.size, 18 * master_weight.size),
        name="adam",
    )(master_weight, m_code, jnp.swapaxes(m_scale, 1, 2), v_code, jnp.swapaxes(v_scale, 1, 2), *grads)
    return (
        master_next,
        m_code_next,
        jnp.swapaxes(m_scale_next, 1, 2),
        v_code_next,
        jnp.swapaxes(v_scale_next, 1, 2),
    )


def swap(array, axis, offset):
    size = lax.axis_size(axis)
    return lax.ppermute(array, axis, [(i, i ^ offset) for i in range(size)])


def exchange(buffer, groups):
    places, width = buffer.shape
    parts = buffer.reshape(groups, places // groups, width)
    members = sorted(range(groups), key=lambda device: order_of(device, groups))
    moved = lax.all_to_all(
        parts, "grp", split_axis=0, concat_axis=0, tiled=True, axis_index_groups=[members]
    )
    return moved.reshape(places, width)


def gather_weight(weight_slice, replicas):
    if replicas != 4:
        return [lax.all_gather(weight_slice, "rep", axis=1, tiled=True)]
    far = swap(weight_slice, "rep", 2)
    near = swap(weight_slice, "rep", 1)
    return [weight_slice, near, far, swap(far, "rep", 1)]


def sum_gradient(parts):
    if len(parts) != 4:
        return [lax.psum_scatter(parts[0], "rep", scatter_dimension=1, tiled=True)]
    far = swap(parts[3], "rep", 1)
    near = swap(parts[1], "rep", 1)
    return [parts[0], near, swap(add_parts(parts[2], far), "rep", 2)]


def per_device(master_weight, m_code, m_scale, v_code, v_scale, placement, route, x_rows, y_cot):
    local_count = master_weight.shape[0]
    row_count = x_rows.shape[0]
    expert_count = placement.shape[0]
    groups = lax.axis_size("grp")
    replicas = lax.axis_size("rep")
    grad_factor = float(row_count * groups * replicas // expert_count) ** (-0.5)
    capacity = max(2, (3 * row_count + 2 * expert_count - 1) // (2 * expert_count))
    places = expert_count * capacity
    sent, target = dispatch(route, placement, x_rows, y_cot, capacity, groups)
    local = exchange(sent, groups)
    early_master, target = lax.optimization_barrier((master_weight, target))
    weight = join_weight(gather_weight(cast_weight(early_master), replicas))
    results = products(local, weight, capacity, local_count)
    local, results = lax.optimization_barrier((local, results))
    home = exchange(results, groups)

    parts = replicas if replicas == 4 else 1
    hidden = x_rows.shape[1]
    grads = sum_gradient(gradient(local, hidden, capacity, local_count, parts, grad_factor))
    updated = adam(master_weight, grads, m_code, m_scale, v_code, v_scale)
    y_rows, x_grad = collect(target, home, hidden)
    return (y_rows, x_grad) + tuple(updated)


def solution(mesh):
    return jax.shard_map(
        per_device,
        mesh=mesh,
        in_specs=(
            P("grp", "rep", None),
            P("grp", "rep", None),
            P("grp", "rep", None),
            P("grp", "rep", None),
            P("grp", "rep", None),
            P(),
            P(("rep", "grp")),
            P(("rep", "grp"), None),
            P(("rep", "grp"), None),
        ),
        out_specs=(
            P(("rep", "grp"), None),
            P(("rep", "grp"), None),
            P("grp", "rep", None),
            P("grp", "rep", None),
            P("grp", "rep", None),
            P("grp", "rep", None),
            P("grp", "rep", None),
        ),
        check_vma=False,
    )
```
